512 devices in a mesh: cuts: 16 (over z), sx: 8 (over x, core), sy: 4 (over y).
Axes of the slice: x: 4, y: 4, z: 16, core: 2. Of those that a mesh axis runs over, the one named last changes fastest.
Arguments:
- starts: float32 [16, 3, 512, 2048], P('cuts', None, 'sx', 'sy'), may hold values from -2 to 2
- viscosity: float32 [512, 2048], P('sx', 'sy'), may hold values from 0.02 to 0.15
- turbine_x: int32 [64], replicated, may hold values from 0 to 511
- turbine_y: int32 [64], replicated, may hold values from 0 to 2047
- yaw_index: int32 [16, 64], replicated, may hold values from 0 to 6
Outputs:
- new_starts: float32 [16, 3, 512, 2048], P('cuts', None, 'sx', 'sy')
The draws below stay inside these ranges and needn't reach their ends.
All inputs are finite; a program needn't handle non-finite values.
Results may differ from the reference program's by a relative error of at most 0.0001.
Values sent between devices are 32-bit elements; how exact they have to be, the bound alone decides.
No kernel may reach another device: no remote copies, remote signals or barrier semaphores. Data moves between devices by JAX's collectives and lax.ppermute only.
A program may use at most 64 MiB of HBM per device.

```python
import math
import jax
import jax.numpy as jnp
from jax import lax

FINE = 4
COARSE = 2
NTURB = 64
YAWS = 7
NX = 512
NY = 2048
N_CUTS = 16


def set_ends(entries, key, low, high):
    shape = entries.shape
    spot = [jax.random.randint(jax.random.fold_in(key, axis), (), 0, shape[axis]) for axis in range(len(shape))]
    entries = entries.at[tuple(spot)].set(low)
    longest = shape.index(max(shape))
    spot[longest] = (spot[longest] + 1) % shape[longest]
    return entries.at[tuple(spot)].set(high)


def shard_levels(own_key, extent, pieces, least, top_value):
    def one(axis_at, blocks):
        draws = jax.random.uniform(jax.random.fold_in(jax.random.fold_in(own_key, 6), axis_at), (blocks,), jnp.float32, least / len(pieces), top_value / len(pieces))
        return jnp.repeat(jnp.exp(draws), extent[axis_at] // blocks).reshape((-1,) + (1,) * (len(extent) - axis_at - 1))

    gain = one(*pieces[0])
    for cut in pieces[1:]:
        gain = gain * one(*cut)
    return gain


def centred(rng, shape, scale, most, split=(), kind=jnp.bfloat16):
    drawn = scale * jax.random.normal(rng, shape, jnp.float32)
    if split:
        drawn = drawn * shard_levels(rng, shape, split, -0.22, 0.18)
    return jnp.clip(drawn, -most, most).astype(kind)


def setup_inputs(seed: int = 0) -> dict:
    arg_keys = jax.random.split(jax.random.key(seed), 6)
    starts = centred(arg_keys[0], (N_CUTS, 3, NX, NY), 0.15, 2.0, ((0, 16), (2, 8), (3, 4)), jnp.float32)
    viscosity = jnp.clip(jnp.exp(math.log(0.15) - 2.014903 * jax.random.uniform(arg_keys[1], (NX, NY), jnp.float32) ** shard_levels(arg_keys[1], (NX, NY), ((0, 8), (1, 4)), -0.2, 0.2)), 0.02, 0.15)
    turbine_x = set_ends(jax.random.randint(arg_keys[2], (NTURB,), 0, NX), jax.random.fold_in(arg_keys[2], 1), 0, NX - 1).astype(jnp.int32)
    turbine_y = set_ends(jax.random.randint(arg_keys[3], (NTURB,), 0, NY), jax.random.fold_in(arg_keys[3], 1), 0, NY - 1).astype(jnp.int32)
    yaw_index = set_ends(jax.random.randint(arg_keys[4], (N_CUTS, NTURB), 0, YAWS), jax.random.fold_in(arg_keys[4], 1), 0, YAWS - 1).astype(jnp.int32)
    return {"starts": starts, "viscosity": viscosity, "turbine_x": turbine_x, "turbine_y": turbine_y, "yaw_index": yaw_index}


rotor_reach = 3
fine_terms = (0.3, 0.5, 0.2, 0.5)
coarse_terms = (0.15, 0.25, 0.1, 1.0)


def centre(field):
    return field[1:-1, 1:-1]


def east_of(field):
    return field[2:, 1:-1]


def west_of(field):
    return field[:-2, 1:-1]


def north_of(field):
    return field[1:-1, 2:]


def south_of(field):
    return field[1:-1, :-2]


def laplace(field):
    return east_of(field) + west_of(field) + north_of(field) + south_of(field) - 4.0 * centre(field)


def advance(padded, nu_here, push_x, push_y, terms):
    carry_rate, steep_rate, couple_rate, thrust_rate = terms
    speed_x = padded[0]
    speed_y = padded[1]
    pressure = padded[2]
    here_x = centre(speed_x)
    here_y = centre(speed_y)
    here_p = centre(pressure)
    slope_xx = 0.5 * (east_of(speed_x) - west_of(speed_x))
    slope_yy = 0.5 * (north_of(speed_y) - south_of(speed_y))
    slope_yx = 0.5 * (east_of(speed_y) - west_of(speed_y))
    lifted = 1.0 + here_x
    drag = thrust_rate * lifted * jnp.abs(lifted) / (1.0 + jnp.abs(lifted))
    new_x = (here_x + nu_here * laplace(speed_x) - carry_rate * (here_x - west_of(speed_x))
             - steep_rate * here_x * slope_xx
             - couple_rate * 0.5 * (east_of(pressure) - west_of(pressure)) - push_x * drag)
    new_y = (here_y + nu_here * laplace(speed_y) - carry_rate * (here_y - west_of(speed_y))
             - steep_rate * here_x * slope_yx
             - couple_rate * 0.5 * (north_of(pressure) - south_of(pressure)) - push_y * drag)
    new_p = here_p + nu_here * laplace(pressure) - couple_rate * (slope_xx + slope_yy)
    return jnp.stack([new_x, new_y, new_p])


def rotor_fields(rows_at, cols_at, turbine_x, turbine_y, yaw_row, block):
    angle = (yaw_row.astype(jnp.float32) - 0.5 * (YAWS - 1)) * (math.pi / 18.0)
    cosine = jnp.cos(angle)
    sine = jnp.sin(angle)
    if block == 1:
        row_hit = (rows_at[None, :] == turbine_x[:, None]).astype(jnp.float32)
        col_hit = (jnp.abs(cols_at[None, :] - turbine_y[:, None]) <= rotor_reach).astype(jnp.float32)
    else:
        row_hit = (rows_at[None, :] == (turbine_x // 4)[:, None]).astype(jnp.float32) * 0.25
        col_hit = jnp.zeros((turbine_y.shape[0], cols_at.shape[0]), jnp.float32)
        for offset in range(4):
            col_hit = col_hit + (jnp.abs(4 * cols_at[None, :] + offset - turbine_y[:, None]) <= rotor_reach).astype(jnp.float32)
        col_hit = col_hit * 0.25
    weight_x = cosine * cosine * cosine
    weight_y = cosine * cosine * sine
    push_x = jnp.einsum("kh,kw->hw", row_hit, col_hit * weight_x[:, None], precision=lax.Precision.HIGHEST)
    push_y = jnp.einsum("kh,kw->hw", row_hit, col_hit * weight_y[:, None], precision=lax.Precision.HIGHEST)
    return push_x, push_y


def restrict(field):
    leading = field.shape[:-2]
    height = field.shape[-2]
    breadth = field.shape[-1]
    return field.reshape(leading + (height // 4, 4, breadth // 4, 4)).mean(axis=(-3, -1))


def prolong(field):
    return jnp.repeat(jnp.repeat(field, 4, axis=-2), 4, axis=-1)


def padded_one(state):
    return jnp.pad(state, ((0, 0), (1, 1), (1, 1)))


def fine_solve(state, viscosity, turbine_x, turbine_y, yaw_row):
    rows_at = jnp.arange(NX, dtype=jnp.int32)
    cols_at = jnp.arange(NY, dtype=jnp.int32)
    push_x, push_y = rotor_fields(rows_at, cols_at, turbine_x, turbine_y, yaw_row, 1)
    for step in range(FINE):
        state = advance(padded_one(state), viscosity, push_x, push_y, fine_terms)
    return state


def coarse_solve(state, coarse_nu, turbine_x, turbine_y, yaw_row):
    rows_at = jnp.arange(NX // 4, dtype=jnp.int32)
    cols_at = jnp.arange(NY // 4, dtype=jnp.int32)
    push_x, push_y = rotor_fields(rows_at, cols_at, turbine_x, turbine_y, yaw_row, 4)
    for step in range(COARSE):
        state = advance(padded_one(state), coarse_nu, push_x, push_y, coarse_terms)
    return state


def reference(starts, viscosity, turbine_x, turbine_y, yaw_index):
    coarse_nu = restrict(viscosity) * 0.5

    def per_slice(item):
        start, yaw_row = item
        fine = fine_solve(start, viscosity, turbine_x, turbine_y, yaw_row)
        guess = coarse_solve(restrict(start), coarse_nu, turbine_x, turbine_y, yaw_row)
        return fine - prolong(guess), restrict(fine) - guess

    fine_part, defects = lax.map(per_slice, (starts, yaw_index))

    def link(current, item):
        defect_row, yaw_row = item
        moved = coarse_solve(current, coarse_nu, turbine_x, turbine_y, yaw_row)
        return moved + defect_row, moved

    final_state, moved_all = lax.scan(link, restrict(starts[0]), (defects, yaw_index))
    return fine_part + prolong(moved_all)
```

```python
import math

import jax
import jax.numpy as jnp
import numpy as np
from jax import lax
from jax.experimental import pallas as pl
from jax.experimental.pallas import tpu as pltpu
from jax.sharding import PartitionSpec as P

YAWS = 7
CUTS = 16
REACH = 3
FINE_TERMS = (0.3, 0.5, 0.2)
FINE_THRUST = 0.5
COARSE_TERMS = (0.15, 0.25, 0.1)
COARSE_THRUST = 1.0
EXACT = lax.Precision.HIGHEST
F32 = jnp.float32

ROWS, COLS = 64, 512
CROWS, CCOLS = 16, 128
REACHED = 2 * (CUTS - 1)
EXT = 80
PLANES = 46
ANGLES = [(k - 0.5 * (YAWS - 1)) * (math.pi / 18.0) for k in range(YAWS)]
WEIGHT_X = [float(np.float32(math.cos(t) ** 3)) for t in ANGLES]
WEIGHT_Y = [float(np.float32(math.cos(t) ** 2 * math.sin(t))) for t in ANGLES]

_CLASS = [
    (0, 80, 32, list(range(9)) + [45]),
    (8, 64, 32, list(range(9, 21))),
    (16, 48, 16, list(range(21, 33))),
    (24, 32, 8, list(range(33, 45))),
]
GROUPS = []
_at = 0
for _first, _count, _width, _members in _CLASS:
    _per = 128 // _width
    for _i in range(0, len(_members), _per):
        GROUPS.append((_at, _first, _count, _width, _members[_i : _i + _per]))
        _at += _count
YROWS = _at
S1_ROWS = 11 * 48 + 12 * 8 + 16
S2_ROWS = 9 * 16 + 12 * 8 + 16


def lanes(shape):
    return lax.broadcasted_iota(jnp.int32, shape, len(shape) - 1)


def sublanes(shape):
    return lax.broadcasted_iota(jnp.int32, shape, len(shape) - 2)


def advance(src, dst, nu, fx, fy, mask, row, count, tiles, wanted, terms, post=None):
    carry, steep, couple = terms
    lane = lanes((count, 128))
    low, high = lane == 0, lane == 127
    here = pl.ds(row, count)
    east = pl.ds(row + 1, count)
    west = pl.ds(row - 1, count)
    mid = [[src[f, c, here, :] for c in range(tiles)] for f in range(3)]
    up = [[pltpu.roll(mid[f][c], 127, 1) for c in range(tiles)] for f in range(3)]
    down = [[pltpu.roll(mid[f][c], 1, 1) for c in range(tiles)] for f in range(3)]
    for c in wanted:
        after, before = (c + 1) % tiles, (c - 1) % tiles
        u, v, p = mid[0][c], mid[1][c], mid[2][c]
        un, vn, pn = [jnp.where(high, up[f][after], up[f][c]) for f in range(3)]
        us, vs, ps = [jnp.where(low, down[f][before], down[f][c]) for f in range(3)]
        ue, ve, pe = [src[f, c, east, :] for f in range(3)]
        uw, vw, pw = [src[f, c, west, :] for f in range(3)]
        nu_here = nu(c, here)
        du = ue - uw
        steeper = (0.5 * steep) * u
        lifted = 1.0 + u
        size = jnp.abs(lifted)
        drag = lifted * size / (1.0 + size)
        new_u = (
            u
            + nu_here * ((ue + uw) + (un + us) - 4.0 * u)
            - carry * (u - uw)
            - steeper * du
            - (0.5 * couple) * (pe - pw)
            - fx(c, here) * drag
        )
        new_v = (
            v
            + nu_here * ((ve + vw) + (vn + vs) - 4.0 * v)
            - carry * (v - vw)
            - steeper * (ve - vw)
            - (0.5 * couple) * (pn - ps)
            - fy(c, here) * drag
        )
        new_p = p + nu_here * ((pe + pw) + (pn + ps) - 4.0 * p) - (0.5 * couple) * (du + (vn - vs))
        new = [new_u, new_v, new_p]
        if mask is not None:
            inside = mask(c, here)
            new = [f * inside for f in new]
        for f in range(3):
            if post is None:
                dst[f, c, here, :] = new[f]
            else:
                post(f, c, here, new[f])


def yaw_weights(yaw):
    wx = jnp.zeros(yaw.shape, F32)
    wy = jnp.zeros(yaw.shape, F32)
    for k in range(YAWS):
        hit = yaw == k
        wx = jnp.where(hit, WEIGHT_X[k], wx)
        wy = jnp.where(hit, WEIGHT_Y[k], wy)
    return wx, wy


def edge_kernel(at, start, visc, send_a, send_b):
    even = lax.rem(at[1], 2) == 0
    for f in range(4):
        first = start[f, 0:8, :] if f < 3 else visc[0:8, :]
        last = start[f, 56:64, :] if f < 3 else visc[56:64, :]
        send_a[f] = jnp.where(even, last, first)
        send_b[f] = jnp.where(even, first, last)


def side_kernel(at, start, visc, got_a, got_b, send_a, send_b):
    even_x = lax.rem(at[1], 2) == 0
    even_y = lax.rem(at[2], 2) == 0
    for r0, count in ((0, 8), (8, 64), (72, 8)):
        lane = lanes((count, 128))
        left = jnp.zeros((count, 128), F32)
        right = jnp.zeros((count, 128), F32)
        for f in range(4):
            own = start.at[f] if f < 3 else visc
            if r0 == 8:
                a, b = own[:, 0:128], own[:, COLS - 128 : COLS]
            else:
                top = jnp.logical_xor(even_x, r0 == 0)
                a = jnp.where(top, got_a[f, :, 0:128], got_b[f, :, 0:128])
                b = jnp.where(top, got_a[f, :, COLS - 128 : COLS], got_b[f, :, COLS - 128 : COLS])
            mine = (lane >= 8 * f) & (lane < 8 * f + 8)
            left = jnp.where(mine, pltpu.roll(a, 8 * f, 1) if f else a, left)
            right = jnp.where(mine, pltpu.roll(b, 8 * f + 8, 1), right)
        send_a[r0 : r0 + count, :] = jnp.where(even_y, right, left)
        send_b[r0 : r0 + count, :] = jnp.where(even_y, left, right)


def push_kernel(at, tx, ty, yaw, fine_push, own_push):
    mine = lanes(yaw.shape) == at[0]
    own_yaw = jnp.sum(jnp.where(mine, yaw[...], 0), axis=1, keepdims=True)
    wx, wy = yaw_weights(own_yaw)
    row = at[1] * ROWS - 16 + sublanes((96, 64))
    row_hit = (row == tx[...]).astype(F32) * FINE_THRUST
    for c in range(5):
        lane = lanes((64, 128))
        if c < 4:
            col = at[2] * COLS + 128 * c + lane
        else:
            col = at[2] * COLS + jnp.where(lane < 64, COLS + lane, lane - 128)
        col_hit = (jnp.abs(col - ty[...]) <= REACH).astype(F32)
        fine_push[0, c] = jnp.dot(row_hit, col_hit * wx, precision=EXACT, preferred_element_type=F32)
        fine_push[1, c] = jnp.dot(row_hit, col_hit * wy, precision=EXACT, preferred_element_type=F32)
    row = at[1] * CROWS - 10 + sublanes((40, 64))
    row_hit = (row == tx[...] // 4).astype(F32) * (0.25 * COARSE_THRUST)
    for c in range(2):
        col_hit = coarse_cols(at[2], c, ty[...])
        own_push[0, c] = jnp.dot(row_hit, col_hit * wx, precision=EXACT, preferred_element_type=F32)
        own_push[1, c] = jnp.dot(row_hit, col_hit * wy, precision=EXACT, preferred_element_type=F32)


def coarse_cols(sy, c, ty):
    lane = lanes((64, 128))
    col = sy * CCOLS + (lane if c == 0 else jnp.where(lane < 64, CCOLS + lane, lane - 128))
    hit = jnp.zeros((64, 128), F32)
    for offset in range(4):
        hit = hit + (jnp.abs(4 * col + offset - ty) <= REACH).astype(F32)
    return hit * 0.25


def chain_push_kernel(at, tx, ty, yaw, push):
    row = at[1] * CROWS - 32 + sublanes((EXT, 64))
    row_hit = (row == tx[...] // 4).astype(F32) * (0.25 * COARSE_THRUST)
    cols = [coarse_cols(at[2], c, ty[...]) for c in range(2)]
    for n in range(1, CUTS):
        weights = yaw_weights(yaw[:, n : n + 1])
        for d in range(2):
            for c in range(2):
                push[n, d, c] = jnp.dot(row_hit, cols[c] * weights[d], precision=EXACT, preferred_element_type=F32)


def fine_kernel(at, start, visc, rows_a, rows_b, cols_a, cols_b, push, own_push, fine, guess, sent, coarse_nu,
                one, two, nu, mask, rough, rough_two, rough_mask):
    even_x = lax.rem(at[1], 2) == 0
    even_y = lax.rem(at[2], 2) == 0
    for f in range(4):
        own = start.at[f] if f < 3 else visc
        for c in range(4):
            dst = one.at[f, c] if f < 3 else nu.at[c]
            cut = slice(128 * c, 128 * c + 128)
            dst[16:80, :] = own[:, cut]
            dst[8:16, :] = jnp.where(even_x, rows_b[f, :, cut], rows_a[f, :, cut])
            dst[80:88, :] = jnp.where(even_x, rows_a[f, :, cut], rows_b[f, :, cut])
        after = jnp.where(even_y, cols_a[...], cols_b[...])
        before = jnp.where(even_y, cols_b[...], cols_a[...])
        lane = lanes((EXT, 128))
        after = pltpu.roll(after, (128 - 8 * f) % 128, 1) if f else after
        before = pltpu.roll(before, 120 - 8 * f, 1)
        dst = one.at[f, 4] if f < 3 else nu.at[4]
        dst[8:88, :] = jnp.where(lane < 8, after, jnp.where(lane >= 120, before, 0.0))
    lane, line = lanes((96, 128)), sublanes((96, 128))
    last_x, last_y = at[3] - 1, at[4] - 1
    in_rows = ((line >= 16) | (at[1] > 0)) & ((line < 80) | (at[1] < last_x))
    in_cols = ((lane >= 64) | (at[2] < last_y)) & ((lane < 64) | (at[2] > 0))
    for c in range(4):
        mask[c] = in_rows.astype(F32)
    mask[4] = (in_rows & in_cols).astype(F32)

    i, j = sublanes((COLS, 128)), lanes((COLS, 128))
    gather = (i // 4 == j).astype(F32) * 0.0625
    i, j = sublanes((128, 128)), lanes((128, 128))
    gather_side = (((i < 8) & (i // 4 == j)) | ((i >= 120) & ((i - 120) // 4 == j - 126))).astype(F32) * 0.0625

    def row_sum(ref, first, count):
        parts = [ref[pl.ds(first + k, count, stride=4), :] for k in range(4)]
        return (parts[0] + parts[1]) + (parts[2] + parts[3])

    body = [jnp.concatenate([row_sum(one.at[f, c] if f < 3 else nu.at[c], 0, 24) for c in range(4)], axis=1) for f in range(4)]
    side = [row_sum(one.at[f, 4] if f < 3 else nu.at[4], 0, 24) for f in range(4)]
    body = jnp.dot(jnp.concatenate(body, axis=0), gather, precision=EXACT, preferred_element_type=F32)
    side = jnp.dot(jnp.concatenate(side, axis=0), gather_side, precision=EXACT, preferred_element_type=F32)
    rough[...] = jnp.zeros(rough.shape, F32)
    rough_two[...] = jnp.zeros(rough_two.shape, F32)
    for f in range(4):
        scale = 0.5 if f == 3 else 1.0
        rough[f, 0, 6:30, :] = body[24 * f : 24 * f + 24, :] * scale
        rough[f, 1, 6:30, :] = side[24 * f : 24 * f + 24, :] * scale
    coarse_nu[...] = rough[3, 0, 10:26, :]
    lane, line = lanes((40, 128)), sublanes((40, 128))
    in_rows = ((line >= 10) | (at[1] > 0)) & ((line < 26) | (at[1] < last_x))
    in_cols = ((lane >= 64) | (at[2] < last_y)) & ((lane < 64) | (at[2] > 0))
    rough_mask[0] = in_rows.astype(F32)
    rough_mask[1] = (in_rows & in_cols).astype(F32)
    coarse = (
        lambda c, r: rough[3, c, r, :],
        lambda c, r: own_push[0, c, r, :],
        lambda c, r: own_push[1, c, r, :],
        lambda c, r: rough_mask[c, r, :],
    )
    for k in range(3):
        advance(rough, rough_two, *coarse, 9 + 8 * k, 8, 2, (0, 1), COARSE_TERMS)

    def keep_guess(f, c, r, value):
        guess[pl.ds(16 * f + r.start - 10, 8), :] = value

    for k in range(2):
        advance(rough_two, None, *coarse, 10 + 8 * k, 8, 2, (0,), COARSE_TERMS, post=keep_guess)

    finest = (
        lambda c, r: nu[c, r, :],
        lambda c, r: push[0, c, r, :],
        lambda c, r: push[1, c, r, :],
        lambda c, r: mask[c, r, :],
    )
    for src, dst, first, count, wanted in (
        (one, two, 12, 9, range(5)),
        (two, one, 12, 9, range(5)),
        (one, two, 12, 9, range(5)),
        (two, one, 16, 8, range(4)),
    ):
        for k in range(count):
            advance(src, dst, *finest, first + 8 * k, 8, 5, wanted, FINE_TERMS)
    for f in range(3):
        for c in range(4):
            fine[f, :, 128 * c : 128 * c + 128] = one[f, c, 16:80, :]
    ends = [jnp.concatenate([row_sum(one.at[f, c], 16, 16) for c in range(4)], axis=1) for f in range(3)]
    ends = jnp.dot(jnp.concatenate(ends, axis=0), gather, precision=EXACT, preferred_element_type=F32)
    defect = ends - jnp.where(at[0] == 0, 0.0, guess[...])
    for m in range(CUTS):
        sent[m] = defect


def rows_kernel(at, held, nu, send_a, send_b, send_c, send_d):
    odd = lax.rem(at[1], 2)
    odd_pair = lax.rem(at[1], 4) // 2
    for ref, lower in ((send_a, odd == 0), (send_b, odd == 1)):
        for m in range(11):
            ref[48 * m : 48 * m + 48, :] = held[m]
        for q in range(12):
            m, f = 11 + q // 3, q % 3
            ref[528 + 8 * q : 536 + 8 * q, :] = jnp.where(
                lower, held[m, 16 * f + 8 : 16 * f + 16, :], held[m, 16 * f : 16 * f + 8, :])
        ref[624:640, :] = nu[...]
    for ref, lower in ((send_c, odd_pair == 0), (send_d, odd_pair == 1)):
        for m in range(3):
            ref[48 * m : 48 * m + 48, :] = held[m]
        for q in range(12):
            m, f = 3 + q // 3, q % 3
            ref[144 + 8 * q : 152 + 8 * q, :] = jnp.where(
                lower, held[m, 16 * f + 8 : 16 * f + 16, :], held[m, 16 * f : 16 * f + 8, :])
        ref[240:256, :] = nu[...]


def cols_kernel(at, held, nu, got_a, got_b, got_c, got_d, whole, send_a, send_b):
    even = lax.rem(at[1], 2) == 0
    even_pair = lax.rem(at[1], 4) < 2
    even_y = lax.rem(at[2], 2) == 0

    def near(first, count):
        a, b = got_a[first : first + count, :], got_b[first : first + count, :]
        return jnp.where(even, b, a), jnp.where(even, a, b)

    def far(first, count):
        a, b = got_c[first : first + count, :], got_d[first : first + count, :]
        return jnp.where(even_pair, b, a), jnp.where(even_pair, a, b)

    for q in range(PLANES):
        m, f = q // 3, q % 3
        is_nu = q == 45
        whole[q, 32:48, :] = nu[...] if is_nu else held[m, 16 * f : 16 * f + 16, :]
        if is_nu or m < 11:
            before, after = near(624 if is_nu else 16 * q, 16)
            whole[q, 16:32, :] = before
            whole[q, 48:64, :] = after
        else:
            before, after = near(528 + 8 * (q - 33), 8)
            whole[q, 24:32, :] = before
            whole[q, 48:56, :] = after
        if is_nu or m < 3:
            before, after = far(240 if is_nu else 16 * q, 16)
            whole[q, 0:16, :] = before
            whole[q, 64:80, :] = after
        elif m < 7:
            before, after = far(144 + 8 * (q - 9), 8)
            whole[q, 8:16, :] = before
            whole[q, 64:72, :] = after
    for at_row, first, count, width, members in GROUPS:
        lane = lanes((count, 128))
        left = jnp.zeros((count, 128), F32)
        right = jnp.zeros((count, 128), F32)
        for slot, q in enumerate(members):
            offset = slot * width
            value = whole[q, first : first + count, :]
            mine = (lane >= offset) & (lane < offset + width)
            left = jnp.where(mine, pltpu.roll(value, offset, 1) if offset else value, left)
            shift = (offset + width) % 128
            right = jnp.where(mine, pltpu.roll(value, shift, 1) if shift else value, right)
        send_a[at_row : at_row + count, :] = jnp.where(even_y, right, left)
        send_b[at_row : at_row + count, :] = jnp.where(even_y, left, right)


def chain_kernel(at, whole, got_a, got_b, push, fine, guess, out, side, one, two, kept, mask, moved):
    even_y = lax.rem(at[2], 2) == 0
    for at_row, first, count, width, members in GROUPS:
        lane = lanes((count, 128))
        a, b = got_a[at_row : at_row + count, :], got_b[at_row : at_row + count, :]
        after, before = jnp.where(even_y, a, b), jnp.where(even_y, b, a)
        for slot, q in enumerate(members):
            offset = slot * width
            hi = pltpu.roll(after, (128 - offset) % 128, 1) if offset else after
            shift = (128 - width - offset) % 128
            lo = pltpu.roll(before, shift, 1) if shift else before
            side[q, first : first + count, :] = jnp.where(lane < width, hi, jnp.where(lane >= 128 - width, lo, 0.0))
    lane, line = lanes((EXT, 128)), sublanes((EXT, 128))
    row = at[1] * CROWS - 32 + line
    in_rows = (row >= 0) & (row < at[3] * CROWS)
    in_cols = ((lane >= 64) | (at[2] < at[4] - 1)) & ((lane < 64) | (at[2] > 0))
    mask[0] = in_rows.astype(F32)
    mask[1] = (in_rows & in_cols).astype(F32)
    for f in range(3):
        one[f, 0, 8:88, :] = whole[f]
        one[f, 1, 8:88, :] = side[f]

    def shifted(r):
        return pl.ds(r.start - 8, r.size)

    for n in range(1, CUTS):
        fields = (
            lambda c, r: (whole if c == 0 else side)[45, shifted(r), :],
            lambda c, r, n=n: push[n, 0, c, shifted(r), :],
            lambda c, r, n=n: push[n, 1, c, shifted(r), :],
            lambda c, r: mask[c, shifted(r), :],
        )
        for half in range(2):
            halo = 2 * (CUTS - 1 - n) + 1 - half
            count = 2 + -(-halo // 4)
            first = min(8 + 32 - halo, 88 - 8 * count)
            src, dst = (one, two) if half == 0 else (two, one)
            wanted = (0, 1) if halo else (0,)
            post = None
            if half == 1:
                def post(f, c, r, value, n=n):
                    if n < CUTS - 1:
                        one[f, c, r, :] = value + (whole if c == 0 else side)[3 * n + f, shifted(r), :]
                    else:
                        one[f, c, r, :] = value
                    if c == 0:
                        kept[f, r, :] = value
            for k in range(count):
                advance(src, dst, *fields, first + 8 * k, 8, 2, wanted, COARSE_TERMS, post=post)
        for f in range(3):
            moved[n, 16 * f : 16 * f + 16, :] = kept[f, 40:56, :]

    change = jnp.where(at[0] == 0, 0.0, moved[at[0]] - guess[...])
    i, j = sublanes((3 * ROWS, 48)), lanes((3 * ROWS, 48))
    repeat_rows = (i // 4 == j).astype(F32)
    i, j = sublanes((128, COLS)), lanes((128, COLS))
    repeat_cols = (i == j // 4).astype(F32)
    change = jnp.dot(repeat_rows, change, precision=EXACT, preferred_element_type=F32)
    change = jnp.dot(change, repeat_cols, precision=EXACT, preferred_element_type=F32)
    for f in range(3):
        out[f] = fine[f] + change[ROWS * f : ROWS * f + ROWS, :]


def call(kernel, args, outs, scratch=()):
    smem = pl.BlockSpec(memory_space=pltpu.SMEM)
    vmem = pl.BlockSpec(memory_space=pltpu.VMEM)
    shapes = [jax.ShapeDtypeStruct(s, F32) for s in outs]
    return pl.pallas_call(
        kernel,
        out_shape=shapes,
        in_specs=[smem] + [vmem] * (len(args) - 1),
        out_specs=[vmem] * len(shapes),
        scratch_shapes=[pltpu.VMEM(s, F32) for s in scratch],
        compiler_params=pltpu.CompilerParams(vmem_limit_bytes=48 * 1024 * 1024),
    )(*args)


def swap(x, axis, pairs):
    return lax.ppermute(x, axis, [(a, b) for a, b in pairs] + [(b, a) for a, b in pairs])


def on_device(starts, viscosity, turbine_x, turbine_y, yaw_index):
    count_x, count_y = lax.axis_size("sx"), lax.axis_size("sy")
    at = jnp.stack([
        lax.axis_index("cuts"), lax.axis_index("sx"), lax.axis_index("sy"),
        jnp.int32(count_x), jnp.int32(count_y),
    ]).astype(jnp.int32)
    start = starts[0]
    tx, ty, yaw = turbine_x[None, :], turbine_y[:, None], yaw_index.T
    x_a = [(i, i + 1) for i in range(0, count_x - 1, 2)]
    x_b = [(i, i + 1) for i in range(1, count_x - 1, 2)]
    x_c = [(i, i + 2) for i in range(count_x - 2) if i % 4 < 2]
    x_d = [(i, i + 2) for i in range(count_x - 2) if i % 4 >= 2]
    y_a = [(i, i + 1) for i in range(0, count_y - 1, 2)]
    y_b = [(i, i + 1) for i in range(1, count_y - 1, 2)]

    edge = (4, 8, COLS)
    send_a, send_b = call(edge_kernel, (at, start, viscosity), [edge, edge])
    rows_b = swap(send_b, "sx", x_b)
    rows_a = swap(send_a, "sx", x_a)
    push, own_push = call(push_kernel, (at, tx, ty, yaw), [(2, 5, 96, 128), (2, 2, 40, 128)])
    (chain_push,) = call(chain_push_kernel, (at, tx, ty, yaw), [(CUTS, 2, 2, EXT, 128)])
    send_a, send_b = call(side_kernel, (at, start, viscosity, rows_a, rows_b), [(EXT, 128)] * 2)
    cols_a = swap(send_a, "sy", y_a)
    cols_b = swap(send_b, "sy", y_b)
    fine, guess, sent, coarse_nu = call(
        fine_kernel,
        (at, start, viscosity, rows_a, rows_b, cols_a, cols_b, push, own_push),
        [(3, ROWS, COLS), (48, 128), (CUTS, 48, 128), (CROWS, 128)],
        [(3, 5, 96, 128), (3, 5, 96, 128), (5, 96, 128), (5, 96, 128), (4, 2, 40, 128), (3, 2, 40, 128), (2, 40, 128)],
    )
    held = lax.all_to_all(sent, "cuts", 0, 0)
    send_a, send_b, send_c, send_d = call(
        rows_kernel, (at, held, coarse_nu), [(S1_ROWS, 128)] * 2 + [(S2_ROWS, 128)] * 2)
    got_b = swap(send_b, "sx", x_b)
    got_c = swap(send_c, "sx", x_c)
    got_d = swap(send_d, "sx", x_d)
    got_a = swap(send_a, "sx", x_a)
    whole, send_a, send_b = call(
        cols_kernel, (at, held, coarse_nu, got_a, got_b, got_c, got_d), [(PLANES, EXT, 128)] + [(YROWS, 128)] * 2)
    got_a = swap(send_a, "sy", y_a)
    got_b = swap(send_b, "sy", y_b)
    (out,) = call(
        chain_kernel,
        (at, whole, got_a, got_b, chain_push, fine, guess),
        [(3, ROWS, COLS)],
        [(PLANES, EXT, 128), (3, 2, 96, 128), (3, 2, 96, 128), (3, 96, 128), (2, EXT, 128), (CUTS, 48, 128)],
    )
    return out[None]


def solution(mesh):
    in_specs = (P("cuts", None, "sx", "sy"), P("sx", "sy"), P(), P(), P())
    out_specs = P("cuts", None, "sx", "sy")
    return jax.shard_map(
        on_device, mesh=mesh, in_specs=in_specs, out_specs=out_specs, check_vma=False
    )
```

```python
import math

import jax
import jax.numpy as jnp
import numpy as np
from jax import lax
from jax.experimental import pallas as pl
from jax.experimental.pallas import tpu as pltpu
from jax.sharding import PartitionSpec as P

YAWS = 7
CUTS = 16
REACH = 3
F32 = jnp.float32
BF16 = jnp.bfloat16

FINE = (0.3, 0.25, 0.01)
FINE_THRUST = 0.5
FINE_SCALE = (0.25, 0.25, 0.025)
COARSE = (0.15, 0.125, 0.0025)
COARSE_THRUST = 1.0
COARSE_SCALE = (0.125, 0.125, 0.00625)
FINE_TO_COARSE = (0.5, 0.5, 0.25)

ROWS, COLS = 64, 512
CROWS, CCOLS = 16, 128
HALF = CUTS // 2
EXT = 48
NU = 45
ANGLES = [(k - 0.5 * (YAWS - 1)) * (math.pi / 18.0) for k in range(YAWS)]
WEIGHT_X = [float(np.float32(math.cos(t) ** 3)) for t in ANGLES]
WEIGHT_Y = [float(np.float32(math.cos(t) ** 2 * math.sin(t))) for t in ANGLES]

GROUPS = []
for _width, _members in (
    (32, list(range(21)) + [NU]),
    (16, list(range(21, 33))),
    (8, list(range(33, 45))),
):
    _per = 128 // _width
    GROUPS += [(_width, _members[_i : _i + _per]) for _i in range(0, len(_members), _per)]
STRIPS = 16 * len(GROUPS)
PARTS = (
    [(q, 16) for q in range(0, 9)] + [(q, 8) for q in range(9, 21)]
    + [(q, 16) for q in range(24, 33)] + [(q, 8) for q in range(33, 45)] + [(NU, 16)]
)
PART_AT = {}
_at = 0
for _q, _rows in PARTS:
    PART_AT[_q] = (_at, _rows)
    _at += _rows
STRIP_AT = _at
MESSAGE = STRIP_AT + 2 * STRIPS


def lanes(shape):
    return lax.broadcasted_iota(jnp.int32, shape, len(shape) - 1)


def sublanes(shape):
    return lax.broadcasted_iota(jnp.int32, shape, len(shape) - 2)


def rolled(x, by):
    return pltpu.roll(x, by % 128, 1) if by % 128 else x


def split3(x):
    high = x.astype(BF16)
    rest = x - high.astype(F32)
    middle = rest.astype(BF16)
    return high, middle, (rest - middle.astype(F32)).astype(BF16)


def exact_dot(x, y, dims=(((1,), (0,)), ((), ()))):
    y = y.astype(BF16)
    a, b, c = [lax.dot_general(part, y, dims, preferred_element_type=F32) for part in split3(x)]
    return a + (b + c)


def dot_exact(y, x):
    y = y.astype(BF16)
    a, b, c = [jnp.dot(y, part, preferred_element_type=F32) for part in split3(x)]
    return a + (b + c)


def advance(src, dst, coef, push, shift, row, count, tiles, wanted, terms, side_mask, post=None):
    _, lift, gain = terms
    lane = lanes((count, 128))
    low, high = lane == 0, lane == 127
    here, east, west = pl.ds(row, count), pl.ds(row + 1, count), pl.ds(row - 1, count)
    there = pl.ds(row - shift, count)
    mid = [[src[f, c, here, :] for c in range(tiles)] for f in range(3)]
    up = [[pltpu.roll(mid[f][c], 127, 1) for c in range(tiles)] for f in range(3)]
    down = [[pltpu.roll(mid[f][c], 1, 1) for c in range(tiles)] for f in range(3)]
    for c in wanted:
        after, before = (c + 1) % tiles, (c - 1) % tiles
        u, v, p = mid[0][c], mid[1][c], mid[2][c]
        un, vn, pn = [jnp.where(high, up[f][after], up[f][c]) for f in range(3)]
        us, vs, ps = [jnp.where(low, down[f][before], down[f][c]) for f in range(3)]
        ue, ve, pe = [src[f, c, east, :] for f in range(3)]
        uw, vw, pw = [src[f, c, west, :] for f in range(3)]
        nu, nu_carry, keep, keep_p = [coef[k, c, there, :] for k in range(4)]
        to_east, to_west = nu - u, nu_carry + u
        lifted = u + lift
        size = jnp.abs(lifted)
        drag = lifted * size / (size + lift)
        new_u = ue * to_east + uw * to_west + nu * (un + us) + keep * u - (pe - pw) - push(0, c, there) * drag
        new_v = ve * to_east + vw * to_west + nu * (vn + vs) + keep * v - (pn - ps) - push(1, c, there) * drag
        new_p = nu * ((pe + pw) + (pn + ps)) + keep_p * p - gain * ((ue - uw) + (vn - vs))
        new = [new_u, new_v, new_p]
        if c == tiles - 1:
            new = [f * side_mask for f in new]
        for f in range(3):
            if post is not None:
                new[f] = post(f, c, here, new[f])
            dst[f, c, here, :] = new[f]


def clear_rows(ref, tiles, before, after, outside):
    for row, factor in ((before, outside[0]), (after, outside[1])):
        for f in range(3):
            for c in range(tiles):
                ref[f, c, pl.ds(row, 1), :] = ref[f, c, pl.ds(row, 1), :] * factor


def edges(at):
    lane = lanes((8, 128))
    outside = [jnp.where(at[1] > 0, 1.0, 0.0), jnp.where(at[1] < at[3] - 1, 1.0, 0.0)]
    side = jnp.where(lane < 64, jnp.where(at[2] < at[4] - 1, 1.0, 0.0), jnp.where(at[2] > 0, 1.0, 0.0))
    return outside, side


def coefficients(coef, c, rows, nu, carry):
    coef[0, c, rows, :] = nu
    coef[1, c, rows, :] = nu + carry
    coef[2, c, rows, :] = (1.0 - carry) - 4.0 * nu
    coef[3, c, rows, :] = 1.0 - 4.0 * nu


def yaw_weights(yaw):
    wx = jnp.zeros(yaw.shape, F32)
    wy = jnp.zeros(yaw.shape, F32)
    for k in range(YAWS):
        hit = yaw == k
        wx = jnp.where(hit, WEIGHT_X[k], wx)
        wy = jnp.where(hit, WEIGHT_Y[k], wy)
    return wx, wy


def fetch(pairs, sems):
    copies = [pltpu.make_async_copy(a, b, sems.at[i]) for i, (a, b) in enumerate(pairs)]
    for copy in copies:
        copy.start()
    for copy in copies:
        copy.wait()


def edge_kernel(at, start, visc, send_a, send_b, sems):
    last = pl.multiple_of(56 * (1 - lax.rem(at[1], 2)), 8)
    first = pl.multiple_of(56 * lax.rem(at[1], 2), 8)
    fetch([
        (start.at[:, pl.ds(last, 8), :], send_a.at[0:3]),
        (visc.at[pl.ds(last, 8), :], send_a.at[3]),
        (start.at[:, pl.ds(first, 8), :], send_b.at[0:3]),
        (visc.at[pl.ds(first, 8), :], send_b.at[3]),
    ], sems)


def load_kernel(at, after, start, visc, out, sems):
    fetch(
        [(start.at[:, :, 128 * c : 128 * c + 128], out.at[0:3, c]) for c in range(4)]
        + [(visc.at[:, 128 * c : 128 * c + 128], out.at[3, c]) for c in range(4)],
        sems,
    )


def side_kernel(at, own, got_a, got_b, send_a, send_b):
    even_x = lax.rem(at[1], 2) == 0
    even_y = lax.rem(at[2], 2) == 0
    for r0, count in ((0, 8), (8, 64), (72, 8)):
        lane = lanes((count, 128))
        left = jnp.zeros((count, 128), F32)
        right = jnp.zeros((count, 128), F32)
        for f in range(4):
            if r0 == 8:
                a, b = own[f, 0], own[f, 3]
            else:
                from_a = jnp.logical_xor(even_x, r0 == 0)
                a = jnp.where(from_a, got_a[f, :, 0:128], got_b[f, :, 0:128])
                b = jnp.where(from_a, got_a[f, :, COLS - 128 : COLS], got_b[f, :, COLS - 128 : COLS])
            mine = (lane >= 8 * f) & (lane < 8 * f + 8)
            left = jnp.where(mine, rolled(a, 8 * f), left)
            right = jnp.where(mine, rolled(b, 8 * f + 8), right)
        send_a[r0 : r0 + count, :] = jnp.where(even_y, right, left)
        send_b[r0 : r0 + count, :] = jnp.where(even_y, left, right)


def fine_cols(sy, c, shape):
    i = sublanes(shape)
    return sy * COLS + (128 * c + i if c < 4 else jnp.where(i < 64, COLS + i, i - 128))


def coarse_cols(sy, c, ty):
    i = sublanes((128, 64))
    col = sy * CCOLS + (i if c == 0 else jnp.where(i < 64, CCOLS + i, i - 128))
    hit = jnp.zeros((128, 64), F32)
    for offset in range(4):
        hit = hit + jnp.where(jnp.abs(4 * col + offset - ty) <= REACH, 0.25, 0.0)
    return hit


LAST_DIMS = (((1,), (1,)), ((), ()))


def push_kernel(at, after, tx_in, ty_in, yaw_in, fine_push, own_push, tx_ref, ty_ref, yaw_ref, sems):
    fetch([(tx_in, tx_ref), (ty_in, ty_ref), (yaw_in, yaw_ref)], sems)
    tx, ty = tx_ref[...], ty_ref[...]
    mine = sublanes((CUTS, 64)) == at[0]
    wx, wy = yaw_weights(jnp.sum(jnp.where(mine, yaw_ref[...], 0), axis=0, keepdims=True))
    row = at[1] * ROWS - 16 + sublanes((96, 64))
    hit = jnp.where(row == tx, FINE_THRUST, 0.0)
    both = jnp.concatenate([hit * wx, hit * wy], axis=0)
    for c in range(5):
        cols = jnp.where(jnp.abs(fine_cols(at[2], c, (128, 64)) - ty) <= REACH, 1.0, 0.0)
        push = exact_dot(both, cols, LAST_DIMS)
        fine_push[0, c] = push[0:96]
        fine_push[1, c] = push[96:192]
    row = at[1] * CROWS - 10 + sublanes((40, 64))
    hit = jnp.where(row == tx // 4, 0.25 * COARSE_THRUST, 0.0)
    both = jnp.concatenate([hit * wx, hit * wy], axis=0)
    for c in range(2):
        push = exact_dot(both, coarse_cols(at[2], c, ty), LAST_DIMS)
        own_push[0, c] = push[0:40]
        own_push[1, c] = push[40:80]


def chain_push_kernel(at, after, tx_in, ty_in, yaw_in, push, tx_ref, ty_ref, yaw_ref, sems):
    fetch([(tx_in, tx_ref), (ty_in, ty_ref), (yaw_in, yaw_ref)], sems)
    tx, ty = tx_ref[...], ty_ref[...]
    row = at[1] * CROWS - 16 + sublanes((EXT, 64))
    hit = jnp.where(row == tx // 4, 0.25 * COARSE_THRUST, 0.0)
    wx, wy = yaw_weights(yaw_ref[...])
    cols = [coarse_cols(at[2], c, ty) for c in range(2)]
    for n in range(1, CUTS):
        both = jnp.concatenate([hit * wx[n : n + 1, :], hit * wy[n : n + 1, :]], axis=0)
        for c in range(2):
            value = exact_dot(both, cols[c], LAST_DIMS)
            push[n, 0, c] = value[0:EXT]
            push[n, 1, c] = value[EXT : 2 * EXT]


def fine_kernel(at, own, rows_a, rows_b, cols_a, cols_b, push, own_push, fine, guess, sent, coarse_nu,
                one, two, coef, rough, rough_two, rough_coef):
    even_x = lax.rem(at[1], 2) == 0
    even_y = lax.rem(at[2], 2) == 0
    outside, side_mask = edges(at)
    after_all = jnp.where(even_y, cols_a[...], cols_b[...])
    before_all = jnp.where(even_y, cols_b[...], cols_a[...])
    lane = lanes((80, 128))
    for f in range(4):
        for c in range(5):
            if c < 4:
                cut = slice(128 * c, 128 * c + 128)
                a, b = rows_a[f, :, cut], rows_b[f, :, cut]
                pieces = [(8, 8, jnp.where(even_x, b, a)), (16, 64, own[f, c]), (80, 8, jnp.where(even_x, a, b))]
            else:
                after, before = rolled(after_all, -8 * f), rolled(before_all, 120 - 8 * f)
                pieces = [(8, 80, jnp.where(lane < 8, after, jnp.where(lane >= 120, before, 0.0)))]
            for r, count, value in pieces:
                if f < 3:
                    one[f, c, r : r + count, :] = value * FINE_SCALE[f]
                else:
                    coefficients(coef, c, pl.ds(r, count), value, FINE[0])

    i, j = sublanes((COLS, 128)), lanes((COLS, 128))
    gather = jnp.where(i // 4 == j, 0.0625, 0.0)
    i, j = sublanes((128, 128)), lanes((128, 128))
    gather_side = jnp.where(((i < 8) & (i // 4 == j)) | ((i >= 120) & ((i - 120) // 4 == j - 126)), 0.0625, 0.0)

    def row_sum(ref, first, count):
        parts = [ref[pl.ds(first + k, count, stride=4), :] for k in range(4)]
        return (parts[0] + parts[1]) + (parts[2] + parts[3])

    def pick(f, c):
        return one.at[f, c] if f < 3 else coef.at[0, c]

    body = [jnp.concatenate([row_sum(pick(f, c), 0, 24) for c in range(4)], axis=1) for f in range(4)]
    side = [row_sum(pick(f, 4), 0, 24) for f in range(4)]
    body = exact_dot(jnp.concatenate(body, axis=0), gather)
    side = exact_dot(jnp.concatenate(side, axis=0), gather_side)
    rough[...] = jnp.zeros(rough.shape, F32)
    rough_two[...] = jnp.zeros(rough_two.shape, F32)
    rough_coef[...] = jnp.zeros(rough_coef.shape, F32)
    for c, value in enumerate((body, side)):
        for f in range(3):
            rough[f, c, 6:30, :] = value[24 * f : 24 * f + 24, :] * FINE_TO_COARSE[f]
        coefficients(rough_coef, c, pl.ds(6, 24), value[72:96, :] * 0.5, COARSE[0])
    coarse_nu[...] = rough_coef[0, 0, 10:26, :]

    def coarse_push(d, c, r):
        return own_push[d, c, r, :]

    for k in range(3):
        advance(rough, rough_two, rough_coef, coarse_push, 0, 9 + 8 * k, 8, 2, (0, 1), COARSE, side_mask)
    clear_rows(rough_two, 2, 9, 26, outside)
    for k in range(2):
        advance(rough_two, rough, rough_coef, coarse_push, 0, 10 + 8 * k, 8, 2, (0,), COARSE, side_mask)
    for f in range(3):
        guess[16 * f : 16 * f + 16, :] = rough[f, 0, 10:26, :]

    def fine_push(d, c, r):
        return push[d, c, r, :]

    for src, dst, first, count, wanted in (
        (one, two, 12, 9, range(5)),
        (two, one, 12, 9, range(5)),
        (one, two, 12, 9, range(5)),
        (two, one, 16, 8, range(4)),
    ):
        for k in range(count):
            advance(src, dst, coef, fine_push, 0, first + 8 * k, 8, 5, wanted, FINE, side_mask)
        if count == 9:
            clear_rows(dst, 5, 15, 80, outside)
    for f in range(3):
        for c in range(4):
            fine[f, :, 128 * c : 128 * c + 128] = one[f, c, 16:80, :] * (1.0 / FINE_SCALE[f])
    ends = [jnp.concatenate([row_sum(one.at[f, c], 16, 16) for c in range(4)], axis=1) for f in range(3)]
    ends = exact_dot(jnp.concatenate(ends, axis=0), gather)
    first_slice = at[0] == 0
    for f in range(3):
        cut = slice(16 * f, 16 * f + 16)
        defect = ends[cut] * FINE_TO_COARSE[f] - jnp.where(first_slice, 0.0, guess[cut, :])
        for m in range(CUTS):
            sent[m, cut, :] = defect


def plane_of(held, nu, q):
    return nu[...] if q == NU else held[q // 3, 16 * (q % 3) : 16 * (q % 3) + 16, :]


def cols_kernel(at, held, nu, send_a, send_b):
    even_y = lax.rem(at[2], 2) == 0
    lane = lanes((16, 128))
    for g, (width, members) in enumerate(GROUPS):
        left = jnp.zeros((16, 128), F32)
        right = jnp.zeros((16, 128), F32)
        for slot, q in enumerate(members):
            offset = slot * width
            value = plane_of(held, nu, q)
            mine = (lane >= offset) & (lane < offset + width)
            left = jnp.where(mine, rolled(value, offset), left)
            right = jnp.where(mine, rolled(value, offset + width), right)
        send_a[16 * g : 16 * g + 16, :] = jnp.where(even_y, right, left)
        send_b[16 * g : 16 * g + 16, :] = jnp.where(even_y, left, right)


def rows_kernel(at, held, nu, cols_a, cols_b, send_a, send_b):
    even = lax.rem(at[1], 2) == 0
    for q, rows in PARTS:
        place, _ = PART_AT[q]
        value = plane_of(held, nu, q)
        if rows == 16:
            send_a[place : place + 16, :] = value
            send_b[place : place + 16, :] = value
        else:
            send_a[place : place + 8, :] = jnp.where(even, value[8:16], value[0:8])
            send_b[place : place + 8, :] = jnp.where(even, value[0:8], value[8:16])
    for ref in (send_a, send_b):
        ref[STRIP_AT : STRIP_AT + STRIPS, :] = cols_a[...]
        ref[STRIP_AT + STRIPS : MESSAGE, :] = cols_b[...]


def assemble(at, planes, held, nu, cols_a, cols_b, rows_a, rows_b, put):
    even_x = lax.rem(at[1], 2) == 0
    even_y = lax.rem(at[2], 2) == 0
    for q in planes:
        put(q, 0, 16, plane_of(held, nu, q))
        if q in PART_AT:
            place, rows = PART_AT[q]
            a, b = rows_a[place : place + rows, :], rows_b[place : place + rows, :]
            put(q, 0, 16 - rows, jnp.where(even_x, b, a))
            put(q, 0, 32, jnp.where(even_x, a, b))
    lane = lanes((16, 128))
    for g, (width, members) in enumerate(GROUPS):
        if not any(q in planes for q in members):
            continue
        cut = slice(16 * g, 16 * g + 16)
        cut_a = slice(STRIP_AT + 16 * g, STRIP_AT + 16 * g + 16)
        cut_b = slice(STRIP_AT + STRIPS + 16 * g, STRIP_AT + STRIPS + 16 * g + 16)
        for first, a, b in (
            (16, cols_a[cut, :], cols_b[cut, :]),
            (0, jnp.where(even_x, rows_b[cut_a, :], rows_a[cut_a, :]), jnp.where(even_x, rows_b[cut_b, :], rows_a[cut_b, :])),
            (32, jnp.where(even_x, rows_a[cut_a, :], rows_b[cut_a, :]), jnp.where(even_x, rows_a[cut_b, :], rows_b[cut_b, :])),
        ):
            after, before = jnp.where(even_y, a, b), jnp.where(even_y, b, a)
            for slot, q in enumerate(members):
                if q in planes and (first == 16 or q in PART_AT):
                    hi, lo = rolled(after, -slot * width), rolled(before, 128 - width - slot * width)
                    put(q, 1, first, jnp.where(lane < width, hi, jnp.where(lane >= 128 - width, lo, 0.0)))


def chain(first_n, last_n, one, two, coef, push, added, at, save):
    outside, side_mask = edges(at)
    for n in range(first_n, last_n + 1):
        def pushed(d, c, r, n=n):
            return push[n, d, c, r, :]

        for half in range(2):
            halo = 2 * (last_n - n) + 1 - half
            count = 2 + -(-halo // 4)
            first = min(8 + 16 - halo, 8 + EXT - 8 * count)
            src, dst = (one, two) if half == 0 else (two, one)
            post = None
            if half == 1:
                def post(f, c, r, value, n=n):
                    return save(n, f, c, r, value, added)

            for k in range(count):
                advance(src, dst, coef, pushed, 8, first + 8 * k, 8, 2, (0, 1), COARSE, side_mask, post=post)
            if halo:
                clear_rows(dst, 2, 8 + 15, 8 + 32, outside)


def with_defect(kept, extra, first_plane, last):
    def save(n, f, c, r, value, added):
        if c == 0:
            kept[n % HALF, f, r, :] = value
        if n == last:
            return value
        return value + extra[3 * n + f - first_plane, c, pl.ds(r.start - 8, r.size), :]

    return save


def lower_kernel(at, held, nu, cols_a, cols_b, rows_a, rows_b, push, state, moved, coef, one, two, extra, kept):
    planes = list(range(3 * HALF)) + [NU]

    def put(q, c, row, value):
        rows = pl.ds(row, value.shape[0])
        if q == NU:
            coefficients(coef, c, rows, value, COARSE[0])
        elif q < 3:
            one[q, c, pl.ds(row + 8, value.shape[0]), :] = value
        else:
            extra[q - 3, c, rows, :] = value

    assemble(at, planes, held, nu, cols_a, cols_b, rows_a, rows_b, put)
    chain(1, HALF - 1, one, two, coef, push, extra, at, with_defect(kept, extra, 3, None))
    for f in range(3):
        for c in range(2):
            state[2 * f + c] = one[f, c, 24:40, :]
    mine = jnp.clip(at[0], 1, HALF - 1)
    for f in range(3):
        moved[16 * f : 16 * f + 16, :] = kept[mine, f, 24:40, :]


def upper_fields_kernel(at, held, nu, cols_a, cols_b, rows_a, rows_b, extra):
    planes = list(range(3 * HALF, NU))

    def put(q, c, row, value):
        extra[q - 3 * HALF, c, pl.ds(row, value.shape[0]), :] = value

    assemble(at, planes, held, nu, cols_a, cols_b, rows_a, rows_b, put)


def upper_kernel(at, state, state_a, state_b, extra, coef, push, fine, guess, moved, out, one, two, kept):
    even_x = lax.rem(at[1], 2) == 0
    for f in range(3):
        for c in range(2):
            a, b = state_a[2 * f + c], state_b[2 * f + c]
            one[f, c, 8:24, :] = jnp.where(even_x, b, a)
            one[f, c, 24:40, :] = state[2 * f + c]
            one[f, c, 40:56, :] = jnp.where(even_x, a, b)
    chain(HALF, CUTS - 1, one, two, coef, push, extra, at, with_defect(kept, extra, 3 * HALF, CUTS - 1))
    mine = jnp.maximum(at[0] - HALF, 0)
    parts = []
    for f in range(3):
        cut = slice(16 * f, 16 * f + 16)
        value = jnp.where(at[0] < HALF, moved[cut, :], kept[mine, f, 24:40, :]) - guess[cut, :]
        parts.append(jnp.where(at[0] == 0, 0.0, value * (1.0 / COARSE_SCALE[f])))
    change = jnp.concatenate(parts, axis=0)
    i, j = sublanes((3 * ROWS, 48)), lanes((3 * ROWS, 48))
    repeat_rows = jnp.where(i // 4 == j, 1.0, 0.0)
    i, j = sublanes((128, COLS)), lanes((128, COLS))
    repeat_cols = jnp.where(i == j // 4, 1.0, 0.0)
    change = exact_dot(dot_exact(repeat_rows, change), repeat_cols)
    for f in range(3):
        out[f] = fine[f] + change[ROWS * f : ROWS * f + ROWS, :]


SMEM = pl.BlockSpec(memory_space=pltpu.SMEM)
VMEM = pl.BlockSpec(memory_space=pltpu.VMEM)
ANY = pl.BlockSpec(memory_space=pl.ANY)


def call(kernel, args, outs, scratch=(), far=0, sems=0):
    shapes = [jax.ShapeDtypeStruct(s, F32) for s in outs]
    near = len(args) - 1 - far
    memory = [s if not isinstance(s, tuple) else pltpu.VMEM(s, F32) for s in scratch]
    if sems:
        memory.append(pltpu.SemaphoreType.DMA((sems,)))
    return pl.pallas_call(
        kernel,
        out_shape=shapes,
        in_specs=[SMEM] + [VMEM] * near + [ANY] * far,
        out_specs=[VMEM] * len(shapes),
        scratch_shapes=memory,
        compiler_params=pltpu.CompilerParams(vmem_limit_bytes=48 * 1024 * 1024),
    )(*args)


def swap(x, axis, pairs):
    return lax.ppermute(x, axis, [(a, b) for a, b in pairs] + [(b, a) for a, b in pairs])


def on_device(starts, viscosity, turbine_x, turbine_y, yaw_index):
    count_x, count_y = lax.axis_size("sx"), lax.axis_size("sy")
    at = jnp.stack([
        lax.axis_index("cuts"), lax.axis_index("sx"), lax.axis_index("sy"),
        jnp.int32(count_x), jnp.int32(count_y),
    ]).astype(jnp.int32)
    start = starts[0]
    x_a = [(i, i + 1) for i in range(0, count_x - 1, 2)]
    x_b = [(i, i + 1) for i in range(1, count_x - 1, 2)]
    y_a = [(i, i + 1) for i in range(0, count_y - 1, 2)]
    y_b = [(i, i + 1) for i in range(1, count_y - 1, 2)]
    turbines = (turbine_x[None, :], turbine_y[None, :], yaw_index)
    turbine_scratch = [pltpu.VMEM((1, 64), jnp.int32), pltpu.VMEM((1, 64), jnp.int32), pltpu.VMEM((CUTS, 64), jnp.int32)]

    edge = (4, 8, COLS)
    send_a, send_b = call(edge_kernel, (at, start, viscosity), [edge, edge], far=2, sems=4)
    rows_a = swap(send_a, "sx", x_a)
    rows_b = swap(send_b, "sx", x_b)
    (own,) = call(load_kernel, (at, send_b, start, viscosity), [(4, 4, ROWS, 128)], far=3, sems=8)
    send_a, send_b = call(side_kernel, (at, own, rows_a, rows_b), [(80, 128)] * 2)
    cols_a = swap(send_a, "sy", y_a)
    cols_b = swap(send_b, "sy", y_b)
    push, own_push = call(
        push_kernel, (at, send_b) + turbines, [(2, 5, 96, 128), (2, 2, 40, 128)], turbine_scratch, far=4, sems=3)
    fine, guess, sent, coarse_nu = call(
        fine_kernel,
        (at, own, rows_a, rows_b, cols_a, cols_b, push, own_push),
        [(3, ROWS, COLS), (48, 128), (CUTS, 48, 128), (CROWS, 128)],
        [(3, 5, 96, 128), (3, 5, 96, 128), (4, 5, 96, 128), (3, 2, 40, 128), (3, 2, 40, 128), (4, 2, 40, 128)],
    )
    held = lax.all_to_all(sent, "cuts", 0, 0)
    send_a, send_b = call(cols_kernel, (at, held, coarse_nu), [(STRIPS, 128)] * 2)
    cols_a = swap(send_a, "sy", y_a)
    cols_b = swap(send_b, "sy", y_b)
    (chain_push,) = call(
        chain_push_kernel, (at, send_b) + turbines, [(CUTS, 2, 2, EXT, 128)], turbine_scratch, far=4, sems=3)
    send_a, send_b = call(rows_kernel, (at, held, coarse_nu, cols_a, cols_b), [(MESSAGE, 128)] * 2)
    rows_a = swap(send_a, "sx", x_a)
    rows_b = swap(send_b, "sx", x_b)
    blocks = (at, held, coarse_nu, cols_a, cols_b, rows_a, rows_b)
    planes = 3 * HALF - 3
    field = (3, 2, 64, 128)
    state, moved, coef = call(
        lower_kernel, blocks + (chain_push,),
        [(6, CROWS, 128), (48, 128), (4, 2, EXT, 128)],
        [field, field, (planes, 2, EXT, 128), (HALF, 3, 64, 128)],
    )
    state_a = swap(state, "sx", x_a)
    state_b = swap(state, "sx", x_b)
    (extra,) = call(upper_fields_kernel, blocks, [(planes, 2, EXT, 128)])
    (out,) = call(
        upper_kernel,
        (at, state, state_a, state_b, extra, coef, chain_push, fine, guess, moved),
        [(3, ROWS, COLS)],
        [field, field, (HALF, 3, 64, 128)],
    )
    return out[None]


def solution(mesh):
    in_specs = (P("cuts", None, "sx", "sy"), P("sx", "sy"), P(), P(), P())
    out_specs = P("cuts", None, "sx", "sy")
    return jax.shard_map(
        on_device, mesh=mesh, in_specs=in_specs, out_specs=out_specs, check_vma=False
    )
```

```python
import math

import jax
import jax.numpy as jnp
import numpy as np
from jax import lax
from jax.experimental import pallas as pl
from jax.experimental.pallas import tpu as pltpu
from jax.sharding import PartitionSpec as P

YAWS = 7
CUTS = 16
REACH = 3
F32 = jnp.float32
BF16 = jnp.bfloat16

FINE = (0.3, 0.25, 0.01)
FINE_THRUST = 0.5
FINE_SCALE = (0.25, 0.25, 0.025)
COARSE = (0.15, 0.125, 0.0025)
COARSE_THRUST = 1.0
COARSE_SCALE = (0.125, 0.125, 0.00625)
FINE_TO_COARSE = (0.5, 0.5, 0.25)

ROWS, COLS = 64, 512
CROWS, CCOLS = 16, 128
HALF = CUTS // 2
EXT = 48
NU = 24
ANGLES = [(k - 0.5 * (YAWS - 1)) * (math.pi / 18.0) for k in range(YAWS)]
WEIGHT_X = [float(np.float32(math.cos(t) ** 3)) for t in ANGLES]
WEIGHT_Y = [float(np.float32(math.cos(t) ** 2 * math.sin(t))) for t in ANGLES]

WIDTH = 32
_ORDER = list(range(21)) + [NU, 21, 22, 23]
GROUPS = [_ORDER[_i : _i + 4] for _i in range(0, len(_ORDER), 4)]
STRIPS = 16 * len(GROUPS)
ROW_STRIPS = 16 * 6
PARTS = [(q, 16) for q in range(0, 9)] + [(q, 8) for q in range(9, 21)] + [(NU, 16)]
PART_AT = {}
_at = 0
for _q, _rows in PARTS:
    PART_AT[_q] = (_at, _rows)
    _at += _rows
STRIP_AT = _at
MESSAGE = STRIP_AT + 2 * ROW_STRIPS


def lanes(shape):
    return lax.broadcasted_iota(jnp.int32, shape, len(shape) - 1)


def sublanes(shape):
    return lax.broadcasted_iota(jnp.int32, shape, len(shape) - 2)


def rolled(x, by):
    return pltpu.roll(x, by % 128, 1) if by % 128 else x


def split3(x):
    high = x.astype(BF16)
    rest = x - high.astype(F32)
    middle = rest.astype(BF16)
    return high, middle, (rest - middle.astype(F32)).astype(BF16)


def exact_dot(x, y, dims=(((1,), (0,)), ((), ()))):
    y = y.astype(BF16)
    a, b, c = [lax.dot_general(part, y, dims, preferred_element_type=F32) for part in split3(x)]
    return a + (b + c)


def dot_exact(y, x):
    y = y.astype(BF16)
    a, b, c = [jnp.dot(y, part, preferred_element_type=F32) for part in split3(x)]
    return a + (b + c)


def advance(src, dst, coef, push, shift, row, count, tiles, wanted, terms, side_mask, post=None):
    _, lift, gain = terms
    lane = lanes((count, 128))
    low, high = lane == 0, lane == 127
    here, east, west = pl.ds(row, count), pl.ds(row + 1, count), pl.ds(row - 1, count)
    there = pl.ds(row - shift, count)
    mid = [[src[f, c, here, :] for c in range(tiles)] for f in range(3)]
    up = [[pltpu.roll(mid[f][c], 127, 1) for c in range(tiles)] for f in range(3)]
    down = [[pltpu.roll(mid[f][c], 1, 1) for c in range(tiles)] for f in range(3)]
    for c in wanted:
        after, before = (c + 1) % tiles, (c - 1) % tiles
        u, v, p = mid[0][c], mid[1][c], mid[2][c]
        un, vn, pn = [jnp.where(high, up[f][after], up[f][c]) for f in range(3)]
        us, vs, ps = [jnp.where(low, down[f][before], down[f][c]) for f in range(3)]
        ue, ve, pe = [src[f, c, east, :] for f in range(3)]
        uw, vw, pw = [src[f, c, west, :] for f in range(3)]
        nu, nu_carry, keep, keep_p = [coef[k, c, there, :] for k in range(4)]
        to_east, to_west = nu - u, nu_carry + u
        lifted = u + lift
        size = jnp.abs(lifted)
        drag = lifted * size / (size + lift)
        new_u = ue * to_east + uw * to_west + nu * (un + us) + keep * u - (pe - pw) - push(0, c, there) * drag
        new_v = ve * to_east + vw * to_west + nu * (vn + vs) + keep * v - (pn - ps) - push(1, c, there) * drag
        new_p = nu * ((pe + pw) + (pn + ps)) + keep_p * p - gain * ((ue - uw) + (vn - vs))
        new = [new_u, new_v, new_p]
        if c == tiles - 1:
            new = [f * side_mask for f in new]
        for f in range(3):
            if post is not None:
                new[f] = post(f, c, here, new[f])
            dst[f, c, here, :] = new[f]


def clear_rows(ref, tiles, before, after, outside):
    for row, factor in ((before, outside[0]), (after, outside[1])):
        for f in range(3):
            for c in range(tiles):
                ref[f, c, pl.ds(row, 1), :] = ref[f, c, pl.ds(row, 1), :] * factor


def edges(at):
    lane = lanes((8, 128))
    outside = [jnp.where(at[1] > 0, 1.0, 0.0), jnp.where(at[1] < at[3] - 1, 1.0, 0.0)]
    side = jnp.where(lane < 64, jnp.where(at[2] < at[4] - 1, 1.0, 0.0), jnp.where(at[2] > 0, 1.0, 0.0))
    return outside, side


def coefficients(coef, c, rows, nu, carry):
    coef[0, c, rows, :] = nu
    coef[1, c, rows, :] = nu + carry
    coef[2, c, rows, :] = (1.0 - carry) - 4.0 * nu
    coef[3, c, rows, :] = 1.0 - 4.0 * nu


def yaw_weights(yaw):
    wx = jnp.zeros(yaw.shape, F32)
    wy = jnp.zeros(yaw.shape, F32)
    for k in range(YAWS):
        hit = yaw == k
        wx = jnp.where(hit, WEIGHT_X[k], wx)
        wy = jnp.where(hit, WEIGHT_Y[k], wy)
    return wx, wy


def fetch(pairs, sems):
    copies = [pltpu.make_async_copy(a, b, sems.at[i]) for i, (a, b) in enumerate(pairs)]
    for copy in copies:
        copy.start()
    for copy in copies:
        copy.wait()


def edge_kernel(at, start, visc, send_a, send_b, sems):
    last = pl.multiple_of(56 * (1 - lax.rem(at[1], 2)), 8)
    first = pl.multiple_of(56 * lax.rem(at[1], 2), 8)
    fetch([
        (start.at[:, pl.ds(last, 8), :], send_a.at[0:3]),
        (visc.at[pl.ds(last, 8), :], send_a.at[3]),
        (start.at[:, pl.ds(first, 8), :], send_b.at[0:3]),
        (visc.at[pl.ds(first, 8), :], send_b.at[3]),
    ], sems)


def load_kernel(at, after, start, visc, out, sems):
    fetch(
        [(start.at[:, :, 128 * c : 128 * c + 128], out.at[0:3, c]) for c in range(4)]
        + [(visc.at[:, 128 * c : 128 * c + 128], out.at[3, c]) for c in range(4)],
        sems,
    )


def side_kernel(at, own, got_a, got_b, send_a, send_b):
    even_x = lax.rem(at[1], 2) == 0
    even_y = lax.rem(at[2], 2) == 0
    for r0, count in ((0, 8), (8, 64), (72, 8)):
        lane = lanes((count, 128))
        left = jnp.zeros((count, 128), F32)
        right = jnp.zeros((count, 128), F32)
        for f in range(4):
            if r0 == 8:
                a, b = own[f, 0], own[f, 3]
            else:
                from_a = jnp.logical_xor(even_x, r0 == 0)
                a = jnp.where(from_a, got_a[f, :, 0:128], got_b[f, :, 0:128])
                b = jnp.where(from_a, got_a[f, :, COLS - 128 : COLS], got_b[f, :, COLS - 128 : COLS])
            mine = (lane >= 8 * f) & (lane < 8 * f + 8)
            left = jnp.where(mine, rolled(a, 8 * f), left)
            right = jnp.where(mine, rolled(b, 8 * f + 8), right)
        send_a[r0 : r0 + count, :] = jnp.where(even_y, right, left)
        send_b[r0 : r0 + count, :] = jnp.where(even_y, left, right)


def fine_cols(sy, c, shape):
    i = sublanes(shape)
    return sy * COLS + (128 * c + i if c < 4 else jnp.where(i < 64, COLS + i, i - 128))


def coarse_cols(sy, c, ty):
    i = sublanes((128, 64))
    col = sy * CCOLS + (i if c == 0 else jnp.where(i < 64, CCOLS + i, i - 128))
    hit = jnp.zeros((128, 64), F32)
    for offset in range(4):
        hit = hit + jnp.where(jnp.abs(4 * col + offset - ty) <= REACH, 0.25, 0.0)
    return hit


LAST_DIMS = (((1,), (1,)), ((), ()))


def push_kernel(at, after, tx_in, ty_in, yaw_in, fine_push, own_push, tx_ref, ty_ref, yaw_ref, sems):
    fetch([(tx_in, tx_ref), (ty_in, ty_ref), (yaw_in, yaw_ref)], sems)
    tx, ty = tx_ref[...], ty_ref[...]
    mine = sublanes((CUTS, 64)) == at[0]
    wx, wy = yaw_weights(jnp.sum(jnp.where(mine, yaw_ref[...], 0), axis=0, keepdims=True))
    row = at[1] * ROWS - 16 + sublanes((96, 64))
    hit = jnp.where(row == tx, FINE_THRUST, 0.0)
    both = jnp.concatenate([hit * wx, hit * wy], axis=0)
    for c in range(5):
        cols = jnp.where(jnp.abs(fine_cols(at[2], c, (128, 64)) - ty) <= REACH, 1.0, 0.0)
        push = exact_dot(both, cols, LAST_DIMS)
        fine_push[0, c] = push[0:96]
        fine_push[1, c] = push[96:192]
    row = at[1] * CROWS - 10 + sublanes((40, 64))
    hit = jnp.where(row == tx // 4, 0.25 * COARSE_THRUST, 0.0)
    both = jnp.concatenate([hit * wx, hit * wy], axis=0)
    for c in range(2):
        push = exact_dot(both, coarse_cols(at[2], c, ty), LAST_DIMS)
        own_push[0, c] = push[0:40]
        own_push[1, c] = push[40:80]


def chain_push_kernel(at, after, tx_in, ty_in, yaw_in, push, tx_ref, ty_ref, yaw_ref, sems):
    fetch([(tx_in, tx_ref), (ty_in, ty_ref), (yaw_in, yaw_ref)], sems)
    tx, ty = tx_ref[...], ty_ref[...]
    row = at[1] * CROWS - 16 + sublanes((EXT, 64))
    hit = jnp.where(row == tx // 4, 0.25 * COARSE_THRUST, 0.0)
    wx, wy = yaw_weights(yaw_ref[pl.ds(pl.multiple_of(at[0] // HALF * HALF, HALF), HALF), :])
    cols = [coarse_cols(at[2], c, ty) for c in range(2)]
    for k in range(HALF):
        both = jnp.concatenate([hit * wx[k : k + 1, :], hit * wy[k : k + 1, :]], axis=0)
        for c in range(2):
            value = exact_dot(both, cols[c], LAST_DIMS)
            push[k, 0, c] = value[0:EXT]
            push[k, 1, c] = value[EXT : 2 * EXT]


def fine_kernel(at, own, rows_a, rows_b, cols_a, cols_b, push, own_push, fine, guess, sent, coarse_nu,
                one, two, coef, rough, rough_two, rough_coef):
    even_x = lax.rem(at[1], 2) == 0
    even_y = lax.rem(at[2], 2) == 0
    outside, side_mask = edges(at)
    after_all = jnp.where(even_y, cols_a[...], cols_b[...])
    before_all = jnp.where(even_y, cols_b[...], cols_a[...])
    lane = lanes((80, 128))
    for f in range(4):
        for c in range(5):
            if c < 4:
                cut = slice(128 * c, 128 * c + 128)
                a, b = rows_a[f, :, cut], rows_b[f, :, cut]
                pieces = [(8, 8, jnp.where(even_x, b, a)), (16, 64, own[f, c]), (80, 8, jnp.where(even_x, a, b))]
            else:
                after, before = rolled(after_all, -8 * f), rolled(before_all, 120 - 8 * f)
                pieces = [(8, 80, jnp.where(lane < 8, after, jnp.where(lane >= 120, before, 0.0)))]
            for r, count, value in pieces:
                if f < 3:
                    one[f, c, r : r + count, :] = value * FINE_SCALE[f]
                else:
                    coefficients(coef, c, pl.ds(r, count), value, FINE[0])

    i, j = sublanes((COLS, 128)), lanes((COLS, 128))
    gather = jnp.where(i // 4 == j, 0.0625, 0.0)
    i, j = sublanes((128, 128)), lanes((128, 128))
    gather_side = jnp.where(((i < 8) & (i // 4 == j)) | ((i >= 120) & ((i - 120) // 4 == j - 126)), 0.0625, 0.0)

    def row_sum(ref, first, count):
        parts = [ref[pl.ds(first + k, count, stride=4), :] for k in range(4)]
        return (parts[0] + parts[1]) + (parts[2] + parts[3])

    def pick(f, c):
        return one.at[f, c] if f < 3 else coef.at[0, c]

    body = [jnp.concatenate([row_sum(pick(f, c), 0, 24) for c in range(4)], axis=1) for f in range(4)]
    side = [row_sum(pick(f, 4), 0, 24) for f in range(4)]
    body = exact_dot(jnp.concatenate(body, axis=0), gather)
    side = exact_dot(jnp.concatenate(side, axis=0), gather_side)
    rough[...] = jnp.zeros(rough.shape, F32)
    rough_two[...] = jnp.zeros(rough_two.shape, F32)
    rough_coef[...] = jnp.zeros(rough_coef.shape, F32)
    for c, value in enumerate((body, side)):
        for f in range(3):
            rough[f, c, 6:30, :] = value[24 * f : 24 * f + 24, :] * FINE_TO_COARSE[f]
        coefficients(rough_coef, c, pl.ds(6, 24), value[72:96, :] * 0.5, COARSE[0])
    coarse_nu[...] = rough_coef[0, 0, 10:26, :]

    def coarse_push(d, c, r):
        return own_push[d, c, r, :]

    for k in range(3):
        advance(rough, rough_two, rough_coef, coarse_push, 0, 9 + 8 * k, 8, 2, (0, 1), COARSE, side_mask)
    clear_rows(rough_two, 2, 9, 26, outside)
    for k in range(2):
        advance(rough_two, rough, rough_coef, coarse_push, 0, 10 + 8 * k, 8, 2, (0,), COARSE, side_mask)
    for f in range(3):
        guess[16 * f : 16 * f + 16, :] = rough[f, 0, 10:26, :]

    def fine_push(d, c, r):
        return push[d, c, r, :]

    for src, dst, first, count, wanted in (
        (one, two, 12, 9, range(5)),
        (two, one, 12, 9, range(5)),
        (one, two, 12, 9, range(5)),
        (two, one, 16, 8, range(4)),
    ):
        for k in range(count):
            advance(src, dst, coef, fine_push, 0, first + 8 * k, 8, 5, wanted, FINE, side_mask)
        if count == 9:
            clear_rows(dst, 5, 15, 80, outside)
    for f in range(3):
        for c in range(4):
            fine[f, :, 128 * c : 128 * c + 128] = one[f, c, 16:80, :] * (1.0 / FINE_SCALE[f])
    ends = [jnp.concatenate([row_sum(one.at[f, c], 16, 16) for c in range(4)], axis=1) for f in range(3)]
    ends = exact_dot(jnp.concatenate(ends, axis=0), gather)
    first_slice = at[0] == 0
    for f in range(3):
        cut = slice(16 * f, 16 * f + 16)
        defect = ends[cut] * FINE_TO_COARSE[f] - jnp.where(first_slice, 0.0, guess[cut, :])
        for m in range(HALF):
            sent[m, cut, :] = defect


def plane_of(held, nu, q):
    return nu[...] if q == NU else held[q // 3, 16 * (q % 3) : 16 * (q % 3) + 16, :]


def cols_kernel(at, held, nu, send_a, send_b):
    even_y = lax.rem(at[2], 2) == 0
    lane = lanes((16, 128))
    for g, members in enumerate(GROUPS):
        left = jnp.zeros((16, 128), F32)
        right = jnp.zeros((16, 128), F32)
        for slot, q in enumerate(members):
            offset = slot * WIDTH
            value = plane_of(held, nu, q)
            mine = (lane >= offset) & (lane < offset + WIDTH)
            left = jnp.where(mine, rolled(value, offset), left)
            right = jnp.where(mine, rolled(value, offset + WIDTH), right)
        send_a[16 * g : 16 * g + 16, :] = jnp.where(even_y, right, left)
        send_b[16 * g : 16 * g + 16, :] = jnp.where(even_y, left, right)


def rows_kernel(at, held, nu, cols_a, cols_b, send_a, send_b):
    even = lax.rem(at[1], 2) == 0
    for q, rows in PARTS:
        place, _ = PART_AT[q]
        value = plane_of(held, nu, q)
        if rows == 16:
            send_a[place : place + 16, :] = value
            send_b[place : place + 16, :] = value
        else:
            send_a[place : place + 8, :] = jnp.where(even, value[8:16], value[0:8])
            send_b[place : place + 8, :] = jnp.where(even, value[0:8], value[8:16])
    for ref in (send_a, send_b):
        ref[STRIP_AT : STRIP_AT + ROW_STRIPS, :] = cols_a[0:ROW_STRIPS, :]
        ref[STRIP_AT + ROW_STRIPS : MESSAGE, :] = cols_b[0:ROW_STRIPS, :]


def assemble(at, held, nu, cols_a, cols_b, rows_a, rows_b, put):
    even_x = lax.rem(at[1], 2) == 0
    even_y = lax.rem(at[2], 2) == 0
    for q in range(NU + 1):
        put(q, 0, 16, plane_of(held, nu, q))
        if q in PART_AT:
            place, rows = PART_AT[q]
            a, b = rows_a[place : place + rows, :], rows_b[place : place + rows, :]
            put(q, 0, 16 - rows, jnp.where(even_x, b, a))
            put(q, 0, 32, jnp.where(even_x, a, b))
    lane = lanes((16, 128))
    for g, members in enumerate(GROUPS):
        cut = slice(16 * g, 16 * g + 16)
        blocks = [(16, cols_a[cut, :], cols_b[cut, :])]
        if 16 * g < ROW_STRIPS:
            cut_a = slice(STRIP_AT + 16 * g, STRIP_AT + 16 * g + 16)
            cut_b = slice(STRIP_AT + ROW_STRIPS + 16 * g, STRIP_AT + ROW_STRIPS + 16 * g + 16)
            aa, ab, ba, bb = rows_a[cut_a, :], rows_a[cut_b, :], rows_b[cut_a, :], rows_b[cut_b, :]
            blocks.append((0, jnp.where(even_x, ba, aa), jnp.where(even_x, bb, ab)))
            blocks.append((32, jnp.where(even_x, aa, ba), jnp.where(even_x, ab, bb)))
        for first, a, b in blocks:
            after, before = jnp.where(even_y, a, b), jnp.where(even_y, b, a)
            for slot, q in enumerate(members):
                if first == 16 or q in PART_AT:
                    hi, lo = rolled(after, -slot * WIDTH), rolled(before, 128 - WIDTH - slot * WIDTH)
                    put(q, 1, first, jnp.where(lane < WIDTH, hi, jnp.where(lane >= 128 - WIDTH, lo, 0.0)))


def chain(first_k, one, two, coef, push, extra, kept, at):
    outside, side_mask = edges(at)

    for k in range(first_k, HALF):
        def pushed(d, c, r, k=k):
            return push[k, d, c, r, :]

        def keep_and_add(f, c, r, value, k=k):
            if c == 0:
                kept[k, f, r, :] = value
            return value + extra[3 * k + f, c, pl.ds(r.start - 8, r.size), :]

        for half in range(2):
            halo = 2 * (HALF - 1 - k) + 1 - half
            count = 2 + -(-halo // 4)
            first = min(8 + 16 - halo, 8 + EXT - 8 * count)
            src, dst = (one, two) if half == 0 else (two, one)
            post = keep_and_add if half else None
            for i in range(count):
                advance(src, dst, coef, pushed, 8, first + 8 * i, 8, 2, (0, 1), COARSE, side_mask, post=post)
            if halo:
                clear_rows(dst, 2, 8 + 15, 8 + 32, outside)


def low_kernel(at, held, nu, cols_a, cols_b, rows_a, rows_b, push, state, moved, extra, coef, one, two, kept):
    def put(q, c, row, value):
        rows = pl.ds(row, value.shape[0])
        if q == NU:
            coefficients(coef, c, rows, value, COARSE[0])
        else:
            extra[q, c, rows, :] = value

    assemble(at, held, nu, cols_a, cols_b, rows_a, rows_b, put)

    @pl.when(at[0] < HALF)
    def _():
        for f in range(3):
            for c in range(2):
                one[f, c, 8:56, :] = extra[f, c]
        chain(1, one, two, coef, push, extra, kept, at)
        for f in range(3):
            for c in range(2):
                state[2 * f + c] = one[f, c, 24:40, :]
            moved[16 * f : 16 * f + 16, :] = kept[jnp.maximum(at[0], 1), f, 24:40, :]


def high_kernel(at, state, state_a, state_b, extra, coef, push, fine, guess, moved_low, out, one, two, kept, moved):
    even_x = lax.rem(at[1], 2) == 0

    @pl.when(at[0] < HALF)
    def _():
        moved[...] = moved_low[...]

    @pl.when(at[0] >= HALF)
    def _():
        for f in range(3):
            for c in range(2):
                a, b = state_a[2 * f + c], state_b[2 * f + c]
                one[f, c, 8:24, :] = jnp.where(even_x, b, a)
                one[f, c, 24:40, :] = state[2 * f + c]
                one[f, c, 40:56, :] = jnp.where(even_x, a, b)
        chain(0, one, two, coef, push, extra, kept, at)
        for f in range(3):
            moved[16 * f : 16 * f + 16, :] = kept[at[0] - HALF, f, 24:40, :]

    parts = []
    for f in range(3):
        cut = slice(16 * f, 16 * f + 16)
        parts.append(jnp.where(at[0] == 0, 0.0, (moved[cut, :] - guess[cut, :]) * (1.0 / COARSE_SCALE[f])))
    change = jnp.concatenate(parts, axis=0)
    i, j = sublanes((3 * ROWS, 48)), lanes((3 * ROWS, 48))
    repeat_rows = jnp.where(i // 4 == j, 1.0, 0.0)
    i, j = sublanes((128, COLS)), lanes((128, COLS))
    repeat_cols = jnp.where(i == j // 4, 1.0, 0.0)
    change = exact_dot(dot_exact(repeat_rows, change), repeat_cols)
    for f in range(3):
        out[f] = fine[f] + change[ROWS * f : ROWS * f + ROWS, :]


SMEM = pl.BlockSpec(memory_space=pltpu.SMEM)
VMEM = pl.BlockSpec(memory_space=pltpu.VMEM)
ANY = pl.BlockSpec(memory_space=pl.ANY)


def call(kernel, args, outs, scratch=(), far=0, sems=0, grant=48):
    shapes = [jax.ShapeDtypeStruct(s, F32) for s in outs]
    near = len(args) - 1 - far
    memory = [s if not isinstance(s, tuple) else pltpu.VMEM(s, F32) for s in scratch]
    if sems:
        memory.append(pltpu.SemaphoreType.DMA((sems,)))
    return pl.pallas_call(
        kernel,
        out_shape=shapes,
        in_specs=[SMEM] + [VMEM] * near + [ANY] * far,
        out_specs=[VMEM] * len(shapes),
        scratch_shapes=memory,
        compiler_params=pltpu.CompilerParams(vmem_limit_bytes=grant * 1024 * 1024) if grant else None,
    )(*args)


def swap(x, axis, pairs):
    return lax.ppermute(x, axis, [(a, b) for a, b in pairs] + [(b, a) for a, b in pairs])


def swap_high(x, count, pairs):
    both = [(a, b) for a, b in pairs] + [(b, a) for a, b in pairs]
    return lax.ppermute(x, ("cuts", "sx"), [(n * count + a, n * count + b) for n in range(HALF, CUTS) for a, b in both])


def on_device(starts, viscosity, turbine_x, turbine_y, yaw_index):
    count_x, count_y = lax.axis_size("sx"), lax.axis_size("sy")
    at = jnp.stack([
        lax.axis_index("cuts"), lax.axis_index("sx"), lax.axis_index("sy"),
        jnp.int32(count_x), jnp.int32(count_y),
    ]).astype(jnp.int32)
    start = starts[0]
    x_a = [(i, i + 1) for i in range(0, count_x - 1, 2)]
    x_b = [(i, i + 1) for i in range(1, count_x - 1, 2)]
    y_a = [(i, i + 1) for i in range(0, count_y - 1, 2)]
    y_b = [(i, i + 1) for i in range(1, count_y - 1, 2)]
    turbines = (turbine_x[None, :], turbine_y[None, :], yaw_index)
    turbine_scratch = [pltpu.VMEM((1, 64), jnp.int32), pltpu.VMEM((1, 64), jnp.int32), pltpu.VMEM((CUTS, 64), jnp.int32)]

    edge = (4, 8, COLS)
    send_a, send_b = call(edge_kernel, (at, start, viscosity), [edge, edge], far=2, sems=4, grant=0)
    rows_a = swap(send_a, "sx", x_a)
    rows_b = swap(send_b, "sx", x_b)
    (own,) = call(load_kernel, (at, send_b, start, viscosity), [(4, 4, ROWS, 128)], far=3, sems=8, grant=0)
    send_a, send_b = call(side_kernel, (at, own, rows_a, rows_b), [(80, 128)] * 2)
    cols_a = swap(send_a, "sy", y_a)
    cols_b = swap(send_b, "sy", y_b)
    push, own_push = call(
        push_kernel, (at, send_b) + turbines, [(2, 5, 96, 128), (2, 2, 40, 128)], turbine_scratch, far=4, sems=3)
    fine, guess, sent, coarse_nu = call(
        fine_kernel,
        (at, own, rows_a, rows_b, cols_a, cols_b, push, own_push),
        [(3, ROWS, COLS), (48, 128), (HALF, 48, 128), (CROWS, 128)],
        [(3, 5, 96, 128), (3, 5, 96, 128), (4, 5, 96, 128), (3, 2, 40, 128), (3, 2, 40, 128), (4, 2, 40, 128)],
    )
    halves = [list(range(HALF)), list(range(HALF, CUTS))]
    held = lax.all_to_all(sent, "cuts", 0, 0, axis_index_groups=halves)
    send_a, send_b = call(cols_kernel, (at, held, coarse_nu), [(STRIPS, 128)] * 2)
    cols_a = swap(send_a, "sy", y_a)
    cols_b = swap(send_b, "sy", y_b)
    (chain_push,) = call(
        chain_push_kernel, (at, send_b) + turbines, [(HALF, 2, 2, EXT, 128)], turbine_scratch, far=4, sems=3)
    send_a, send_b = call(rows_kernel, (at, held, coarse_nu, cols_a, cols_b), [(MESSAGE, 128)] * 2)
    rows_a = swap(send_a, "sx", x_a)
    rows_b = swap(send_b, "sx", x_b)
    blocks = (at, held, coarse_nu, cols_a, cols_b, rows_a, rows_b)
    field = (3, 2, 64, 128)
    state, moved, extra, coef = call(
        low_kernel, blocks + (chain_push,),
        [(6, CROWS, 128), (48, 128), (3 * HALF, 2, EXT, 128), (4, 2, EXT, 128)],
        [field, field, (HALF, 3, 64, 128)],
    )
    state = lax.ppermute(state, "cuts", [(m, CUTS - 1 - m) for m in range(HALF)])
    state_a = swap_high(state, count_x, x_a)
    state_b = swap_high(state, count_x, x_b)
    (out,) = call(
        high_kernel,
        (at, state, state_a, state_b, extra, coef, chain_push, fine, guess, moved),
        [(3, ROWS, COLS)],
        [field, field, (HALF, 3, 64, 128), (48, 128)],
    )
    return out[None]


def solution(mesh):
    in_specs = (P("cuts", None, "sx", "sy"), P("sx", "sy"), P(), P(), P())
    out_specs = P("cuts", None, "sx", "sy")
    return jax.shard_map(
        on_device, mesh=mesh, in_specs=in_specs, out_specs=out_specs, check_vma=False
    )
```

```python
import math

import jax
import jax.numpy as jnp
import numpy as np
from jax import lax
from jax.experimental import pallas as pl
from jax.experimental.pallas import tpu as pltpu
from jax.sharding import PartitionSpec as P

YAWS = 7
CUTS = 16
REACH = 3
F32 = jnp.float32
BF16 = jnp.bfloat16

FINE = (0.3, 0.25, 0.01)
FINE_THRUST = 0.5
FINE_SCALE = (0.25, 0.25, 0.025)
COARSE = (0.15, 0.125, 0.0025)
COARSE_THRUST = 1.0
COARSE_SCALE = (0.125, 0.125, 0.00625)
FINE_TO_COARSE = (0.5, 0.5, 0.25)

ROWS, COLS = 64, 512
CROWS, CCOLS = 16, 128
HALF = CUTS // 2
EXT = 48
NU = 24
ANGLES = [(k - 0.5 * (YAWS - 1)) * (math.pi / 18.0) for k in range(YAWS)]
WEIGHT_X = [float(np.float32(math.cos(t) ** 3)) for t in ANGLES]
WEIGHT_Y = [float(np.float32(math.cos(t) ** 2 * math.sin(t))) for t in ANGLES]

WIDTH = 32
_ORDER = list(range(21)) + [NU, 21, 22, 23]
GROUPS = [_ORDER[_i : _i + 4] for _i in range(0, len(_ORDER), 4)]
STRIPS = 16 * len(GROUPS)
ROW_STRIPS = 16 * 6
PARTS = [(q, 16) for q in range(0, 9)] + [(q, 8) for q in range(9, 21)] + [(NU, 16)]
PART_AT = {}
_at = 0
for _q, _rows in PARTS:
    PART_AT[_q] = (_at, _rows)
    _at += _rows
STRIP_AT = _at
MESSAGE = STRIP_AT + 2 * ROW_STRIPS


def lanes(shape):
    return lax.broadcasted_iota(jnp.int32, shape, len(shape) - 1)


def sublanes(shape):
    return lax.broadcasted_iota(jnp.int32, shape, len(shape) - 2)


def rolled(x, by):
    return pltpu.roll(x, by % 128, 1) if by % 128 else x


def split3(x):
    high = x.astype(BF16)
    rest = x - high.astype(F32)
    middle = rest.astype(BF16)
    return high, middle, (rest - middle.astype(F32)).astype(BF16)


def exact_dot(x, y, dims=(((1,), (0,)), ((), ()))):
    y = y.astype(BF16)
    a, b, c = [lax.dot_general(part, y, dims, preferred_element_type=F32) for part in split3(x)]
    return a + (b + c)


def dot_exact(y, x):
    y = y.astype(BF16)
    a, b, c = [jnp.dot(y, part, preferred_element_type=F32) for part in split3(x)]
    return a + (b + c)


def advance(src, dst, coef, push, shift, row, count, tiles, wanted, terms, side_mask, post=None):
    _, lift, gain = terms
    lane = lanes((count, 128))
    low, high = lane == 0, lane == 127
    here, east, west = pl.ds(row, count), pl.ds(row + 1, count), pl.ds(row - 1, count)
    there = pl.ds(row - shift, count)
    mid = [[src[f, c, here, :] for c in range(tiles)] for f in range(3)]
    up = [[pltpu.roll(mid[f][c], 127, 1) for c in range(tiles)] for f in range(3)]
    down = [[pltpu.roll(mid[f][c], 1, 1) for c in range(tiles)] for f in range(3)]
    for c in wanted:
        after, before = (c + 1) % tiles, (c - 1) % tiles
        u, v, p = mid[0][c], mid[1][c], mid[2][c]
        un, vn, pn = [jnp.where(high, up[f][after], up[f][c]) for f in range(3)]
        us, vs, ps = [jnp.where(low, down[f][before], down[f][c]) for f in range(3)]
        ue, ve, pe = [src[f, c, east, :] for f in range(3)]
        uw, vw, pw = [src[f, c, west, :] for f in range(3)]
        nu, nu_carry, keep, keep_p = [coef[k, c, there, :] for k in range(4)]
        to_east, to_west = nu - u, nu_carry + u
        lifted = u + lift
        size = jnp.abs(lifted)
        drag = lifted * size / (size + lift)
        new_u = ue * to_east + uw * to_west + nu * (un + us) + keep * u - (pe - pw) - push(0, c, there) * drag
        new_v = ve * to_east + vw * to_west + nu * (vn + vs) + keep * v - (pn - ps) - push(1, c, there) * drag
        new_p = nu * ((pe + pw) + (pn + ps)) + keep_p * p - gain * ((ue - uw) + (vn - vs))
        new = [new_u, new_v, new_p]
        if c == tiles - 1:
            new = [f * side_mask for f in new]
        for f in range(3):
            if post is not None:
                new[f] = post(f, c, here, new[f])
            dst[f, c, here, :] = new[f]


def clear_rows(ref, tiles, before, after, outside):
    for row, factor in ((before, outside[0]), (after, outside[1])):
        for f in range(3):
            for c in range(tiles):
                ref[f, c, pl.ds(row, 1), :] = ref[f, c, pl.ds(row, 1), :] * factor


def edges(at):
    lane = lanes((8, 128))
    outside = [jnp.where(at[1] > 0, 1.0, 0.0), jnp.where(at[1] < at[3] - 1, 1.0, 0.0)]
    side = jnp.where(lane < 64, jnp.where(at[2] < at[4] - 1, 1.0, 0.0), jnp.where(at[2] > 0, 1.0, 0.0))
    return outside, side


def coefficients(coef, c, rows, nu, carry):
    coef[0, c, rows, :] = nu
    coef[1, c, rows, :] = nu + carry
    coef[2, c, rows, :] = (1.0 - carry) - 4.0 * nu
    coef[3, c, rows, :] = 1.0 - 4.0 * nu


def yaw_weights(yaw):
    wx = jnp.zeros(yaw.shape, F32)
    wy = jnp.zeros(yaw.shape, F32)
    for k in range(YAWS):
        hit = yaw == k
        wx = jnp.where(hit, WEIGHT_X[k], wx)
        wy = jnp.where(hit, WEIGHT_Y[k], wy)
    return wx, wy


def fetch(pairs, sems):
    copies = [pltpu.make_async_copy(a, b, sems.at[i]) for i, (a, b) in enumerate(pairs)]
    for copy in copies:
        copy.start()
    for copy in copies:
        copy.wait()


def open_kernel(at, start, visc, send_a, send_b, own, sems):
    last = pl.multiple_of(56 * (1 - lax.rem(at[1], 2)), 8)
    first = pl.multiple_of(56 * lax.rem(at[1], 2), 8)
    fetch(
        [
            (start.at[:, pl.ds(last, 8), :], send_a.at[0:3]),
            (visc.at[pl.ds(last, 8), :], send_a.at[3]),
            (start.at[:, pl.ds(first, 8), :], send_b.at[0:3]),
            (visc.at[pl.ds(first, 8), :], send_b.at[3]),
        ]
        + [(start.at[:, :, 128 * c : 128 * c + 128], own.at[0:3, c]) for c in range(4)]
        + [(visc.at[:, 128 * c : 128 * c + 128], own.at[3, c]) for c in range(4)],
        sems,
    )


def side_kernel(at, own, got_a, got_b, send_a, send_b):
    even_x = lax.rem(at[1], 2) == 0
    even_y = lax.rem(at[2], 2) == 0
    for r0, count in ((0, 8), (8, 64), (72, 8)):
        lane = lanes((count, 128))
        left = jnp.zeros((count, 128), F32)
        right = jnp.zeros((count, 128), F32)
        for f in range(4):
            if r0 == 8:
                a, b = own[f, 0], own[f, 3]
            else:
                from_a = jnp.logical_xor(even_x, r0 == 0)
                a = jnp.where(from_a, got_a[f, :, 0:128], got_b[f, :, 0:128])
                b = jnp.where(from_a, got_a[f, :, COLS - 128 : COLS], got_b[f, :, COLS - 128 : COLS])
            mine = (lane >= 8 * f) & (lane < 8 * f + 8)
            left = jnp.where(mine, rolled(a, 8 * f), left)
            right = jnp.where(mine, rolled(b, 8 * f + 8), right)
        send_a[r0 : r0 + count, :] = jnp.where(even_y, right, left)
        send_b[r0 : r0 + count, :] = jnp.where(even_y, left, right)


def fine_cols(sy, c, shape):
    i = sublanes(shape)
    return sy * COLS + (128 * c + i if c < 4 else jnp.where(i < 64, COLS + i, i - 128))


def coarse_cols(sy, c, ty):
    i = sublanes((128, 64))
    col = sy * CCOLS + (i if c == 0 else jnp.where(i < 64, CCOLS + i, i - 128))
    hit = jnp.zeros((128, 64), F32)
    for offset in range(4):
        hit = hit + jnp.where(jnp.abs(4 * col + offset - ty) <= REACH, 0.25, 0.0)
    return hit


LAST_DIMS = (((1,), (1,)), ((), ()))


def push_kernel(at, tx_in, ty_in, yaw_in, fine_push, own_push, tx_ref, ty_ref, yaw_ref, sems):
    fetch([(tx_in, tx_ref), (ty_in, ty_ref), (yaw_in, yaw_ref)], sems)
    tx, ty = tx_ref[...], ty_ref[...]
    mine = sublanes((CUTS, 64)) == at[0]
    wx, wy = yaw_weights(jnp.sum(jnp.where(mine, yaw_ref[...], 0), axis=0, keepdims=True))
    row = at[1] * ROWS - 16 + sublanes((96, 64))
    hit = jnp.where(row == tx, FINE_THRUST, 0.0)
    both = jnp.concatenate([hit * wx, hit * wy], axis=0)
    for c in range(5):
        cols = jnp.where(jnp.abs(fine_cols(at[2], c, (128, 64)) - ty) <= REACH, 1.0, 0.0)
        push = exact_dot(both, cols, LAST_DIMS)
        fine_push[0, c] = push[0:96]
        fine_push[1, c] = push[96:192]
    row = at[1] * CROWS - 10 + sublanes((40, 64))
    hit = jnp.where(row == tx // 4, 0.25 * COARSE_THRUST, 0.0)
    both = jnp.concatenate([hit * wx, hit * wy], axis=0)
    for c in range(2):
        push = exact_dot(both, coarse_cols(at[2], c, ty), LAST_DIMS)
        own_push[0, c] = push[0:40]
        own_push[1, c] = push[40:80]


def chain_push_kernel(at, tx_in, ty_in, yaw_in, push, tx_ref, ty_ref, yaw_ref, sems):
    fetch([(tx_in, tx_ref), (ty_in, ty_ref), (yaw_in, yaw_ref)], sems)
    tx, ty = tx_ref[...], ty_ref[...]
    row = at[1] * CROWS - 16 + sublanes((EXT, 64))
    hit = jnp.where(row == tx // 4, 0.25 * COARSE_THRUST, 0.0)
    wx, wy = yaw_weights(yaw_ref[pl.ds(pl.multiple_of(at[0] // HALF * HALF, HALF), HALF), :])
    cols = [coarse_cols(at[2], c, ty) for c in range(2)]
    for k in range(HALF):
        both = jnp.concatenate([hit * wx[k : k + 1, :], hit * wy[k : k + 1, :]], axis=0)
        for c in range(2):
            value = exact_dot(both, cols[c], LAST_DIMS)
            push[k, 0, c] = value[0:EXT]
            push[k, 1, c] = value[EXT : 2 * EXT]


def fine_kernel(at, own, rows_a, rows_b, cols_a, cols_b, push, own_push, fine, guess, sent, coarse_nu,
                one, two, coef, rough, rough_two, rough_coef):
    even_x = lax.rem(at[1], 2) == 0
    even_y = lax.rem(at[2], 2) == 0
    outside, side_mask = edges(at)
    after_all = jnp.where(even_y, cols_a[...], cols_b[...])
    before_all = jnp.where(even_y, cols_b[...], cols_a[...])
    lane = lanes((80, 128))
    for f in range(4):
        for c in range(5):
            if c < 4:
                cut = slice(128 * c, 128 * c + 128)
                a, b = rows_a[f, :, cut], rows_b[f, :, cut]
                pieces = [(8, 8, jnp.where(even_x, b, a)), (16, 64, own[f, c]), (80, 8, jnp.where(even_x, a, b))]
            else:
                after, before = rolled(after_all, -8 * f), rolled(before_all, 120 - 8 * f)
                pieces = [(8, 80, jnp.where(lane < 8, after, jnp.where(lane >= 120, before, 0.0)))]
            for r, count, value in pieces:
                if f < 3:
                    one[f, c, r : r + count, :] = value * FINE_SCALE[f]
                else:
                    coefficients(coef, c, pl.ds(r, count), value, FINE[0])

    i, j = sublanes((COLS, 128)), lanes((COLS, 128))
    gather = jnp.where(i // 4 == j, 0.0625, 0.0)
    i, j = sublanes((128, 128)), lanes((128, 128))
    gather_side = jnp.where(((i < 8) & (i // 4 == j)) | ((i >= 120) & ((i - 120) // 4 == j - 126)), 0.0625, 0.0)

    def row_sum(ref, first, count):
        parts = [ref[pl.ds(first + k, count, stride=4), :] for k in range(4)]
        return (parts[0] + parts[1]) + (parts[2] + parts[3])

    def pick(f, c):
        return one.at[f, c] if f < 3 else coef.at[0, c]

    body = [jnp.concatenate([row_sum(pick(f, c), 0, 24) for c in range(4)], axis=1) for f in range(4)]
    side = [row_sum(pick(f, 4), 0, 24) for f in range(4)]
    body = exact_dot(jnp.concatenate(body, axis=0), gather)
    side = exact_dot(jnp.concatenate(side, axis=0), gather_side)
    rough[...] = jnp.zeros(rough.shape, F32)
    rough_two[...] = jnp.zeros(rough_two.shape, F32)
    rough_coef[...] = jnp.zeros(rough_coef.shape, F32)
    for c, value in enumerate((body, side)):
        for f in range(3):
            rough[f, c, 6:30, :] = value[24 * f : 24 * f + 24, :] * FINE_TO_COARSE[f]
        coefficients(rough_coef, c, pl.ds(6, 24), value[72:96, :] * 0.5, COARSE[0])
    coarse_nu[...] = rough_coef[0, 0, 10:26, :]

    def coarse_push(d, c, r):
        return own_push[d, c, r, :]

    for k in range(3):
        advance(rough, rough_two, rough_coef, coarse_push, 0, 9 + 8 * k, 8, 2, (0, 1), COARSE, side_mask)
    clear_rows(rough_two, 2, 9, 26, outside)
    for k in range(2):
        advance(rough_two, rough, rough_coef, coarse_push, 0, 10 + 8 * k, 8, 2, (0,), COARSE, side_mask)
    for f in range(3):
        guess[16 * f : 16 * f + 16, :] = rough[f, 0, 10:26, :]

    def fine_push(d, c, r):
        return push[d, c, r, :]

    for src, dst, first, count, wanted in (
        (one, two, 12, 9, range(5)),
        (two, one, 12, 9, range(5)),
        (one, two, 12, 9, range(5)),
        (two, one, 16, 8, range(4)),
    ):
        for k in range(count):
            advance(src, dst, coef, fine_push, 0, first + 8 * k, 8, 5, wanted, FINE, side_mask)
        if count == 9:
            clear_rows(dst, 5, 15, 80, outside)
    for f in range(3):
        for c in range(4):
            fine[f, :, 128 * c : 128 * c + 128] = one[f, c, 16:80, :] * (1.0 / FINE_SCALE[f])
    ends = [jnp.concatenate([row_sum(one.at[f, c], 16, 16) for c in range(4)], axis=1) for f in range(3)]
    ends = exact_dot(jnp.concatenate(ends, axis=0), gather)
    first_slice = at[0] == 0
    for f in range(3):
        cut = slice(16 * f, 16 * f + 16)
        defect = ends[cut] * FINE_TO_COARSE[f] - jnp.where(first_slice, 0.0, guess[cut, :])
        for m in range(HALF):
            sent[m, cut, :] = defect


def plane_of(held, nu, q):
    return nu[...] if q == NU else held[q // 3, 16 * (q % 3) : 16 * (q % 3) + 16, :]


def cols_kernel(at, held, nu, send_a, send_b):
    even_y = lax.rem(at[2], 2) == 0
    lane = lanes((16, 128))
    for g, members in enumerate(GROUPS):
        left = jnp.zeros((16, 128), F32)
        right = jnp.zeros((16, 128), F32)
        for slot, q in enumerate(members):
            offset = slot * WIDTH
            value = plane_of(held, nu, q)
            mine = (lane >= offset) & (lane < offset + WIDTH)
            left = jnp.where(mine, rolled(value, offset), left)
            right = jnp.where(mine, rolled(value, offset + WIDTH), right)
        send_a[16 * g : 16 * g + 16, :] = jnp.where(even_y, right, left)
        send_b[16 * g : 16 * g + 16, :] = jnp.where(even_y, left, right)


def rows_kernel(at, held, nu, cols_a, cols_b, send_a, send_b):
    even = lax.rem(at[1], 2) == 0
    for q, rows in PARTS:
        place, _ = PART_AT[q]
        value = plane_of(held, nu, q)
        if rows == 16:
            send_a[place : place + 16, :] = value
            send_b[place : place + 16, :] = value
        else:
            send_a[place : place + 8, :] = jnp.where(even, value[8:16], value[0:8])
            send_b[place : place + 8, :] = jnp.where(even, value[0:8], value[8:16])
    for ref in (send_a, send_b):
        ref[STRIP_AT : STRIP_AT + ROW_STRIPS, :] = cols_a[0:ROW_STRIPS, :]
        ref[STRIP_AT + ROW_STRIPS : MESSAGE, :] = cols_b[0:ROW_STRIPS, :]


def assemble(at, held, nu, cols_a, cols_b, rows_a, rows_b, put):
    even_x = lax.rem(at[1], 2) == 0
    even_y = lax.rem(at[2], 2) == 0
    for q in range(NU + 1):
        put(q, 0, 16, plane_of(held, nu, q))
        if q in PART_AT:
            place, rows = PART_AT[q]
            a, b = rows_a[place : place + rows, :], rows_b[place : place + rows, :]
            put(q, 0, 16 - rows, jnp.where(even_x, b, a))
            put(q, 0, 32, jnp.where(even_x, a, b))
    lane = lanes((16, 128))
    for g, members in enumerate(GROUPS):
        cut = slice(16 * g, 16 * g + 16)
        blocks = [(16, cols_a[cut, :], cols_b[cut, :])]
        if 16 * g < ROW_STRIPS:
            cut_a = slice(STRIP_AT + 16 * g, STRIP_AT + 16 * g + 16)
            cut_b = slice(STRIP_AT + ROW_STRIPS + 16 * g, STRIP_AT + ROW_STRIPS + 16 * g + 16)
            aa, ab, ba, bb = rows_a[cut_a, :], rows_a[cut_b, :], rows_b[cut_a, :], rows_b[cut_b, :]
            blocks.append((0, jnp.where(even_x, ba, aa), jnp.where(even_x, bb, ab)))
            blocks.append((32, jnp.where(even_x, aa, ba), jnp.where(even_x, ab, bb)))
        for first, a, b in blocks:
            after, before = jnp.where(even_y, a, b), jnp.where(even_y, b, a)
            for slot, q in enumerate(members):
                if first == 16 or q in PART_AT:
                    hi, lo = rolled(after, -slot * WIDTH), rolled(before, 128 - WIDTH - slot * WIDTH)
                    put(q, 1, first, jnp.where(lane < WIDTH, hi, jnp.where(lane >= 128 - WIDTH, lo, 0.0)))


def chain(first_k, one, two, coef, push, extra, kept, at):
    outside, side_mask = edges(at)

    for k in range(first_k, HALF):
        def pushed(d, c, r, k=k):
            return push[k, d, c, r, :]

        def keep_and_add(f, c, r, value, k=k):
            if c == 0:
                kept[k, f, r, :] = value
            return value + extra[3 * k + f, c, pl.ds(r.start - 8, r.size), :]

        for half in range(2):
            halo = 2 * (HALF - 1 - k) + 1 - half
            count = 2 + -(-halo // 4)
            first = min(8 + 16 - halo, 8 + EXT - 8 * count)
            src, dst = (one, two) if half == 0 else (two, one)
            post = keep_and_add if half else None
            for i in range(count):
                advance(src, dst, coef, pushed, 8, first + 8 * i, 8, 2, (0, 1), COARSE, side_mask, post=post)
            if halo:
                clear_rows(dst, 2, 8 + 15, 8 + 32, outside)


def low_kernel(at, held, nu, cols_a, cols_b, rows_a, rows_b, push, state, moved, extra, coef, one, two, kept):
    def put(q, c, row, value):
        rows = pl.ds(row, value.shape[0])
        if q == NU:
            coefficients(coef, c, rows, value, COARSE[0])
        else:
            extra[q, c, rows, :] = value

    assemble(at, held, nu, cols_a, cols_b, rows_a, rows_b, put)

    @pl.when(at[0] < HALF)
    def _():
        for f in range(3):
            for c in range(2):
                one[f, c, 8:56, :] = extra[f, c]
        chain(1, one, two, coef, push, extra, kept, at)
        lane = lanes((CROWS, 128))
        sides = jnp.zeros((CROWS, 128), F32)
        for f in range(3):
            state[16 * f : 16 * f + 16, :] = one[f, 0, 24:40, :]
            sides = jnp.where(lane // 32 == f, rolled(one[f, 1, 24:40, :], 16 + 32 * f), sides)
        state[48:64, :] = sides
        for f in range(3):
            moved[16 * f : 16 * f + 16, :] = kept[jnp.maximum(at[0], 1), f, 24:40, :]


def high_kernel(at, state, state_a, state_b, extra, coef, push, fine, guess, moved_low, out, one, two, kept, moved):
    even_x = lax.rem(at[1], 2) == 0

    @pl.when(at[0] < HALF)
    def _():
        moved[...] = moved_low[...]

    @pl.when(at[0] >= HALF)
    def _():
        lane = lanes((CROWS, 128))
        a, b = state_a[...], state_b[...]
        for row, block in ((8, jnp.where(even_x, b, a)), (24, state[...]), (40, jnp.where(even_x, a, b))):
            for f in range(3):
                one[f, 0, row : row + 16, :] = block[16 * f : 16 * f + 16]
                side = rolled(block[48:64], -(16 + 32 * f))
                one[f, 1, row : row + 16, :] = jnp.where((lane < 16) | (lane >= 112), side, 0.0)
        chain(0, one, two, coef, push, extra, kept, at)
        for f in range(3):
            moved[16 * f : 16 * f + 16, :] = kept[at[0] - HALF, f, 24:40, :]

    parts = []
    for f in range(3):
        cut = slice(16 * f, 16 * f + 16)
        parts.append(jnp.where(at[0] == 0, 0.0, (moved[cut, :] - guess[cut, :]) * (1.0 / COARSE_SCALE[f])))
    change = jnp.concatenate(parts, axis=0)
    i, j = sublanes((3 * ROWS, 48)), lanes((3 * ROWS, 48))
    repeat_rows = jnp.where(i // 4 == j, 1.0, 0.0)
    i, j = sublanes((128, COLS)), lanes((128, COLS))
    repeat_cols = jnp.where(i == j // 4, 1.0, 0.0)
    change = exact_dot(dot_exact(repeat_rows, change), repeat_cols)
    for f in range(3):
        out[f] = fine[f] + change[ROWS * f : ROWS * f + ROWS, :]


SMEM = pl.BlockSpec(memory_space=pltpu.SMEM)
VMEM = pl.BlockSpec(memory_space=pltpu.VMEM)
HBM = pl.BlockSpec(memory_space=pltpu.HBM)


def call(kernel, args, outs, scratch=(), far=0, sems=0):
    shapes = [jax.ShapeDtypeStruct(s, F32) for s in outs]
    near = len(args) - 1 - far
    memory = [s if not isinstance(s, tuple) else pltpu.VMEM(s, F32) for s in scratch]
    if sems:
        memory.append(pltpu.SemaphoreType.DMA((sems,)))
    return pl.pallas_call(
        kernel,
        out_shape=shapes,
        in_specs=[SMEM] + [VMEM] * near + [HBM] * far,
        out_specs=[VMEM] * len(shapes),
        scratch_shapes=memory,
        compiler_params=pltpu.CompilerParams(vmem_limit_bytes=48 * 1024 * 1024),
    )(*args)


def swap(x, axis, pairs):
    return lax.ppermute(x, axis, [(a, b) for a, b in pairs] + [(b, a) for a, b in pairs])


def swap_high(x, count, pairs):
    both = [(a, b) for a, b in pairs] + [(b, a) for a, b in pairs]
    return lax.ppermute(x, ("cuts", "sx"), [(n * count + a, n * count + b) for n in range(HALF, CUTS) for a, b in both])


def on_device(starts, viscosity, turbine_x, turbine_y, yaw_index):
    count_x, count_y = lax.axis_size("sx"), lax.axis_size("sy")
    at = jnp.stack([
        lax.axis_index("cuts"), lax.axis_index("sx"), lax.axis_index("sy"),
        jnp.int32(count_x), jnp.int32(count_y),
    ]).astype(jnp.int32)
    start = starts[0]
    x_a = [(i, i + 1) for i in range(0, count_x - 1, 2)]
    x_b = [(i, i + 1) for i in range(1, count_x - 1, 2)]
    y_a = [(i, i + 1) for i in range(0, count_y - 1, 2)]
    y_b = [(i, i + 1) for i in range(1, count_y - 1, 2)]
    turbines = (turbine_x[None, :], turbine_y[None, :], yaw_index)
    turbine_scratch = [pltpu.VMEM((1, 64), jnp.int32), pltpu.VMEM((1, 64), jnp.int32), pltpu.VMEM((CUTS, 64), jnp.int32)]

    edge = (4, 8, COLS)
    send_a, send_b, own = call(
        open_kernel, (at, start, viscosity), [edge, edge, (4, 4, ROWS, 128)], far=2, sems=12)
    rows_a = swap(send_a, "sx", x_a)
    rows_b = swap(send_b, "sx", x_b)
    send_a, send_b = call(side_kernel, (at, own, rows_a, rows_b), [(80, 128)] * 2)
    cols_a = swap(send_a, "sy", y_a)
    cols_b = swap(send_b, "sy", y_b)
    push, own_push = call(
        push_kernel, (at,) + turbines, [(2, 5, 96, 128), (2, 2, 40, 128)], turbine_scratch, far=3, sems=3)
    fine, guess, sent, coarse_nu = call(
        fine_kernel,
        (at, own, rows_a, rows_b, cols_a, cols_b, push, own_push),
        [(3, ROWS, COLS), (48, 128), (HALF, 48, 128), (CROWS, 128)],
        [(3, 5, 96, 128), (3, 5, 96, 128), (4, 5, 96, 128), (3, 2, 40, 128), (3, 2, 40, 128), (4, 2, 40, 128)],
    )
    halves = [list(range(HALF)), list(range(HALF, CUTS))]
    held = lax.all_to_all(sent, "cuts", 0, 0, axis_index_groups=halves)
    send_a, send_b = call(cols_kernel, (at, held, coarse_nu), [(STRIPS, 128)] * 2)
    cols_a = swap(send_a, "sy", y_a)
    cols_b = swap(send_b, "sy", y_b)
    (chain_push,) = call(
        chain_push_kernel, (at,) + turbines, [(HALF, 2, 2, EXT, 128)], turbine_scratch, far=3, sems=3)
    send_a, send_b = call(rows_kernel, (at, held, coarse_nu, cols_a, cols_b), [(MESSAGE, 128)] * 2)
    rows_a = swap(send_a, "sx", x_a)
    rows_b = swap(send_b, "sx", x_b)
    blocks = (at, held, coarse_nu, cols_a, cols_b, rows_a, rows_b)
    field = (3, 2, 64, 128)
    state, moved, extra, coef = call(
        low_kernel, blocks + (chain_push,),
        [(64, 128), (48, 128), (3 * HALF, 2, EXT, 128), (4, 2, EXT, 128)],
        [field, field, (HALF, 3, 64, 128)],
    )
    state = lax.ppermute(state, "cuts", [(m, (m + 4 if m >= 4 else m + 12)) for m in range(HALF)])
    state_a = swap_high(state, count_x, x_a)
    state_b = swap_high(state, count_x, x_b)
    (out,) = call(
        high_kernel,
        (at, state, state_a, state_b, extra, coef, chain_push, fine, guess, moved),
        [(3, ROWS, COLS)],
        [field, field, (HALF, 3, 64, 128), (48, 128)],
    )
    return out[None]


def solution(mesh):
    in_specs = (P("cuts", None, "sx", "sy"), P("sx", "sy"), P(), P(), P())
    out_specs = P("cuts", None, "sx", "sy")
    return jax.shard_map(
        on_device, mesh=mesh, in_specs=in_specs, out_specs=out_specs, check_vma=False
    )
```

```python
import math

import jax
import jax.numpy as jnp
import numpy as np
from jax import lax
from jax.experimental import pallas as pl
from jax.experimental.pallas import tpu as pltpu
from jax.sharding import PartitionSpec as P

YAWS = 7
CUTS = 16
REACH = 3
F32 = jnp.float32
BF16 = jnp.bfloat16

FINE = (0.3, 0.25, 0.01)
FINE_THRUST = 0.5
FINE_SCALE = (0.25, 0.25, 0.025)
COARSE = (0.15, 0.125, 0.0025)
COARSE_THRUST = 1.0
COARSE_SCALE = (0.125, 0.125, 0.00625)
FINE_TO_COARSE = (0.5, 0.5, 0.25)

ROWS, COLS = 64, 512
CROWS, CCOLS = 16, 128
HALF = CUTS // 2
EXT = 48
NU = 24
ANGLES = [(k - 0.5 * (YAWS - 1)) * (math.pi / 18.0) for k in range(YAWS)]
WEIGHT_X = [float(np.float32(math.cos(t) ** 3)) for t in ANGLES]
WEIGHT_Y = [float(np.float32(math.cos(t) ** 2 * math.sin(t))) for t in ANGLES]

WIDTH = 32
_ORDER = list(range(21)) + [NU, 21, 22, 23]
GROUPS = [_ORDER[_i : _i + 4] for _i in range(0, len(_ORDER), 4)]
STRIPS = 16 * len(GROUPS)
ROW_STRIPS = 16 * 6
PARTS = [(q, 16) for q in range(0, 9)] + [(q, 8) for q in range(9, 21)] + [(NU, 16)]
PART_AT = {}
_at = 0
for _q, _rows in PARTS:
    PART_AT[_q] = (_at, _rows)
    _at += _rows
STRIP_AT = _at
MESSAGE = STRIP_AT + 2 * ROW_STRIPS


def lanes(shape):
    return lax.broadcasted_iota(jnp.int32, shape, len(shape) - 1)


def sublanes(shape):
    return lax.broadcasted_iota(jnp.int32, shape, len(shape) - 2)


def rolled(x, by):
    return pltpu.roll(x, by % 128, 1) if by % 128 else x


def split3(x):
    high = x.astype(BF16)
    rest = x - high.astype(F32)
    middle = rest.astype(BF16)
    return high, middle, (rest - middle.astype(F32)).astype(BF16)


def exact_dot(x, y, dims=(((1,), (0,)), ((), ()))):
    y = y.astype(BF16)
    a, b, c = [lax.dot_general(part, y, dims, preferred_element_type=F32) for part in split3(x)]
    return a + (b + c)


def dot_exact(y, x):
    y = y.astype(BF16)
    a, b, c = [jnp.dot(y, part, preferred_element_type=F32) for part in split3(x)]
    return a + (b + c)


def advance(src, dst, coef, push, shift, row, count, tiles, wanted, terms, side_mask, post=None):
    _, lift, gain = terms
    lane = lanes((count, 128))
    low, high = lane == 0, lane == 127
    here, east, west = pl.ds(row, count), pl.ds(row + 1, count), pl.ds(row - 1, count)
    there = pl.ds(row - shift, count)
    mid = [[src[f, c, here, :] for c in range(tiles)] for f in range(3)]
    up = [[pltpu.roll(mid[f][c], 127, 1) for c in range(tiles)] for f in range(3)]
    down = [[pltpu.roll(mid[f][c], 1, 1) for c in range(tiles)] for f in range(3)]
    for c in wanted:
        after, before = (c + 1) % tiles, (c - 1) % tiles
        u, v, p = mid[0][c], mid[1][c], mid[2][c]
        un, vn, pn = [jnp.where(high, up[f][after], up[f][c]) for f in range(3)]
        us, vs, ps = [jnp.where(low, down[f][before], down[f][c]) for f in range(3)]
        ue, ve, pe = [src[f, c, east, :] for f in range(3)]
        uw, vw, pw = [src[f, c, west, :] for f in range(3)]
        nu, nu_carry, keep, keep_p = [coef[k, c, there, :] for k in range(4)]
        to_east, to_west = nu - u, nu_carry + u
        lifted = u + lift
        size = jnp.abs(lifted)
        drag = lifted * size / (size + lift)
        new_u = ue * to_east + uw * to_west + nu * (un + us) + keep * u - (pe - pw) - push(0, c, there) * drag
        new_v = ve * to_east + vw * to_west + nu * (vn + vs) + keep * v - (pn - ps) - push(1, c, there) * drag
        new_p = nu * ((pe + pw) + (pn + ps)) + keep_p * p - gain * ((ue - uw) + (vn - vs))
        new = [new_u, new_v, new_p]
        if c == tiles - 1:
            new = [f * side_mask for f in new]
        for f in range(3):
            if post is not None:
                new[f] = post(f, c, here, new[f])
            dst[f, c, here, :] = new[f]


def clear_rows(ref, tiles, before, after, outside):
    for row, factor in ((before, outside[0]), (after, outside[1])):
        for f in range(3):
            for c in range(tiles):
                ref[f, c, pl.ds(row, 1), :] = ref[f, c, pl.ds(row, 1), :] * factor


def edges(at):
    lane = lanes((8, 128))
    outside = [jnp.where(at[1] > 0, 1.0, 0.0), jnp.where(at[1] < at[3] - 1, 1.0, 0.0)]
    side = jnp.where(lane < 64, jnp.where(at[2] < at[4] - 1, 1.0, 0.0), jnp.where(at[2] > 0, 1.0, 0.0))
    return outside, side


def coefficients(coef, c, rows, nu, carry):
    coef[0, c, rows, :] = nu
    coef[1, c, rows, :] = nu + carry
    coef[2, c, rows, :] = (1.0 - carry) - 4.0 * nu
    coef[3, c, rows, :] = 1.0 - 4.0 * nu


def yaw_weights(yaw):
    wx = jnp.zeros(yaw.shape, F32)
    wy = jnp.zeros(yaw.shape, F32)
    for k in range(YAWS):
        hit = yaw == k
        wx = jnp.where(hit, WEIGHT_X[k], wx)
        wy = jnp.where(hit, WEIGHT_Y[k], wy)
    return wx, wy


def fetch(pairs, sems):
    copies = [pltpu.make_async_copy(a, b, sems.at[i]) for i, (a, b) in enumerate(pairs)]
    for copy in copies:
        copy.start()
    for copy in copies:
        copy.wait()


def load_kernel(at, start, visc, own, sems):
    fetch(
        [(start.at[:, :, 128 * c : 128 * c + 128], own.at[0:3, c]) for c in range(4)]
        + [(visc.at[:, 128 * c : 128 * c + 128], own.at[3, c]) for c in range(4)],
        sems,
    )


def edge_rows(start, visc, first):
    return jnp.concatenate([
        lax.dynamic_slice(start, (0, first, 0), (3, 8, COLS)),
        lax.dynamic_slice(visc, (first, 0), (8, COLS))[None],
    ])


def side_kernel(at, own, got_a, got_b, send_a, send_b):
    even_x = lax.rem(at[1], 2) == 0
    even_y = lax.rem(at[2], 2) == 0
    for r0, count in ((0, 8), (8, 64), (72, 8)):
        lane = lanes((count, 128))
        left = jnp.zeros((count, 128), F32)
        right = jnp.zeros((count, 128), F32)
        for f in range(4):
            if r0 == 8:
                a, b = own[f, 0], own[f, 3]
            else:
                from_a = jnp.logical_xor(even_x, r0 == 0)
                a = jnp.where(from_a, got_a[f, :, 0:128], got_b[f, :, 0:128])
                b = jnp.where(from_a, got_a[f, :, COLS - 128 : COLS], got_b[f, :, COLS - 128 : COLS])
            mine = (lane >= 8 * f) & (lane < 8 * f + 8)
            left = jnp.where(mine, rolled(a, 8 * f), left)
            right = jnp.where(mine, rolled(b, 8 * f + 8), right)
        send_a[r0 : r0 + count, :] = jnp.where(even_y, right, left)
        send_b[r0 : r0 + count, :] = jnp.where(even_y, left, right)


def fine_cols(sy, c, shape):
    i = sublanes(shape)
    return sy * COLS + (128 * c + i if c < 4 else jnp.where(i < 64, COLS + i, i - 128))


def coarse_cols(sy, c, ty):
    i = sublanes((128, 64))
    col = sy * CCOLS + (i if c == 0 else jnp.where(i < 64, CCOLS + i, i - 128))
    hit = jnp.zeros((128, 64), F32)
    for offset in range(4):
        hit = hit + jnp.where(jnp.abs(4 * col + offset - ty) <= REACH, 0.25, 0.0)
    return hit


LAST_DIMS = (((1,), (1,)), ((), ()))


def push_kernel(at, tx_in, ty_in, yaw_in, fine_push, own_push, tx_ref, ty_ref, yaw_ref, sems):
    fetch([(tx_in, tx_ref), (ty_in, ty_ref), (yaw_in, yaw_ref)], sems)
    tx, ty = tx_ref[...], ty_ref[...]
    mine = sublanes((CUTS, 64)) == at[0]
    wx, wy = yaw_weights(jnp.sum(jnp.where(mine, yaw_ref[...], 0), axis=0, keepdims=True))
    row = at[1] * ROWS - 16 + sublanes((96, 64))
    hit = jnp.where(row == tx, FINE_THRUST, 0.0)
    both = jnp.concatenate([hit * wx, hit * wy], axis=0)
    for c in range(5):
        cols = jnp.where(jnp.abs(fine_cols(at[2], c, (128, 64)) - ty) <= REACH, 1.0, 0.0)
        push = exact_dot(both, cols, LAST_DIMS)
        fine_push[0, c] = push[0:96]
        fine_push[1, c] = push[96:192]
    row = at[1] * CROWS - 10 + sublanes((40, 64))
    hit = jnp.where(row == tx // 4, 0.25 * COARSE_THRUST, 0.0)
    both = jnp.concatenate([hit * wx, hit * wy], axis=0)
    for c in range(2):
        push = exact_dot(both, coarse_cols(at[2], c, ty), LAST_DIMS)
        own_push[0, c] = push[0:40]
        own_push[1, c] = push[40:80]


def chain_push_kernel(at, tx_in, ty_in, yaw_in, push, tx_ref, ty_ref, yaw_ref, sems):
    fetch([(tx_in, tx_ref), (ty_in, ty_ref), (yaw_in, yaw_ref)], sems)
    tx, ty = tx_ref[...], ty_ref[...]
    row = at[1] * CROWS - 16 + sublanes((EXT, 64))
    hit = jnp.where(row == tx // 4, 0.25 * COARSE_THRUST, 0.0)
    wx, wy = yaw_weights(yaw_ref[pl.ds(pl.multiple_of(at[0] // HALF * HALF, HALF), HALF), :])
    cols = [coarse_cols(at[2], c, ty) for c in range(2)]
    for k in range(HALF):
        both = jnp.concatenate([hit * wx[k : k + 1, :], hit * wy[k : k + 1, :]], axis=0)
        for c in range(2):
            value = exact_dot(both, cols[c], LAST_DIMS)
            push[k, 0, c] = value[0:EXT]
            push[k, 1, c] = value[EXT : 2 * EXT]


def fine_kernel(at, own, rows_a, rows_b, cols_a, cols_b, push, own_push, fine, guess, sent, coarse_nu,
                one, two, coef, rough, rough_two, rough_coef):
    even_x = lax.rem(at[1], 2) == 0
    even_y = lax.rem(at[2], 2) == 0
    outside, side_mask = edges(at)
    after_all = jnp.where(even_y, cols_a[...], cols_b[...])
    before_all = jnp.where(even_y, cols_b[...], cols_a[...])
    lane = lanes((80, 128))
    for f in range(4):
        for c in range(5):
            if c < 4:
                cut = slice(128 * c, 128 * c + 128)
                a, b = rows_a[f, :, cut], rows_b[f, :, cut]
                pieces = [(8, 8, jnp.where(even_x, b, a)), (16, 64, own[f, c]), (80, 8, jnp.where(even_x, a, b))]
            else:
                after, before = rolled(after_all, -8 * f), rolled(before_all, 120 - 8 * f)
                pieces = [(8, 80, jnp.where(lane < 8, after, jnp.where(lane >= 120, before, 0.0)))]
            for r, count, value in pieces:
                if f < 3:
                    one[f, c, r : r + count, :] = value * FINE_SCALE[f]
                else:
                    coefficients(coef, c, pl.ds(r, count), value, FINE[0])

    i, j = sublanes((COLS, 128)), lanes((COLS, 128))
    gather = jnp.where(i // 4 == j, 0.0625, 0.0)
    i, j = sublanes((128, 128)), lanes((128, 128))
    gather_side = jnp.where(((i < 8) & (i // 4 == j)) | ((i >= 120) & ((i - 120) // 4 == j - 126)), 0.0625, 0.0)

    def row_sum(ref, first, count):
        parts = [ref[pl.ds(first + k, count, stride=4), :] for k in range(4)]
        return (parts[0] + parts[1]) + (parts[2] + parts[3])

    def pick(f, c):
        return one.at[f, c] if f < 3 else coef.at[0, c]

    body = [jnp.concatenate([row_sum(pick(f, c), 0, 24) for c in range(4)], axis=1) for f in range(4)]
    side = [row_sum(pick(f, 4), 0, 24) for f in range(4)]
    body = exact_dot(jnp.concatenate(body, axis=0), gather)
    side = exact_dot(jnp.concatenate(side, axis=0), gather_side)
    rough[...] = jnp.zeros(rough.shape, F32)
    rough_two[...] = jnp.zeros(rough_two.shape, F32)
    rough_coef[...] = jnp.zeros(rough_coef.shape, F32)
    for c, value in enumerate((body, side)):
        for f in range(3):
            rough[f, c, 6:30, :] = value[24 * f : 24 * f + 24, :] * FINE_TO_COARSE[f]
        coefficients(rough_coef, c, pl.ds(6, 24), value[72:96, :] * 0.5, COARSE[0])
    coarse_nu[...] = rough_coef[0, 0, 10:26, :]

    def coarse_push(d, c, r):
        return own_push[d, c, r, :]

    for k in range(3):
        advance(rough, rough_two, rough_coef, coarse_push, 0, 9 + 8 * k, 8, 2, (0, 1), COARSE, side_mask)
    clear_rows(rough_two, 2, 9, 26, outside)
    for k in range(2):
        advance(rough_two, rough, rough_coef, coarse_push, 0, 10 + 8 * k, 8, 2, (0,), COARSE, side_mask)
    for f in range(3):
        guess[16 * f : 16 * f + 16, :] = rough[f, 0, 10:26, :]

    def fine_push(d, c, r):
        return push[d, c, r, :]

    for src, dst, first, count, wanted in (
        (one, two, 12, 9, range(5)),
        (two, one, 12, 9, range(5)),
        (one, two, 12, 9, range(5)),
        (two, one, 16, 8, range(4)),
    ):
        for k in range(count):
            advance(src, dst, coef, fine_push, 0, first + 8 * k, 8, 5, wanted, FINE, side_mask)
        if count == 9:
            clear_rows(dst, 5, 15, 80, outside)
    for f in range(3):
        for c in range(4):
            fine[f, :, 128 * c : 128 * c + 128] = one[f, c, 16:80, :] * (1.0 / FINE_SCALE[f])
    ends = [jnp.concatenate([row_sum(one.at[f, c], 16, 16) for c in range(4)], axis=1) for f in range(3)]
    ends = exact_dot(jnp.concatenate(ends, axis=0), gather)
    first_slice = at[0] == 0
    for f in range(3):
        cut = slice(16 * f, 16 * f + 16)
        defect = ends[cut] * FINE_TO_COARSE[f] - jnp.where(first_slice, 0.0, guess[cut, :])
        for m in range(HALF):
            sent[m, cut, :] = defect


def plane_of(held, nu, q):
    return nu[...] if q == NU else held[q // 3, 16 * (q % 3) : 16 * (q % 3) + 16, :]


def cols_kernel(at, held, nu, send_a, send_b):
    even_y = lax.rem(at[2], 2) == 0
    lane = lanes((16, 128))
    for g, members in enumerate(GROUPS):
        left = jnp.zeros((16, 128), F32)
        right = jnp.zeros((16, 128), F32)
        for slot, q in enumerate(members):
            offset = slot * WIDTH
            value = plane_of(held, nu, q)
            mine = (lane >= offset) & (lane < offset + WIDTH)
            left = jnp.where(mine, rolled(value, offset), left)
            right = jnp.where(mine, rolled(value, offset + WIDTH), right)
        send_a[16 * g : 16 * g + 16, :] = jnp.where(even_y, right, left)
        send_b[16 * g : 16 * g + 16, :] = jnp.where(even_y, left, right)


def rows_kernel(at, held, nu, cols_a, cols_b, send_a, send_b):
    even = lax.rem(at[1], 2) == 0
    for q, rows in PARTS:
        place, _ = PART_AT[q]
        value = plane_of(held, nu, q)
        if rows == 16:
            send_a[place : place + 16, :] = value
            send_b[place : place + 16, :] = value
        else:
            send_a[place : place + 8, :] = jnp.where(even, value[8:16], value[0:8])
            send_b[place : place + 8, :] = jnp.where(even, value[0:8], value[8:16])
    for ref in (send_a, send_b):
        ref[STRIP_AT : STRIP_AT + ROW_STRIPS, :] = cols_a[0:ROW_STRIPS, :]
        ref[STRIP_AT + ROW_STRIPS : MESSAGE, :] = cols_b[0:ROW_STRIPS, :]


def assemble(at, held, nu, cols_a, cols_b, rows_a, rows_b, put):
    even_x = lax.rem(at[1], 2) == 0
    even_y = lax.rem(at[2], 2) == 0
    for q in range(NU + 1):
        put(q, 0, 16, plane_of(held, nu, q))
        if q in PART_AT:
            place, rows = PART_AT[q]
            a, b = rows_a[place : place + rows, :], rows_b[place : place + rows, :]
            put(q, 0, 16 - rows, jnp.where(even_x, b, a))
            put(q, 0, 32, jnp.where(even_x, a, b))
    lane = lanes((16, 128))
    for g, members in enumerate(GROUPS):
        cut = slice(16 * g, 16 * g + 16)
        blocks = [(16, cols_a[cut, :], cols_b[cut, :])]
        if 16 * g < ROW_STRIPS:
            cut_a = slice(STRIP_AT + 16 * g, STRIP_AT + 16 * g + 16)
            cut_b = slice(STRIP_AT + ROW_STRIPS + 16 * g, STRIP_AT + ROW_STRIPS + 16 * g + 16)
            aa, ab, ba, bb = rows_a[cut_a, :], rows_a[cut_b, :], rows_b[cut_a, :], rows_b[cut_b, :]
            blocks.append((0, jnp.where(even_x, ba, aa), jnp.where(even_x, bb, ab)))
            blocks.append((32, jnp.where(even_x, aa, ba), jnp.where(even_x, ab, bb)))
        for first, a, b in blocks:
            after, before = jnp.where(even_y, a, b), jnp.where(even_y, b, a)
            for slot, q in enumerate(members):
                if first == 16 or q in PART_AT:
                    hi, lo = rolled(after, -slot * WIDTH), rolled(before, 128 - WIDTH - slot * WIDTH)
                    put(q, 1, first, jnp.where(lane < WIDTH, hi, jnp.where(lane >= 128 - WIDTH, lo, 0.0)))


def chain(first_k, one, two, coef, push, extra, kept, at):
    outside, side_mask = edges(at)

    for k in range(first_k, HALF):
        def pushed(d, c, r, k=k):
            return push[k, d, c, r, :]

        def keep_and_add(f, c, r, value, k=k):
            if c == 0:
                kept[k, f, r, :] = value
            return value + extra[3 * k + f, c, pl.ds(r.start - 8, r.size), :]

        for half in range(2):
            halo = 2 * (HALF - 1 - k) + 1 - half
            count = 2 + -(-halo // 4)
            first = min(8 + 16 - halo, 8 + EXT - 8 * count)
            src, dst = (one, two) if half == 0 else (two, one)
            post = keep_and_add if half else None
            for i in range(count):
                advance(src, dst, coef, pushed, 8, first + 8 * i, 8, 2, (0, 1), COARSE, side_mask, post=post)
            if halo:
                clear_rows(dst, 2, 8 + 15, 8 + 32, outside)


def low_kernel(at, held, nu, cols_a, cols_b, rows_a, rows_b, push, state, moved, extra, coef, one, two, kept):
    def put(q, c, row, value):
        rows = pl.ds(row, value.shape[0])
        if q == NU:
            coefficients(coef, c, rows, value, COARSE[0])
        else:
            extra[q, c, rows, :] = value

    assemble(at, held, nu, cols_a, cols_b, rows_a, rows_b, put)

    @pl.when(at[0] < HALF)
    def _():
        for f in range(3):
            for c in range(2):
                one[f, c, 8:56, :] = extra[f, c]
        chain(1, one, two, coef, push, extra, kept, at)
        lane = lanes((CROWS, 128))
        sides = jnp.zeros((CROWS, 128), F32)
        for f in range(3):
            state[16 * f : 16 * f + 16, :] = one[f, 0, 24:40, :]
            sides = jnp.where(lane // 32 == f, rolled(one[f, 1, 24:40, :], 16 + 32 * f), sides)
        state[48:64, :] = sides
        for f in range(3):
            moved[16 * f : 16 * f + 16, :] = kept[jnp.maximum(at[0], 1), f, 24:40, :]


def high_kernel(at, state, state_a, state_b, extra, coef, push, fine, guess, moved_low, out, one, two, kept, moved):
    even_x = lax.rem(at[1], 2) == 0

    @pl.when(at[0] < HALF)
    def _():
        moved[...] = moved_low[...]

    @pl.when(at[0] >= HALF)
    def _():
        lane = lanes((CROWS, 128))
        a, b = state_a[...], state_b[...]
        for row, block in ((8, jnp.where(even_x, b, a)), (24, state[...]), (40, jnp.where(even_x, a, b))):
            for f in range(3):
                one[f, 0, row : row + 16, :] = block[16 * f : 16 * f + 16]
                side = rolled(block[48:64], -(16 + 32 * f))
                one[f, 1, row : row + 16, :] = jnp.where((lane < 16) | (lane >= 112), side, 0.0)
        chain(0, one, two, coef, push, extra, kept, at)
        for f in range(3):
            moved[16 * f : 16 * f + 16, :] = kept[at[0] - HALF, f, 24:40, :]

    parts = []
    for f in range(3):
        cut = slice(16 * f, 16 * f + 16)
        parts.append(jnp.where(at[0] == 0, 0.0, (moved[cut, :] - guess[cut, :]) * (1.0 / COARSE_SCALE[f])))
    change = jnp.concatenate(parts, axis=0)
    i, j = sublanes((3 * ROWS, 48)), lanes((3 * ROWS, 48))
    repeat_rows = jnp.where(i // 4 == j, 1.0, 0.0)
    i, j = sublanes((128, COLS)), lanes((128, COLS))
    repeat_cols = jnp.where(i == j // 4, 1.0, 0.0)
    change = exact_dot(dot_exact(repeat_rows, change), repeat_cols)
    for f in range(3):
        out[f] = fine[f] + change[ROWS * f : ROWS * f + ROWS, :]


SMEM = pl.BlockSpec(memory_space=pltpu.SMEM)
VMEM = pl.BlockSpec(memory_space=pltpu.VMEM)
HBM = pl.BlockSpec(memory_space=pltpu.HBM)


def call(kernel, args, outs, scratch=(), far=0, sems=0):
    shapes = [jax.ShapeDtypeStruct(s, F32) for s in outs]
    near = len(args) - 1 - far
    memory = [s if not isinstance(s, tuple) else pltpu.VMEM(s, F32) for s in scratch]
    if sems:
        memory.append(pltpu.SemaphoreType.DMA((sems,)))
    return pl.pallas_call(
        kernel,
        out_shape=shapes,
        in_specs=[SMEM] + [VMEM] * near + [HBM] * far,
        out_specs=[VMEM] * len(shapes),
        scratch_shapes=memory,
        compiler_params=pltpu.CompilerParams(vmem_limit_bytes=48 * 1024 * 1024),
    )(*args)


def swap(x, axis, pairs):
    return lax.ppermute(x, axis, [(a, b) for a, b in pairs] + [(b, a) for a, b in pairs])


def swap_high(x, count, pairs):
    both = [(a, b) for a, b in pairs] + [(b, a) for a, b in pairs]
    return lax.ppermute(x, ("cuts", "sx"), [(n * count + a, n * count + b) for n in range(HALF, CUTS) for a, b in both])


def on_device(starts, viscosity, turbine_x, turbine_y, yaw_index):
    count_x, count_y = lax.axis_size("sx"), lax.axis_size("sy")
    at = jnp.stack([
        lax.axis_index("cuts"), lax.axis_index("sx"), lax.axis_index("sy"),
        jnp.int32(count_x), jnp.int32(count_y),
    ]).astype(jnp.int32)
    start = starts[0]
    x_a = [(i, i + 1) for i in range(0, count_x - 1, 2)]
    x_b = [(i, i + 1) for i in range(1, count_x - 1, 2)]
    y_a = [(i, i + 1) for i in range(0, count_y - 1, 2)]
    y_b = [(i, i + 1) for i in range(1, count_y - 1, 2)]
    turbines = (turbine_x[None, :], turbine_y[None, :], yaw_index)
    turbine_scratch = [pltpu.VMEM((1, 64), jnp.int32), pltpu.VMEM((1, 64), jnp.int32), pltpu.VMEM((CUTS, 64), jnp.int32)]

    odd = at[1] % 2
    rows_b = swap(edge_rows(start, viscosity, 56 * odd), "sx", x_b)
    rows_a = swap(edge_rows(start, viscosity, 56 * (1 - odd)), "sx", x_a)
    (own,) = call(load_kernel, (at, start, viscosity), [(4, 4, ROWS, 128)], far=2, sems=8)
    send_a, send_b = call(side_kernel, (at, own, rows_a, rows_b), [(80, 128)] * 2)
    cols_a = swap(send_a, "sy", y_a)
    cols_b = swap(send_b, "sy", y_b)
    push, own_push = call(
        push_kernel, (at,) + turbines, [(2, 5, 96, 128), (2, 2, 40, 128)], turbine_scratch, far=3, sems=3)
    fine, guess, sent, coarse_nu = call(
        fine_kernel,
        (at, own, rows_a, rows_b, cols_a, cols_b, push, own_push),
        [(3, ROWS, COLS), (48, 128), (HALF, 48, 128), (CROWS, 128)],
        [(3, 5, 96, 128), (3, 5, 96, 128), (4, 5, 96, 128), (3, 2, 40, 128), (3, 2, 40, 128), (4, 2, 40, 128)],
    )
    halves = [list(range(HALF)), list(range(HALF, CUTS))]
    held = lax.all_to_all(sent, "cuts", 0, 0, axis_index_groups=halves)
    send_a, send_b = call(cols_kernel, (at, held, coarse_nu), [(STRIPS, 128)] * 2)
    cols_a = swap(send_a, "sy", y_a)
    cols_b = swap(send_b, "sy", y_b)
    (chain_push,) = call(
        chain_push_kernel, (at,) + turbines, [(HALF, 2, 2, EXT, 128)], turbine_scratch, far=3, sems=3)
    send_a, send_b = call(rows_kernel, (at, held, coarse_nu, cols_a, cols_b), [(MESSAGE, 128)] * 2)
    rows_a = swap(send_a, "sx", x_a)
    rows_b = swap(send_b, "sx", x_b)
    blocks = (at, held, coarse_nu, cols_a, cols_b, rows_a, rows_b)
    field = (3, 2, 64, 128)
    state, moved, extra, coef = call(
        low_kernel, blocks + (chain_push,),
        [(64, 128), (48, 128), (3 * HALF, 2, EXT, 128), (4, 2, EXT, 128)],
        [field, field, (HALF, 3, 64, 128)],
    )
    state = lax.ppermute(state, "cuts", [(m, (m + 4 if m >= 4 else m + 12)) for m in range(HALF)])
    state_a = swap_high(state, count_x, x_a)
    state_b = swap_high(state, count_x, x_b)
    (out,) = call(
        high_kernel,
        (at, state, state_a, state_b, extra, coef, chain_push, fine, guess, moved),
        [(3, ROWS, COLS)],
        [field, field, (HALF, 3, 64, 128), (48, 128)],
    )
    return out[None]


def solution(mesh):
    in_specs = (P("cuts", None, "sx", "sy"), P("sx", "sy"), P(), P(), P())
    out_specs = P("cuts", None, "sx", "sy")
    return jax.shard_map(
        on_device, mesh=mesh, in_specs=in_specs, out_specs=out_specs, check_vma=False
    )
```

```python
import math

import jax
import jax.numpy as jnp
import numpy as np
from jax import lax
from jax.experimental import pallas as pl
from jax.experimental.pallas import tpu as pltpu
from jax.sharding import PartitionSpec as P

YAWS = 7
CUTS = 16
REACH = 3
F32 = jnp.float32
BF16 = jnp.bfloat16

FINE = (0.3, 0.25, 0.01)
FINE_THRUST = 0.5
FINE_SCALE = (0.25, 0.25, 0.025)
COARSE = (0.15, 0.125, 0.0025)
COARSE_THRUST = 1.0
COARSE_SCALE = (0.125, 0.125, 0.00625)
FINE_TO_COARSE = (0.5, 0.5, 0.25)

ROWS, COLS = 64, 512
CROWS, CCOLS = 16, 128
HALF = CUTS // 2
EXT = 48
NU = 24
ANGLES = [(k - 0.5 * (YAWS - 1)) * (math.pi / 18.0) for k in range(YAWS)]
WEIGHT_X = [float(np.float32(math.cos(t) ** 3)) for t in ANGLES]
WEIGHT_Y = [float(np.float32(math.cos(t) ** 2 * math.sin(t))) for t in ANGLES]

WIDTH = 32
_ORDER = list(range(9)) + [NU, 21, 22] + list(range(9, 21)) + [23]
GROUPS = [_ORDER[_i : _i + 4] for _i in range(0, len(_ORDER), 4)]
STRIPS = 16 * len(GROUPS)
PARTS = [(q, 16) for q in range(0, 9)] + [(q, 8) for q in range(9, 21)] + [(NU, 16)]
PART_AT = {}
_at = 0
for _q, _rows in PARTS:
    PART_AT[_q] = (_at, _rows)
    _at += _rows
STRIP_AT = {}
for _g, _rows in ((0, 16), (1, 16), (2, 16), (3, 8), (4, 8), (5, 8)):
    STRIP_AT[_g] = (_at, _rows)
    _at += 2 * _rows
MESSAGE = _at


def lanes(shape):
    return lax.broadcasted_iota(jnp.int32, shape, len(shape) - 1)


def sublanes(shape):
    return lax.broadcasted_iota(jnp.int32, shape, len(shape) - 2)


def rolled(x, by):
    return pltpu.roll(x, by % 128, 1) if by % 128 else x


def split3(x):
    high = x.astype(BF16)
    rest = x - high.astype(F32)
    middle = rest.astype(BF16)
    return high, middle, (rest - middle.astype(F32)).astype(BF16)


def exact_dot(x, y, dims=(((1,), (0,)), ((), ()))):
    count = x.shape[0]
    stacked = jnp.concatenate(split3(x), axis=0)
    out = lax.dot_general(stacked, y.astype(BF16), dims, preferred_element_type=F32)
    return out[0:count] + (out[count : 2 * count] + out[2 * count : 3 * count])


def advance(src, dst, coef, push, shift, row, count, tiles, wanted, terms, side_mask, post=None):
    _, lift, gain = terms
    lane = lanes((count, 128))
    low, high = lane == 0, lane == 127
    here, east, west = pl.ds(row, count), pl.ds(row + 1, count), pl.ds(row - 1, count)
    there = pl.ds(row - shift, count)
    mid = [[src[f, c, here, :] for c in range(tiles)] for f in range(3)]
    up = [[pltpu.roll(mid[f][c], 127, 1) for c in range(tiles)] for f in range(3)]
    down = [[pltpu.roll(mid[f][c], 1, 1) for c in range(tiles)] for f in range(3)]
    for c in wanted:
        after, before = (c + 1) % tiles, (c - 1) % tiles
        u, v, p = mid[0][c], mid[1][c], mid[2][c]
        un, vn, pn = [jnp.where(high, up[f][after], up[f][c]) for f in range(3)]
        us, vs, ps = [jnp.where(low, down[f][before], down[f][c]) for f in range(3)]
        ue, ve, pe = [src[f, c, east, :] for f in range(3)]
        uw, vw, pw = [src[f, c, west, :] for f in range(3)]
        nu, nu_carry, keep, keep_p = [coef[k, c, there, :] for k in range(4)]
        to_east, to_west = nu - u, nu_carry + u
        lifted = u + lift
        size = jnp.abs(lifted)
        drag = lifted * size / (size + lift)
        new_u = ue * to_east + uw * to_west + nu * (un + us) + keep * u - (pe - pw) - push(0, c, there) * drag
        new_v = ve * to_east + vw * to_west + nu * (vn + vs) + keep * v - (pn - ps) - push(1, c, there) * drag
        new_p = nu * ((pe + pw) + (pn + ps)) + keep_p * p - gain * ((ue - uw) + (vn - vs))
        new = [new_u, new_v, new_p]
        if c == tiles - 1:
            new = [f * side_mask for f in new]
        for f in range(3):
            if post is not None:
                new[f] = post(f, c, here, new[f])
            dst[f, c, here, :] = new[f]


def clear_rows(ref, tiles, before, after, outside):
    for row, factor in ((before, outside[0]), (after, outside[1])):
        for f in range(3):
            for c in range(tiles):
                ref[f, c, pl.ds(row, 1), :] = ref[f, c, pl.ds(row, 1), :] * factor


def edges(at):
    lane = lanes((8, 128))
    outside = [jnp.where(at[1] > 0, 1.0, 0.0), jnp.where(at[1] < at[3] - 1, 1.0, 0.0)]
    side = jnp.where(lane < 64, jnp.where(at[2] < at[4] - 1, 1.0, 0.0), jnp.where(at[2] > 0, 1.0, 0.0))
    return outside, side


def coefficients(coef, c, rows, nu, carry):
    coef[0, c, rows, :] = nu
    coef[1, c, rows, :] = nu + carry
    coef[2, c, rows, :] = (1.0 - carry) - 4.0 * nu
    coef[3, c, rows, :] = 1.0 - 4.0 * nu


def yaw_weights(yaw):
    wx = jnp.zeros(yaw.shape, F32)
    wy = jnp.zeros(yaw.shape, F32)
    for k in range(YAWS):
        hit = yaw == k
        wx = jnp.where(hit, WEIGHT_X[k], wx)
        wy = jnp.where(hit, WEIGHT_Y[k], wy)
    return wx, wy


def fetch(pairs, sems):
    copies = [pltpu.make_async_copy(a, b, sems.at[i]) for i, (a, b) in enumerate(pairs)]
    for copy in copies:
        copy.start()
    for copy in copies:
        copy.wait()


def load_kernel(at, start, visc, own, sems):
    fetch(
        [(start.at[:, :, 128 * c : 128 * c + 128], own.at[0:3, c]) for c in range(4)]
        + [(visc.at[:, 128 * c : 128 * c + 128], own.at[3, c]) for c in range(4)],
        sems,
    )


def edge_rows(start, visc, first):
    return jnp.concatenate([
        lax.dynamic_slice(start, (0, first, 0), (3, 8, COLS)),
        lax.dynamic_slice(visc, (first, 0), (8, COLS))[None],
    ])


def side_kernel(at, own, got_a, got_b, send_a, send_b):
    even_x = lax.rem(at[1], 2) == 0
    even_y = lax.rem(at[2], 2) == 0
    for r0, count in ((0, 8), (8, 64), (72, 8)):
        lane = lanes((count, 128))
        left = jnp.zeros((count, 128), F32)
        right = jnp.zeros((count, 128), F32)
        for f in range(4):
            if r0 == 8:
                a, b = own[f, 0], own[f, 3]
            else:
                from_a = jnp.logical_xor(even_x, r0 == 0)
                a = jnp.where(from_a, got_a[f, :, 0:128], got_b[f, :, 0:128])
                b = jnp.where(from_a, got_a[f, :, COLS - 128 : COLS], got_b[f, :, COLS - 128 : COLS])
            mine = (lane >= 8 * f) & (lane < 8 * f + 8)
            left = jnp.where(mine, rolled(a, 8 * f), left)
            right = jnp.where(mine, rolled(b, 8 * f + 8), right)
        send_a[r0 : r0 + count, :] = jnp.where(even_y, right, left)
        send_b[r0 : r0 + count, :] = jnp.where(even_y, left, right)


def fine_cols(sy, c, shape):
    i = sublanes(shape)
    return sy * COLS + (128 * c + i if c < 4 else jnp.where(i < 64, COLS + i, i - 128))


def coarse_cols(sy, c, ty):
    i = sublanes((128, 64))
    col = sy * CCOLS + (i if c == 0 else jnp.where(i < 64, CCOLS + i, i - 128))
    hit = jnp.zeros((128, 64), F32)
    for offset in range(4):
        hit = hit + jnp.where(jnp.abs(4 * col + offset - ty) <= REACH, 0.25, 0.0)
    return hit


LAST_DIMS = (((1,), (1,)), ((), ()))


def push_kernel(at, tx_in, ty_in, yaw_in, fine_push, own_push, tx_ref, ty_ref, yaw_ref, sems):
    fetch([(tx_in, tx_ref), (ty_in, ty_ref), (yaw_in, yaw_ref)], sems)
    tx, ty = tx_ref[...], ty_ref[...]
    mine = sublanes((CUTS, 64)) == at[0]
    wx, wy = yaw_weights(jnp.sum(jnp.where(mine, yaw_ref[...], 0), axis=0, keepdims=True))
    row = at[1] * ROWS - 16 + sublanes((96, 64))
    hit = jnp.where(row == tx, FINE_THRUST, 0.0)
    both = jnp.concatenate([hit * wx, hit * wy], axis=0)
    for c in range(5):
        cols = jnp.where(jnp.abs(fine_cols(at[2], c, (128, 64)) - ty) <= REACH, 1.0, 0.0)
        push = exact_dot(both, cols, LAST_DIMS)
        fine_push[0, c] = push[0:96]
        fine_push[1, c] = push[96:192]
    row = at[1] * CROWS - 10 + sublanes((40, 64))
    hit = jnp.where(row == tx // 4, 0.25 * COARSE_THRUST, 0.0)
    both = jnp.concatenate([hit * wx, hit * wy], axis=0)
    for c in range(2):
        push = exact_dot(both, coarse_cols(at[2], c, ty), LAST_DIMS)
        own_push[0, c] = push[0:40]
        own_push[1, c] = push[40:80]


def chain_push_kernel(at, tx_in, ty_in, yaw_in, push, tx_ref, ty_ref, yaw_ref, sems):
    fetch([(tx_in, tx_ref), (ty_in, ty_ref), (yaw_in, yaw_ref)], sems)
    tx, ty = tx_ref[...], ty_ref[...]
    row = at[1] * CROWS - 16 + sublanes((EXT, 64))
    hit = jnp.where(row == tx // 4, 0.25 * COARSE_THRUST, 0.0)
    wx, wy = yaw_weights(yaw_ref[pl.ds(pl.multiple_of(at[0] // HALF * HALF, HALF), HALF), :])
    cols = [coarse_cols(at[2], c, ty) for c in range(2)]
    for k in range(HALF):
        both = jnp.concatenate([hit * wx[k : k + 1, :], hit * wy[k : k + 1, :]], axis=0)
        for c in range(2):
            value = exact_dot(both, cols[c], LAST_DIMS)
            push[k, 0, c] = value[0:EXT]
            push[k, 1, c] = value[EXT : 2 * EXT]


def fine_kernel(at, own, rows_a, rows_b, cols_a, cols_b, push, own_push, fine, guess, sent, coarse_nu,
                one, two, coef, rough, rough_two, rough_coef):
    even_x = lax.rem(at[1], 2) == 0
    even_y = lax.rem(at[2], 2) == 0
    outside, side_mask = edges(at)
    after_all = jnp.where(even_y, cols_a[...], cols_b[...])
    before_all = jnp.where(even_y, cols_b[...], cols_a[...])
    lane = lanes((80, 128))
    for f in range(4):
        for c in range(5):
            if c < 4:
                cut = slice(128 * c, 128 * c + 128)
                a, b = rows_a[f, :, cut], rows_b[f, :, cut]
                pieces = [(8, 8, jnp.where(even_x, b, a)), (16, 64, own[f, c]), (80, 8, jnp.where(even_x, a, b))]
            else:
                after, before = rolled(after_all, -8 * f), rolled(before_all, 120 - 8 * f)
                pieces = [(8, 80, jnp.where(lane < 8, after, jnp.where(lane >= 120, before, 0.0)))]
            for r, count, value in pieces:
                if f < 3:
                    one[f, c, r : r + count, :] = value * FINE_SCALE[f]
                else:
                    coefficients(coef, c, pl.ds(r, count), value, FINE[0])

    i, j = sublanes((COLS, 128)), lanes((COLS, 128))
    gather = jnp.where(i // 4 == j, 0.0625, 0.0)
    i, j = sublanes((128, 128)), lanes((128, 128))
    gather_side = jnp.where(((i < 8) & (i // 4 == j)) | ((i >= 120) & ((i - 120) // 4 == j - 126)), 0.0625, 0.0)

    def row_sum(ref, first, count):
        parts = [ref[pl.ds(first + k, count, stride=4), :] for k in range(4)]
        return (parts[0] + parts[1]) + (parts[2] + parts[3])

    def pick(f, c):
        return one.at[f, c] if f < 3 else coef.at[0, c]

    body = [jnp.concatenate([row_sum(pick(f, c), 0, 24) for c in range(4)], axis=1) for f in range(4)]
    side = [row_sum(pick(f, 4), 0, 24) for f in range(4)]
    body = exact_dot(jnp.concatenate(body, axis=0), gather)
    side = exact_dot(jnp.concatenate(side, axis=0), gather_side)
    rough[...] = jnp.zeros(rough.shape, F32)
    rough_two[...] = jnp.zeros(rough_two.shape, F32)
    rough_coef[...] = jnp.zeros(rough_coef.shape, F32)
    for c, value in enumerate((body, side)):
        for f in range(3):
            rough[f, c, 6:30, :] = value[24 * f : 24 * f + 24, :] * FINE_TO_COARSE[f]
        coefficients(rough_coef, c, pl.ds(6, 24), value[72:96, :] * 0.5, COARSE[0])
    coarse_nu[...] = rough_coef[0, 0, 10:26, :]

    def coarse_push(d, c, r):
        return own_push[d, c, r, :]

    for k in range(3):
        advance(rough, rough_two, rough_coef, coarse_push, 0, 9 + 8 * k, 8, 2, (0, 1), COARSE, side_mask)
    clear_rows(rough_two, 2, 9, 26, outside)
    for k in range(2):
        advance(rough_two, rough, rough_coef, coarse_push, 0, 10 + 8 * k, 8, 2, (0,), COARSE, side_mask)
    for f in range(3):
        guess[16 * f : 16 * f + 16, :] = rough[f, 0, 10:26, :]

    def fine_push(d, c, r):
        return push[d, c, r, :]

    for src, dst, first, count, wanted in (
        (one, two, 12, 9, range(5)),
        (two, one, 12, 9, range(5)),
        (one, two, 12, 9, range(5)),
        (two, one, 16, 8, range(4)),
    ):
        for k in range(count):
            advance(src, dst, coef, fine_push, 0, first + 8 * k, 8, 5, wanted, FINE, side_mask)
        if count == 9:
            clear_rows(dst, 5, 15, 80, outside)
    for f in range(3):
        for c in range(4):
            fine[f, :, 128 * c : 128 * c + 128] = one[f, c, 16:80, :] * (1.0 / FINE_SCALE[f])
    ends = [jnp.concatenate([row_sum(one.at[f, c], 16, 16) for c in range(4)], axis=1) for f in range(3)]
    ends = exact_dot(jnp.concatenate(ends, axis=0), gather)
    first_slice = at[0] == 0
    for f in range(3):
        cut = slice(16 * f, 16 * f + 16)
        defect = ends[cut] * FINE_TO_COARSE[f] - jnp.where(first_slice, 0.0, guess[cut, :])
        for m in range(HALF):
            sent[m, cut, :] = defect


def plane_of(held, nu, q):
    return nu[...] if q == NU else held[q // 3, 16 * (q % 3) : 16 * (q % 3) + 16, :]


def cols_kernel(at, held, nu, send_a, send_b):
    even_y = lax.rem(at[2], 2) == 0
    lane = lanes((16, 128))
    for g, members in enumerate(GROUPS):
        left = jnp.zeros((16, 128), F32)
        right = jnp.zeros((16, 128), F32)
        for slot, q in enumerate(members):
            offset = slot * WIDTH
            value = plane_of(held, nu, q)
            mine = (lane >= offset) & (lane < offset + WIDTH)
            left = jnp.where(mine, rolled(value, offset), left)
            right = jnp.where(mine, rolled(value, offset + WIDTH), right)
        send_a[16 * g : 16 * g + 16, :] = jnp.where(even_y, right, left)
        send_b[16 * g : 16 * g + 16, :] = jnp.where(even_y, left, right)


def rows_kernel(at, held, nu, cols_a, cols_b, send_a, send_b):
    even = lax.rem(at[1], 2) == 0

    def put(place, rows, value):
        if rows == 16:
            send_a[place : place + 16, :] = value
            send_b[place : place + 16, :] = value
        else:
            send_a[place : place + 8, :] = jnp.where(even, value[8:16], value[0:8])
            send_b[place : place + 8, :] = jnp.where(even, value[0:8], value[8:16])

    for q, rows in PARTS:
        put(PART_AT[q][0], rows, plane_of(held, nu, q))
    for g, (place, rows) in STRIP_AT.items():
        put(place, rows, cols_a[16 * g : 16 * g + 16, :])
        put(place + rows, rows, cols_b[16 * g : 16 * g + 16, :])


def assemble(at, held, nu, cols_a, cols_b, rows_a, rows_b, put):
    even_x = lax.rem(at[1], 2) == 0
    even_y = lax.rem(at[2], 2) == 0

    def sides(place, rows):
        a, b = rows_a[place : place + rows, :], rows_b[place : place + rows, :]
        return jnp.where(even_x, b, a), jnp.where(even_x, a, b)

    for q in range(NU + 1):
        put(q, 0, 16, plane_of(held, nu, q))
        if q in PART_AT:
            place, rows = PART_AT[q]
            before, after = sides(place, rows)
            put(q, 0, 16 - rows, before)
            put(q, 0, 32, after)
    for g, members in enumerate(GROUPS):
        cut = slice(16 * g, 16 * g + 16)
        blocks = [(16, cols_a[cut, :], cols_b[cut, :])]
        if g in STRIP_AT:
            place, rows = STRIP_AT[g]
            before_a, after_a = sides(place, rows)
            before_b, after_b = sides(place + rows, rows)
            blocks += [(16 - rows, before_a, before_b), (32, after_a, after_b)]
        for first, a, b in blocks:
            lane = lanes(a.shape)
            after, before = jnp.where(even_y, a, b), jnp.where(even_y, b, a)
            for slot, q in enumerate(members):
                if first == 16 or q in PART_AT:
                    hi, lo = rolled(after, -slot * WIDTH), rolled(before, 128 - WIDTH - slot * WIDTH)
                    put(q, 1, first, jnp.where(lane < WIDTH, hi, jnp.where(lane >= 128 - WIDTH, lo, 0.0)))


def putter(extra, coef):
    def put(q, c, row, value):
        rows = pl.ds(row, value.shape[0])
        if q == NU:
            coefficients(coef, c, rows, value, COARSE[0])
        else:
            extra[q, c, rows, :] = value

    return put


def chain(first_k, one, two, coef, push, extra, kept, at):
    outside, side_mask = edges(at)

    for k in range(first_k, HALF):
        def pushed(d, c, r, k=k):
            return push[k, d, c, r, :]

        def keep_and_add(f, c, r, value, k=k):
            if c == 0:
                kept[k, f, r, :] = value
            return value + extra[3 * k + f, c, pl.ds(r.start - 8, r.size), :]

        for half in range(2):
            halo = 2 * (HALF - 1 - k) + 1 - half
            count = 2 + -(-halo // 4)
            first = min(8 + 16 - halo, 8 + EXT - 8 * count)
            src, dst = (one, two) if half == 0 else (two, one)
            post = keep_and_add if half else None
            for i in range(count):
                advance(src, dst, coef, pushed, 8, first + 8 * i, 8, 2, (0, 1), COARSE, side_mask, post=post)
            if halo:
                clear_rows(dst, 2, 8 + 15, 8 + 32, outside)


def low_kernel(at, held, nu, cols_a, cols_b, rows_a, rows_b, push, state, moved, extra, coef, one, two, kept):
    @pl.when(at[0] < HALF)
    def _():
        assemble(at, held, nu, cols_a, cols_b, rows_a, rows_b, putter(extra, coef))
        for f in range(3):
            for c in range(2):
                one[f, c, 8:56, :] = extra[f, c]
        chain(1, one, two, coef, push, extra, kept, at)
        lane = lanes((CROWS, 128))
        sides = jnp.zeros((CROWS, 128), F32)
        for f in range(3):
            state[16 * f : 16 * f + 16, :] = one[f, 0, 24:40, :]
            sides = jnp.where(lane // 32 == f, rolled(one[f, 1, 24:40, :], 16 + 32 * f), sides)
        state[48:64, :] = sides
        for f in range(3):
            moved[16 * f : 16 * f + 16, :] = kept[jnp.maximum(at[0], 1), f, 24:40, :]


def planes_kernel(at, held, nu, cols_a, cols_b, rows_a, rows_b, extra, coef):
    @pl.when(at[0] >= HALF)
    def _():
        assemble(at, held, nu, cols_a, cols_b, rows_a, rows_b, putter(extra, coef))


def high_kernel(at, state, state_a, state_b, extra, coef, push, fine, guess, moved_low, out, one, two, kept, moved, spread):
    even_x = lax.rem(at[1], 2) == 0

    @pl.when(at[0] < HALF)
    def _():
        moved[...] = moved_low[...]

    @pl.when(at[0] >= HALF)
    def _():
        lane = lanes((CROWS, 128))
        a, b = state_a[...], state_b[...]
        for row, block in ((8, jnp.where(even_x, b, a)), (24, state[...]), (40, jnp.where(even_x, a, b))):
            for f in range(3):
                one[f, 0, row : row + 16, :] = block[16 * f : 16 * f + 16]
                side = rolled(block[48:64], -(16 + 32 * f))
                one[f, 1, row : row + 16, :] = jnp.where((lane < 16) | (lane >= 112), side, 0.0)
        chain(0, one, two, coef, push, extra, kept, at)
        for f in range(3):
            moved[16 * f : 16 * f + 16, :] = kept[at[0] - HALF, f, 24:40, :]

    parts = []
    for f in range(3):
        cut = slice(16 * f, 16 * f + 16)
        parts.append(jnp.where(at[0] == 0, 0.0, (moved[cut, :] - guess[cut, :]) * (1.0 / COARSE_SCALE[f])))
    change = jnp.concatenate(parts, axis=0)
    i, j = sublanes((128, COLS)), lanes((128, COLS))
    change = exact_dot(change, jnp.where(i == j // 4, 1.0, 0.0))
    for f in range(3):
        for c in range(4):
            cut = slice(128 * c, 128 * c + 128)
            for k in range(4):
                spread[f, c, pl.ds(k, CROWS, stride=4), :] = change[16 * f : 16 * f + 16, cut]
            out[f, :, cut] = fine[f, :, cut] + spread[f, c]


SMEM = pl.BlockSpec(memory_space=pltpu.SMEM)
VMEM = pl.BlockSpec(memory_space=pltpu.VMEM)
HBM = pl.BlockSpec(memory_space=pltpu.HBM)


def call(kernel, args, outs, scratch=(), far=0, sems=0):
    shapes = [jax.ShapeDtypeStruct(s, F32) for s in outs]
    near = len(args) - 1 - far
    memory = [s if not isinstance(s, tuple) else pltpu.VMEM(s, F32) for s in scratch]
    if sems:
        memory.append(pltpu.SemaphoreType.DMA((sems,)))
    return pl.pallas_call(
        kernel,
        out_shape=shapes,
        in_specs=[SMEM] + [VMEM] * near + [HBM] * far,
        out_specs=[VMEM] * len(shapes),
        scratch_shapes=memory,
        compiler_params=pltpu.CompilerParams(vmem_limit_bytes=48 * 1024 * 1024),
    )(*args)


def swap(x, axis, pairs):
    return lax.ppermute(x, axis, [(a, b) for a, b in pairs] + [(b, a) for a, b in pairs])


def swap_high(x, count, pairs):
    both = [(a, b) for a, b in pairs] + [(b, a) for a, b in pairs]
    return lax.ppermute(x, ("cuts", "sx"), [(n * count + a, n * count + b) for n in range(HALF, CUTS) for a, b in both])


def on_device(starts, viscosity, turbine_x, turbine_y, yaw_index):
    count_x, count_y = lax.axis_size("sx"), lax.axis_size("sy")
    at = jnp.stack([
        lax.axis_index("cuts"), lax.axis_index("sx"), lax.axis_index("sy"),
        jnp.int32(count_x), jnp.int32(count_y),
    ]).astype(jnp.int32)
    start = starts[0]
    x_a = [(i, i + 1) for i in range(0, count_x - 1, 2)]
    x_b = [(i, i + 1) for i in range(1, count_x - 1, 2)]
    y_a = [(i, i + 1) for i in range(0, count_y - 1, 2)]
    y_b = [(i, i + 1) for i in range(1, count_y - 1, 2)]
    turbines = (turbine_x[None, :], turbine_y[None, :], yaw_index)
    turbine_scratch = [pltpu.VMEM((1, 64), jnp.int32), pltpu.VMEM((1, 64), jnp.int32), pltpu.VMEM((CUTS, 64), jnp.int32)]

    odd = at[1] % 2
    rows_b = swap(edge_rows(start, viscosity, 56 * odd), "sx", x_b)
    rows_a = swap(edge_rows(start, viscosity, 56 * (1 - odd)), "sx", x_a)
    (own,) = call(load_kernel, (at, start, viscosity), [(4, 4, ROWS, 128)], far=2, sems=8)
    send_a, send_b = call(side_kernel, (at, own, rows_a, rows_b), [(80, 128)] * 2)
    cols_a = swap(send_a, "sy", y_a)
    cols_b = swap(send_b, "sy", y_b)
    push, own_push = call(
        push_kernel, (at,) + turbines, [(2, 5, 96, 128), (2, 2, 40, 128)], turbine_scratch, far=3, sems=3)
    fine, guess, sent, coarse_nu = call(
        fine_kernel,
        (at, own, rows_a, rows_b, cols_a, cols_b, push, own_push),
        [(3, ROWS, COLS), (48, 128), (HALF, 48, 128), (CROWS, 128)],
        [(3, 5, 96, 128), (3, 5, 96, 128), (4, 5, 96, 128), (3, 2, 40, 128), (3, 2, 40, 128), (4, 2, 40, 128)],
    )
    halves = [list(range(HALF)), list(range(HALF, CUTS))]
    held = lax.all_to_all(sent, "cuts", 0, 0, axis_index_groups=halves)
    send_a, send_b = call(cols_kernel, (at, held, coarse_nu), [(STRIPS, 128)] * 2)
    cols_a = swap(send_a, "sy", y_a)
    cols_b = swap(send_b, "sy", y_b)
    (chain_push,) = call(
        chain_push_kernel, (at,) + turbines, [(HALF, 2, 2, EXT, 128)], turbine_scratch, far=3, sems=3)
    send_a, send_b = call(rows_kernel, (at, held, coarse_nu, cols_a, cols_b), [(MESSAGE, 128)] * 2)
    rows_a = swap(send_a, "sx", x_a)
    rows_b = swap(send_b, "sx", x_b)
    blocks = (at, held, coarse_nu, cols_a, cols_b, rows_a, rows_b)
    field, planes, terms = (3, 2, 64, 128), (3 * HALF, 2, EXT, 128), (4, 2, EXT, 128)
    state, moved = call(
        low_kernel, blocks + (chain_push,), [(64, 128), (48, 128)], [planes, terms, field, field, (HALF, 3, 64, 128)])
    goes = [(m, m + 4 if m >= 4 else m + 12) for m in range(HALF)]
    state_b, state_a = [
        lax.ppermute(state, ("cuts", "sx"), [(m * count_x + i, n * count_x + (i ^ flip)) for m, n in goes for i in range(count_x)])
        for flip in (0, 1)
    ]
    state = state_b
    state_b = swap_high(state, count_x, x_b)
    extra, coef = call(planes_kernel, blocks, [planes, terms])
    (out,) = call(
        high_kernel,
        (at, state, state_a, state_b, extra, coef, chain_push, fine, guess, moved),
        [(3, ROWS, COLS)],
        [field, field, (HALF, 3, 64, 128), (48, 128), (3, 4, ROWS, 128)],
    )
    return out[None]


def solution(mesh):
    in_specs = (P("cuts", None, "sx", "sy"), P("sx", "sy"), P(), P(), P())
    out_specs = P("cuts", None, "sx", "sy")
    return jax.shard_map(
        on_device, mesh=mesh, in_specs=in_specs, out_specs=out_specs, check_vma=False
    )
```

```python
import math

import jax
import jax.numpy as jnp
import numpy as np
from jax import lax
from jax.experimental import pallas as pl
from jax.experimental.pallas import tpu as pltpu
from jax.sharding import PartitionSpec as P

YAWS = 7
CUTS = 16
REACH = 3
F32 = jnp.float32
BF16 = jnp.bfloat16

FINE = (0.3, 0.25, 0.01)
FINE_THRUST = 0.5
FINE_SCALE = (0.25, 0.25, 0.025)
COARSE = (0.15, 0.125, 0.0025)
COARSE_THRUST = 1.0
COARSE_SCALE = (0.125, 0.125, 0.00625)
FINE_TO_COARSE = (0.5, 0.5, 0.25)

ROWS, COLS = 64, 512
CROWS, CCOLS = 16, 128
HALF = CUTS // 2
EXT = 48
NU = 24
ANGLES = [(k - 0.5 * (YAWS - 1)) * (math.pi / 18.0) for k in range(YAWS)]
WEIGHT_X = [float(np.float32(math.cos(t) ** 3)) for t in ANGLES]
WEIGHT_Y = [float(np.float32(math.cos(t) ** 2 * math.sin(t))) for t in ANGLES]

WIDTH = 32
_ORDER = list(range(9)) + [NU, 21, 22] + list(range(9, 21)) + [23]
GROUPS = [_ORDER[_i : _i + 4] for _i in range(0, len(_ORDER), 4)]
STRIPS = 16 * len(GROUPS)
PARTS = [(q, 16) for q in range(0, 9)] + [(q, 8) for q in range(9, 21)] + [(NU, 16)]
PART_AT = {}
_at = 0
for _q, _rows in PARTS:
    PART_AT[_q] = (_at, _rows)
    _at += _rows
STRIP_AT = {}
for _g, _rows in ((0, 16), (1, 16), (2, 16), (3, 8), (4, 8), (5, 8)):
    STRIP_AT[_g] = (_at, _rows)
    _at += 2 * _rows
MESSAGE = _at


def lanes(shape):
    return lax.broadcasted_iota(jnp.int32, shape, len(shape) - 1)


def sublanes(shape):
    return lax.broadcasted_iota(jnp.int32, shape, len(shape) - 2)


def rolled(x, by):
    return pltpu.roll(x, by % 128, 1) if by % 128 else x


def split3(x):
    high = x.astype(BF16)
    rest = x - high.astype(F32)
    middle = rest.astype(BF16)
    return high, middle, (rest - middle.astype(F32)).astype(BF16)


def exact_dot(x, y, dims=(((1,), (0,)), ((), ()))):
    count = x.shape[0]
    stacked = jnp.concatenate(split3(x), axis=0)
    out = lax.dot_general(stacked, y.astype(BF16), dims, preferred_element_type=F32)
    return out[0:count] + (out[count : 2 * count] + out[2 * count : 3 * count])


def advance(src, dst, coef, push, shift, row, count, tiles, wanted, terms, side_mask, post=None):
    _, lift, gain = terms
    lane = lanes((count, 128))
    low, high = lane == 0, lane == 127
    here, east, west = pl.ds(row, count), pl.ds(row + 1, count), pl.ds(row - 1, count)
    there = pl.ds(row - shift, count)
    mid = [[src[f, c, here, :] for c in range(tiles)] for f in range(3)]
    up = [[pltpu.roll(mid[f][c], 127, 1) for c in range(tiles)] for f in range(3)]
    down = [[pltpu.roll(mid[f][c], 1, 1) for c in range(tiles)] for f in range(3)]
    for c in wanted:
        after, before = (c + 1) % tiles, (c - 1) % tiles
        u, v, p = mid[0][c], mid[1][c], mid[2][c]
        un, vn, pn = [jnp.where(high, up[f][after], up[f][c]) for f in range(3)]
        us, vs, ps = [jnp.where(low, down[f][before], down[f][c]) for f in range(3)]
        ue, ve, pe = [src[f, c, east, :] for f in range(3)]
        uw, vw, pw = [src[f, c, west, :] for f in range(3)]
        nu, nu_carry, keep, keep_p = [coef[k, c, there, :] for k in range(4)]
        to_east, to_west = nu - u, nu_carry + u
        lifted = u + lift
        size = jnp.abs(lifted)
        drag = lifted * size / (size + lift)
        new_u = ue * to_east + uw * to_west + nu * (un + us) + keep * u - (pe - pw) - push(0, c, there) * drag
        new_v = ve * to_east + vw * to_west + nu * (vn + vs) + keep * v - (pn - ps) - push(1, c, there) * drag
        new_p = nu * ((pe + pw) + (pn + ps)) + keep_p * p - gain * ((ue - uw) + (vn - vs))
        new = [new_u, new_v, new_p]
        if c == tiles - 1:
            new = [f * side_mask for f in new]
        for f in range(3):
            if post is not None:
                new[f] = post(f, c, here, new[f])
            dst[f, c, here, :] = new[f]


def clear_rows(ref, tiles, before, after, outside):
    for row, factor in ((before, outside[0]), (after, outside[1])):
        for f in range(3):
            for c in range(tiles):
                ref[f, c, pl.ds(row, 1), :] = ref[f, c, pl.ds(row, 1), :] * factor


def edges(at):
    lane = lanes((8, 128))
    outside = [jnp.where(at[1] > 0, 1.0, 0.0), jnp.where(at[1] < at[3] - 1, 1.0, 0.0)]
    side = jnp.where(lane < 64, jnp.where(at[2] < at[4] - 1, 1.0, 0.0), jnp.where(at[2] > 0, 1.0, 0.0))
    return outside, side


def coefficients(coef, c, rows, nu, carry):
    coef[0, c, rows, :] = nu
    coef[1, c, rows, :] = nu + carry
    coef[2, c, rows, :] = (1.0 - carry) - 4.0 * nu
    coef[3, c, rows, :] = 1.0 - 4.0 * nu


def yaw_weights(yaw):
    wx = jnp.zeros(yaw.shape, F32)
    wy = jnp.zeros(yaw.shape, F32)
    for k in range(YAWS):
        hit = yaw == k
        wx = jnp.where(hit, WEIGHT_X[k], wx)
        wy = jnp.where(hit, WEIGHT_Y[k], wy)
    return wx, wy


def fetch(pairs, sems):
    copies = [pltpu.make_async_copy(a, b, sems.at[i]) for i, (a, b) in enumerate(pairs)]
    for copy in copies:
        copy.start()
    for copy in copies:
        copy.wait()


def edge_rows(start, visc, first):
    return jnp.concatenate([
        lax.dynamic_slice(start, (0, first, 0), (3, 8, COLS)),
        lax.dynamic_slice(visc, (first, 0), (8, COLS))[None],
    ])


def side_kernel(at, own, got_a, got_b, send_a, send_b):
    even_x = lax.rem(at[1], 2) == 0
    even_y = lax.rem(at[2], 2) == 0
    for r0, count in ((0, 8), (8, 64), (72, 8)):
        lane = lanes((count, 128))
        left = jnp.zeros((count, 128), F32)
        right = jnp.zeros((count, 128), F32)
        for f in range(4):
            if r0 == 8:
                a, b = own[f, :, 0:128], own[f, :, COLS - 128 : COLS]
            else:
                from_a = jnp.logical_xor(even_x, r0 == 0)
                a = jnp.where(from_a, got_a[f, :, 0:128], got_b[f, :, 0:128])
                b = jnp.where(from_a, got_a[f, :, COLS - 128 : COLS], got_b[f, :, COLS - 128 : COLS])
            mine = (lane >= 8 * f) & (lane < 8 * f + 8)
            left = jnp.where(mine, rolled(a, 8 * f), left)
            right = jnp.where(mine, rolled(b, 8 * f + 8), right)
        send_a[r0 : r0 + count, :] = jnp.where(even_y, right, left)
        send_b[r0 : r0 + count, :] = jnp.where(even_y, left, right)


def fine_cols(sy, c, shape):
    i = sublanes(shape)
    return sy * COLS + (128 * c + i if c < 4 else jnp.where(i < 64, COLS + i, i - 128))


def coarse_cols(sy, c, ty):
    i = sublanes((128, 64))
    col = sy * CCOLS + (i if c == 0 else jnp.where(i < 64, CCOLS + i, i - 128))
    hit = jnp.zeros((128, 64), F32)
    for offset in range(4):
        hit = hit + jnp.where(jnp.abs(4 * col + offset - ty) <= REACH, 0.25, 0.0)
    return hit


LAST_DIMS = (((1,), (1,)), ((), ()))


def push_kernel(at, tx_in, ty_in, yaw_in, fine_push, own_push, tx_ref, ty_ref, yaw_ref, sems):
    fetch([(tx_in, tx_ref), (ty_in, ty_ref), (yaw_in, yaw_ref)], sems)
    tx, ty = tx_ref[...], ty_ref[...]
    mine = sublanes((CUTS, 64)) == at[0]
    wx, wy = yaw_weights(jnp.sum(jnp.where(mine, yaw_ref[...], 0), axis=0, keepdims=True))
    row = at[1] * ROWS - 16 + sublanes((96, 64))
    hit = jnp.where(row == tx, FINE_THRUST, 0.0)
    both = jnp.concatenate([hit * wx, hit * wy], axis=0)
    for c in range(5):
        cols = jnp.where(jnp.abs(fine_cols(at[2], c, (128, 64)) - ty) <= REACH, 1.0, 0.0)
        push = exact_dot(both, cols, LAST_DIMS)
        fine_push[0, c] = push[0:96]
        fine_push[1, c] = push[96:192]
    row = at[1] * CROWS - 10 + sublanes((40, 64))
    hit = jnp.where(row == tx // 4, 0.25 * COARSE_THRUST, 0.0)
    both = jnp.concatenate([hit * wx, hit * wy], axis=0)
    for c in range(2):
        push = exact_dot(both, coarse_cols(at[2], c, ty), LAST_DIMS)
        own_push[0, c] = push[0:40]
        own_push[1, c] = push[40:80]


def chain_push_kernel(at, tx_in, ty_in, yaw_in, push, tx_ref, ty_ref, yaw_ref, sems):
    fetch([(tx_in, tx_ref), (ty_in, ty_ref), (yaw_in, yaw_ref)], sems)
    tx, ty = tx_ref[...], ty_ref[...]
    row = at[1] * CROWS - 16 + sublanes((EXT, 64))
    hit = jnp.where(row == tx // 4, 0.25 * COARSE_THRUST, 0.0)
    wx, wy = yaw_weights(yaw_ref[pl.ds(pl.multiple_of(at[0] // HALF * HALF, HALF), HALF), :])
    cols = [coarse_cols(at[2], c, ty) for c in range(2)]
    for k in range(HALF):
        both = jnp.concatenate([hit * wx[k : k + 1, :], hit * wy[k : k + 1, :]], axis=0)
        for c in range(2):
            value = exact_dot(both, cols[c], LAST_DIMS)
            push[k, 0, c] = value[0:EXT]
            push[k, 1, c] = value[EXT : 2 * EXT]


def fine_kernel(at, own, rows_a, rows_b, cols_a, cols_b, push, own_push, fine, guess, sent, coarse_nu,
                one, two, coef, rough, rough_two, rough_coef):
    even_x = lax.rem(at[1], 2) == 0
    even_y = lax.rem(at[2], 2) == 0
    outside, side_mask = edges(at)
    after_all = jnp.where(even_y, cols_a[...], cols_b[...])
    before_all = jnp.where(even_y, cols_b[...], cols_a[...])
    lane = lanes((80, 128))
    for f in range(4):
        for c in range(5):
            if c < 4:
                cut = slice(128 * c, 128 * c + 128)
                a, b = rows_a[f, :, cut], rows_b[f, :, cut]
                pieces = [(8, 8, jnp.where(even_x, b, a)), (16, 64, own[f, :, cut]), (80, 8, jnp.where(even_x, a, b))]
            else:
                after, before = rolled(after_all, -8 * f), rolled(before_all, 120 - 8 * f)
                pieces = [(8, 80, jnp.where(lane < 8, after, jnp.where(lane >= 120, before, 0.0)))]
            for r, count, value in pieces:
                if f < 3:
                    one[f, c, r : r + count, :] = value * FINE_SCALE[f]
                else:
                    coefficients(coef, c, pl.ds(r, count), value, FINE[0])

    i, j = sublanes((COLS, 128)), lanes((COLS, 128))
    gather = jnp.where(i // 4 == j, 0.0625, 0.0)
    i, j = sublanes((128, 128)), lanes((128, 128))
    gather_side = jnp.where(((i < 8) & (i // 4 == j)) | ((i >= 120) & ((i - 120) // 4 == j - 126)), 0.0625, 0.0)

    def row_sum(ref, first, count):
        parts = [ref[pl.ds(first + k, count, stride=4), :] for k in range(4)]
        return (parts[0] + parts[1]) + (parts[2] + parts[3])

    def pick(f, c):
        return one.at[f, c] if f < 3 else coef.at[0, c]

    body = [jnp.concatenate([row_sum(pick(f, c), 0, 24) for c in range(4)], axis=1) for f in range(4)]
    side = [row_sum(pick(f, 4), 0, 24) for f in range(4)]
    body = exact_dot(jnp.concatenate(body, axis=0), gather)
    side = exact_dot(jnp.concatenate(side, axis=0), gather_side)
    rough[...] = jnp.zeros(rough.shape, F32)
    rough_two[...] = jnp.zeros(rough_two.shape, F32)
    rough_coef[...] = jnp.zeros(rough_coef.shape, F32)
    for c, value in enumerate((body, side)):
        for f in range(3):
            rough[f, c, 6:30, :] = value[24 * f : 24 * f + 24, :] * FINE_TO_COARSE[f]
        coefficients(rough_coef, c, pl.ds(6, 24), value[72:96, :] * 0.5, COARSE[0])
    coarse_nu[...] = rough_coef[0, 0, 10:26, :]

    def coarse_push(d, c, r):
        return own_push[d, c, r, :]

    for k in range(3):
        advance(rough, rough_two, rough_coef, coarse_push, 0, 9 + 8 * k, 8, 2, (0, 1), COARSE, side_mask)
    clear_rows(rough_two, 2, 9, 26, outside)
    for k in range(2):
        advance(rough_two, rough, rough_coef, coarse_push, 0, 10 + 8 * k, 8, 2, (0,), COARSE, side_mask)
    for f in range(3):
        guess[16 * f : 16 * f + 16, :] = rough[f, 0, 10:26, :]

    def fine_push(d, c, r):
        return push[d, c, r, :]

    for src, dst, first, count, wanted in (
        (one, two, 12, 9, range(5)),
        (two, one, 12, 9, range(5)),
        (one, two, 12, 9, range(5)),
        (two, one, 16, 8, range(4)),
    ):
        for k in range(count):
            advance(src, dst, coef, fine_push, 0, first + 8 * k, 8, 5, wanted, FINE, side_mask)
        if count == 9:
            clear_rows(dst, 5, 15, 80, outside)
    for f in range(3):
        for c in range(4):
            fine[f, :, 128 * c : 128 * c + 128] = one[f, c, 16:80, :] * (1.0 / FINE_SCALE[f])
    ends = [jnp.concatenate([row_sum(one.at[f, c], 16, 16) for c in range(4)], axis=1) for f in range(3)]
    ends = exact_dot(jnp.concatenate(ends, axis=0), gather)
    first_slice = at[0] == 0
    for f in range(3):
        cut = slice(16 * f, 16 * f + 16)
        defect = ends[cut] * FINE_TO_COARSE[f] - jnp.where(first_slice, 0.0, guess[cut, :])
        for m in range(HALF):
            sent[m, cut, :] = defect


def plane_of(held, nu, q):
    return nu[...] if q == NU else held[q // 3, 16 * (q % 3) : 16 * (q % 3) + 16, :]


def cols_kernel(at, held, nu, send_a, send_b):
    even_y = lax.rem(at[2], 2) == 0
    lane = lanes((16, 128))
    for g, members in enumerate(GROUPS):
        left = jnp.zeros((16, 128), F32)
        right = jnp.zeros((16, 128), F32)
        for slot, q in enumerate(members):
            offset = slot * WIDTH
            value = plane_of(held, nu, q)
            mine = (lane >= offset) & (lane < offset + WIDTH)
            left = jnp.where(mine, rolled(value, offset), left)
            right = jnp.where(mine, rolled(value, offset + WIDTH), right)
        send_a[16 * g : 16 * g + 16, :] = jnp.where(even_y, right, left)
        send_b[16 * g : 16 * g + 16, :] = jnp.where(even_y, left, right)


def rows_kernel(at, held, nu, cols_a, cols_b, send_a, send_b):
    even = lax.rem(at[1], 2) == 0

    def put(place, rows, value):
        if rows == 16:
            send_a[place : place + 16, :] = value
            send_b[place : place + 16, :] = value
        else:
            send_a[place : place + 8, :] = jnp.where(even, value[8:16], value[0:8])
            send_b[place : place + 8, :] = jnp.where(even, value[0:8], value[8:16])

    for q, rows in PARTS:
        put(PART_AT[q][0], rows, plane_of(held, nu, q))
    for g, (place, rows) in STRIP_AT.items():
        put(place, rows, cols_a[16 * g : 16 * g + 16, :])
        put(place + rows, rows, cols_b[16 * g : 16 * g + 16, :])


def assemble(at, held, nu, cols_a, cols_b, rows_a, rows_b, put):
    even_x = lax.rem(at[1], 2) == 0
    even_y = lax.rem(at[2], 2) == 0

    def sides(place, rows):
        a, b = rows_a[place : place + rows, :], rows_b[place : place + rows, :]
        return jnp.where(even_x, b, a), jnp.where(even_x, a, b)

    for q in range(NU + 1):
        put(q, 0, 16, plane_of(held, nu, q))
        if q in PART_AT:
            place, rows = PART_AT[q]
            before, after = sides(place, rows)
            put(q, 0, 16 - rows, before)
            put(q, 0, 32, after)
    for g, members in enumerate(GROUPS):
        cut = slice(16 * g, 16 * g + 16)
        blocks = [(16, cols_a[cut, :], cols_b[cut, :])]
        if g in STRIP_AT:
            place, rows = STRIP_AT[g]
            before_a, after_a = sides(place, rows)
            before_b, after_b = sides(place + rows, rows)
            blocks += [(16 - rows, before_a, before_b), (32, after_a, after_b)]
        for first, a, b in blocks:
            lane = lanes(a.shape)
            after, before = jnp.where(even_y, a, b), jnp.where(even_y, b, a)
            for slot, q in enumerate(members):
                if first == 16 or q in PART_AT:
                    hi, lo = rolled(after, -slot * WIDTH), rolled(before, 128 - WIDTH - slot * WIDTH)
                    put(q, 1, first, jnp.where(lane < WIDTH, hi, jnp.where(lane >= 128 - WIDTH, lo, 0.0)))


def putter(extra, coef):
    def put(q, c, row, value):
        rows = pl.ds(row, value.shape[0])
        if q == NU:
            coefficients(coef, c, rows, value, COARSE[0])
        else:
            extra[q, c, rows, :] = value

    return put


def chain(first_k, one, two, coef, push, extra, kept, at):
    outside, side_mask = edges(at)

    for k in range(first_k, HALF):
        def pushed(d, c, r, k=k):
            return push[k, d, c, r, :]

        def keep_and_add(f, c, r, value, k=k):
            if c == 0:
                kept[k, f, r, :] = value
            return value + extra[3 * k + f, c, pl.ds(r.start - 8, r.size), :]

        for half in range(2):
            halo = 2 * (HALF - 1 - k) + 1 - half
            count = 2 + -(-halo // 4)
            first = min(8 + 16 - halo, 8 + EXT - 8 * count)
            src, dst = (one, two) if half == 0 else (two, one)
            post = keep_and_add if half else None
            for i in range(count):
                advance(src, dst, coef, pushed, 8, first + 8 * i, 8, 2, (0, 1), COARSE, side_mask, post=post)
            if halo:
                clear_rows(dst, 2, 8 + 15, 8 + 32, outside)


def low_kernel(at, held, nu, cols_a, cols_b, rows_b, rows_a, push, state, moved, extra, coef, one, two, kept):
    @pl.when(at[0] < HALF)
    def _():
        assemble(at, held, nu, cols_a, cols_b, rows_a, rows_b, putter(extra, coef))
        for f in range(3):
            for c in range(2):
                one[f, c, 8:56, :] = extra[f, c]
        chain(1, one, two, coef, push, extra, kept, at)
        lane = lanes((CROWS, 128))
        sides = jnp.zeros((CROWS, 128), F32)
        for f in range(3):
            state[16 * f : 16 * f + 16, :] = one[f, 0, 24:40, :]
            sides = jnp.where(lane // 32 == f, rolled(one[f, 1, 24:40, :], 16 + 32 * f), sides)
        state[48:64, :] = sides
        for f in range(3):
            moved[16 * f : 16 * f + 16, :] = kept[jnp.maximum(at[0], 1), f, 24:40, :]


def planes_kernel(at, held, nu, cols_a, cols_b, rows_b, rows_a, extra, coef):
    @pl.when(at[0] >= HALF)
    def _():
        assemble(at, held, nu, cols_a, cols_b, rows_a, rows_b, putter(extra, coef))


def high_kernel(at, state, state_a, state_b, extra, coef, push, fine, guess, moved_low, out, one, two, kept, moved, spread):
    even_x = lax.rem(at[1], 2) == 0

    @pl.when(at[0] < HALF)
    def _():
        moved[...] = moved_low[...]

    @pl.when(at[0] >= HALF)
    def _():
        lane = lanes((CROWS, 128))
        a, b = state_a[...], state_b[...]
        for row, block in ((8, jnp.where(even_x, b, a)), (24, state[...]), (40, jnp.where(even_x, a, b))):
            for f in range(3):
                one[f, 0, row : row + 16, :] = block[16 * f : 16 * f + 16]
                side = rolled(block[48:64], -(16 + 32 * f))
                one[f, 1, row : row + 16, :] = jnp.where((lane < 16) | (lane >= 112), side, 0.0)
        chain(0, one, two, coef, push, extra, kept, at)
        for f in range(3):
            moved[16 * f : 16 * f + 16, :] = kept[at[0] - HALF, f, 24:40, :]

    parts = []
    for f in range(3):
        cut = slice(16 * f, 16 * f + 16)
        parts.append(jnp.where(at[0] == 0, 0.0, (moved[cut, :] - guess[cut, :]) * (1.0 / COARSE_SCALE[f])))
    change = jnp.concatenate(parts, axis=0)
    i, j = sublanes((128, COLS)), lanes((128, COLS))
    change = exact_dot(change, jnp.where(i == j // 4, 1.0, 0.0))
    for f in range(3):
        for c in range(4):
            cut = slice(128 * c, 128 * c + 128)
            for k in range(4):
                spread[f, c, pl.ds(k, CROWS, stride=4), :] = change[16 * f : 16 * f + 16, cut]
            out[f, :, cut] = fine[f, :, cut] + spread[f, c]


SMEM = pl.BlockSpec(memory_space=pltpu.SMEM)
VMEM = pl.BlockSpec(memory_space=pltpu.VMEM)
HBM = pl.BlockSpec(memory_space=pltpu.HBM)


def call(kernel, args, outs, scratch=(), far=0, sems=0):
    shapes = [jax.ShapeDtypeStruct(s, F32) for s in outs]
    near = len(args) - 1 - far
    memory = [s if not isinstance(s, tuple) else pltpu.VMEM(s, F32) for s in scratch]
    if sems:
        memory.append(pltpu.SemaphoreType.DMA((sems,)))
    return pl.pallas_call(
        kernel,
        out_shape=shapes,
        in_specs=[SMEM] + [VMEM] * near + [HBM] * far,
        out_specs=[VMEM] * len(shapes),
        scratch_shapes=memory,
        compiler_params=pltpu.CompilerParams(vmem_limit_bytes=48 * 1024 * 1024),
    )(*args)


def swap(x, axis, pairs):
    return lax.ppermute(x, axis, [(a, b) for a, b in pairs] + [(b, a) for a, b in pairs])


def swap_high(x, count, pairs):
    both = [(a, b) for a, b in pairs] + [(b, a) for a, b in pairs]
    return lax.ppermute(x, ("cuts", "sx"), [(n * count + a, n * count + b) for n in range(HALF, CUTS) for a, b in both])


def on_device(starts, viscosity, turbine_x, turbine_y, yaw_index):
    count_x, count_y = lax.axis_size("sx"), lax.axis_size("sy")
    at = jnp.stack([
        lax.axis_index("cuts"), lax.axis_index("sx"), lax.axis_index("sy"),
        jnp.int32(count_x), jnp.int32(count_y),
    ]).astype(jnp.int32)
    start = starts[0]
    x_a = [(i, i + 1) for i in range(0, count_x - 1, 2)]
    x_b = [(i, i + 1) for i in range(1, count_x - 1, 2)]
    y_a = [(i, i + 1) for i in range(0, count_y - 1, 2)]
    y_b = [(i, i + 1) for i in range(1, count_y - 1, 2)]
    turbines = (turbine_x[None, :], turbine_y[None, :], yaw_index)
    turbine_scratch = [pltpu.VMEM((1, 64), jnp.int32), pltpu.VMEM((1, 64), jnp.int32), pltpu.VMEM((CUTS, 64), jnp.int32)]

    odd = at[1] % 2
    rows_b = swap(edge_rows(start, viscosity, 56 * odd), "sx", x_b)
    rows_a = swap(edge_rows(start, viscosity, 56 * (1 - odd)), "sx", x_a)
    own = jnp.concatenate([start, viscosity[None]])
    send_a, send_b = call(side_kernel, (at, own, rows_a, rows_b), [(80, 128)] * 2)
    cols_a = swap(send_a, "sy", y_a)
    cols_b = swap(send_b, "sy", y_b)
    push, own_push = call(
        push_kernel, (at,) + turbines, [(2, 5, 96, 128), (2, 2, 40, 128)], turbine_scratch, far=3, sems=3)
    fine, guess, sent, coarse_nu = call(
        fine_kernel,
        (at, own, rows_a, rows_b, cols_a, cols_b, push, own_push),
        [(3, ROWS, COLS), (48, 128), (HALF, 48, 128), (CROWS, 128)],
        [(3, 5, 96, 128), (3, 5, 96, 128), (4, 5, 96, 128), (3, 2, 40, 128), (3, 2, 40, 128), (4, 2, 40, 128)],
    )
    halves = [list(range(HALF)), list(range(HALF, CUTS))]
    held = lax.all_to_all(sent, "cuts", 0, 0, axis_index_groups=halves)
    send_a, send_b = call(cols_kernel, (at, held, coarse_nu), [(STRIPS, 128)] * 2)
    cols_a = swap(send_a, "sy", y_a)
    cols_b = swap(send_b, "sy", y_b)
    (chain_push,) = call(
        chain_push_kernel, (at,) + turbines, [(HALF, 2, 2, EXT, 128)], turbine_scratch, far=3, sems=3)
    send_a, send_b = call(rows_kernel, (at, held, coarse_nu, cols_a, cols_b), [(MESSAGE, 128)] * 2)
    rows_a = swap(send_a, "sx", x_a)
    rows_b = swap(send_b, "sx", x_b)
    blocks = (at, held, coarse_nu, cols_a, cols_b, rows_b, rows_a)
    field, planes, terms = (3, 2, 64, 128), (3 * HALF, 2, EXT, 128), (4, 2, EXT, 128)
    state, moved = call(
        low_kernel, blocks + (chain_push,), [(64, 128), (48, 128)], [planes, terms, field, field, (HALF, 3, 64, 128)])
    goes = [(m, m + 4 if m >= 4 else m + 12) for m in range(HALF)]
    state_b, state_a = [
        lax.ppermute(state, ("cuts", "sx"), [(m * count_x + i, n * count_x + (i ^ flip)) for m, n in goes for i in range(count_x)])
        for flip in (0, 1)
    ]
    state = state_b
    state_b = swap_high(state, count_x, x_b)
    extra, coef = call(planes_kernel, blocks, [planes, terms])
    (out,) = call(
        high_kernel,
        (at, state, state_a, state_b, extra, coef, chain_push, fine, guess, moved),
        [(3, ROWS, COLS)],
        [field, field, (HALF, 3, 64, 128), (48, 128), (3, 4, ROWS, 128)],
    )
    return out[None]


def solution(mesh):
    in_specs = (P("cuts", None, "sx", "sy"), P("sx", "sy"), P(), P(), P())
    out_specs = P("cuts", None, "sx", "sy")
    return jax.shard_map(
        on_device, mesh=mesh, in_specs=in_specs, out_specs=out_specs, check_vma=False
    )
```

```python
import math

import jax
import jax.numpy as jnp
import numpy as np
from jax import lax
from jax.experimental import pallas as pl
from jax.experimental.pallas import tpu as pltpu
from jax.sharding import PartitionSpec as P

YAWS = 7
CUTS = 16
REACH = 3
F32 = jnp.float32
BF16 = jnp.bfloat16

FINE = (0.3, 0.25, 0.01)
FINE_THRUST = 0.5
FINE_SCALE = (0.25, 0.25, 0.025)
COARSE = (0.15, 0.125, 0.0025)
COARSE_THRUST = 1.0
COARSE_SCALE = (0.125, 0.125, 0.00625)
FINE_TO_COARSE = (0.5, 0.5, 0.25)

ROWS, COLS = 64, 512
CROWS, CCOLS = 16, 128
HALF = CUTS // 2
EXT = 48
NU = 24
ANGLES = [(k - 0.5 * (YAWS - 1)) * (math.pi / 18.0) for k in range(YAWS)]
WEIGHT_X = [float(np.float32(math.cos(t) ** 3)) for t in ANGLES]
WEIGHT_Y = [float(np.float32(math.cos(t) ** 2 * math.sin(t))) for t in ANGLES]

WIDTH = 32
_ORDER = list(range(9)) + [NU, 21, 22] + list(range(9, 21)) + [23]
GROUPS = [_ORDER[_i : _i + 4] for _i in range(0, len(_ORDER), 4)]
STRIPS = 16 * len(GROUPS)
PARTS = [(q, 16) for q in range(0, 9)] + [(q, 8) for q in range(9, 21)] + [(NU, 16)]
PART_AT = {}
_at = 0
for _q, _rows in PARTS:
    PART_AT[_q] = (_at, _rows)
    _at += _rows
STRIP_AT = {}
for _g, _rows in ((0, 16), (1, 16), (2, 16), (3, 8), (4, 8), (5, 8)):
    STRIP_AT[_g] = (_at, _rows)
    _at += 2 * _rows
MESSAGE = _at


def lanes(shape):
    return lax.broadcasted_iota(jnp.int32, shape, len(shape) - 1)


def sublanes(shape):
    return lax.broadcasted_iota(jnp.int32, shape, len(shape) - 2)


def rolled(x, by):
    return pltpu.roll(x, by % 128, 1) if by % 128 else x


def split3(x):
    high = x.astype(BF16)
    rest = x - high.astype(F32)
    middle = rest.astype(BF16)
    return high, middle, (rest - middle.astype(F32)).astype(BF16)


def exact_dot(x, y, dims=(((1,), (0,)), ((), ()))):
    count = x.shape[0]
    stacked = jnp.concatenate(split3(x), axis=0)
    out = lax.dot_general(stacked, y.astype(BF16), dims, preferred_element_type=F32)
    return out[0:count] + (out[count : 2 * count] + out[2 * count : 3 * count])


def advance(src, dst, coef, push, shift, row, count, tiles, wanted, terms, edge, post=None):
    (row_before, row_after), (factor_before, factor_after), side_mask = edge
    _, lift, gain = terms
    lane = lanes((count, 128))
    low, high = lane == 0, lane == 127
    here, east, west = pl.ds(row, count), pl.ds(row + 1, count), pl.ds(row - 1, count)
    there = pl.ds(row - shift, count)
    mid = [[src[f, c, here, :] for c in range(tiles)] for f in range(3)]
    up = [[pltpu.roll(mid[f][c], 127, 1) for c in range(tiles)] for f in range(3)]
    down = [[pltpu.roll(mid[f][c], 1, 1) for c in range(tiles)] for f in range(3)]
    for c in wanted:
        after, before = (c + 1) % tiles, (c - 1) % tiles
        u, v, p = mid[0][c], mid[1][c], mid[2][c]
        un, vn, pn = [jnp.where(high, up[f][after], up[f][c]) for f in range(3)]
        us, vs, ps = [jnp.where(low, down[f][before], down[f][c]) for f in range(3)]
        ue, ve, pe = [src[f, c, east, :] for f in range(3)]
        uw, vw, pw = [src[f, c, west, :] for f in range(3)]
        nu, nu_carry, keep, keep_p = [coef[k, c, there, :] for k in range(4)]
        to_east, to_west = nu - u, nu_carry + u
        lifted = u + lift
        size = jnp.abs(lifted)
        drag = lifted * size / (size + lift)
        new_u = ue * to_east + uw * to_west + nu * (un + us) + keep * u - (pe - pw) - push(0, c, there) * drag
        new_v = ve * to_east + vw * to_west + nu * (vn + vs) + keep * v - (pn - ps) - push(1, c, there) * drag
        new_p = nu * ((pe + pw) + (pn + ps)) + keep_p * p - gain * ((ue - uw) + (vn - vs))
        new = [new_u, new_v, new_p]
        if c == tiles - 1:
            new = [f * side_mask for f in new]
        line = sublanes((count, 128))
        if row <= row_before < row + count:
            inside = jnp.where(line == row_before - row, factor_before, 1.0)
            new = [f * inside for f in new]
        if row <= row_after < row + count:
            inside = jnp.where(line == row_after - row, factor_after, 1.0)
            new = [f * inside for f in new]
        for f in range(3):
            if post is not None:
                new[f] = post(f, c, here, new[f])
            dst[f, c, here, :] = new[f]


def edges(at):
    lane = lanes((8, 128))
    outside = [jnp.where(at[1] > 0, 1.0, 0.0), jnp.where(at[1] < at[3] - 1, 1.0, 0.0)]
    side = jnp.where(lane < 64, jnp.where(at[2] < at[4] - 1, 1.0, 0.0), jnp.where(at[2] > 0, 1.0, 0.0))
    return tuple(outside), side


def coefficients(coef, c, rows, nu, carry):
    coef[0, c, rows, :] = nu
    coef[1, c, rows, :] = nu + carry
    coef[2, c, rows, :] = (1.0 - carry) - 4.0 * nu
    coef[3, c, rows, :] = 1.0 - 4.0 * nu


def yaw_weights(yaw):
    wx = jnp.zeros(yaw.shape, F32)
    wy = jnp.zeros(yaw.shape, F32)
    for k in range(YAWS):
        hit = yaw == k
        wx = jnp.where(hit, WEIGHT_X[k], wx)
        wy = jnp.where(hit, WEIGHT_Y[k], wy)
    return wx, wy


def fetch(pairs, sems):
    copies = [pltpu.make_async_copy(a, b, sems.at[i]) for i, (a, b) in enumerate(pairs)]
    for copy in copies:
        copy.start()
    for copy in copies:
        copy.wait()


def edge_rows(start, visc, first):
    return jnp.concatenate([
        lax.dynamic_slice(start, (0, first, 0), (3, 8, COLS)),
        lax.dynamic_slice(visc, (first, 0), (8, COLS))[None],
    ])


def side_kernel(at, own, got_b, got_a, send_a, send_b):
    even_x = lax.rem(at[1], 2) == 0
    even_y = lax.rem(at[2], 2) == 0
    for r0, count in ((0, 8), (8, 64), (72, 8)):
        lane = lanes((count, 128))
        left = jnp.zeros((count, 128), F32)
        right = jnp.zeros((count, 128), F32)
        for f in range(4):
            if r0 == 8:
                a, b = own[f, :, 0:128], own[f, :, COLS - 128 : COLS]
            else:
                from_a = jnp.logical_xor(even_x, r0 == 0)
                a = jnp.where(from_a, got_a[f, :, 0:128], got_b[f, :, 0:128])
                b = jnp.where(from_a, got_a[f, :, COLS - 128 : COLS], got_b[f, :, COLS - 128 : COLS])
            mine = (lane >= 8 * f) & (lane < 8 * f + 8)
            left = jnp.where(mine, rolled(a, 8 * f), left)
            right = jnp.where(mine, rolled(b, 8 * f + 8), right)
        send_a[r0 : r0 + count, :] = jnp.where(even_y, right, left)
        send_b[r0 : r0 + count, :] = jnp.where(even_y, left, right)


def fine_cols(sy, c, shape):
    i = sublanes(shape)
    return sy * COLS + (128 * c + i if c < 4 else jnp.where(i < 64, COLS + i, i - 128))


def coarse_cols(sy, c, ty):
    i = sublanes((128, 64))
    col = sy * CCOLS + (i if c == 0 else jnp.where(i < 64, CCOLS + i, i - 128))
    hit = jnp.zeros((128, 64), F32)
    for offset in range(4):
        hit = hit + jnp.where(jnp.abs(4 * col + offset - ty) <= REACH, 0.25, 0.0)
    return hit


LAST_DIMS = (((1,), (1,)), ((), ()))


def push_kernel(at, tx_in, ty_in, yaw_in, fine_push, own_push, tx_ref, ty_ref, yaw_ref, sems):
    fetch([(tx_in, tx_ref), (ty_in, ty_ref), (yaw_in, yaw_ref)], sems)
    tx, ty = tx_ref[...], ty_ref[...]
    mine = sublanes((CUTS, 64)) == at[0]
    wx, wy = yaw_weights(jnp.sum(jnp.where(mine, yaw_ref[...], 0), axis=0, keepdims=True))
    row = at[1] * ROWS - 16 + sublanes((96, 64))
    hit = jnp.where(row == tx, FINE_THRUST, 0.0)
    both = jnp.concatenate([hit * wx, hit * wy], axis=0)
    for c in range(5):
        cols = jnp.where(jnp.abs(fine_cols(at[2], c, (128, 64)) - ty) <= REACH, 1.0, 0.0)
        push = exact_dot(both, cols, LAST_DIMS)
        fine_push[0, c] = push[0:96]
        fine_push[1, c] = push[96:192]
    row = at[1] * CROWS - 10 + sublanes((40, 64))
    hit = jnp.where(row == tx // 4, 0.25 * COARSE_THRUST, 0.0)
    both = jnp.concatenate([hit * wx, hit * wy], axis=0)
    for c in range(2):
        push = exact_dot(both, coarse_cols(at[2], c, ty), LAST_DIMS)
        own_push[0, c] = push[0:40]
        own_push[1, c] = push[40:80]


def chain_push_kernel(at, tx_in, ty_in, yaw_in, push, tx_ref, ty_ref, yaw_ref, sems):
    fetch([(tx_in, tx_ref), (ty_in, ty_ref), (yaw_in, yaw_ref)], sems)
    tx, ty = tx_ref[...], ty_ref[...]
    row = at[1] * CROWS - 16 + sublanes((EXT, 64))
    hit = jnp.where(row == tx // 4, 0.25 * COARSE_THRUST, 0.0)
    wx, wy = yaw_weights(yaw_ref[pl.ds(pl.multiple_of(at[0] // HALF * HALF, HALF), HALF), :])
    cols = [coarse_cols(at[2], c, ty) for c in range(2)]
    for k in range(HALF):
        both = jnp.concatenate([hit * wx[k : k + 1, :], hit * wy[k : k + 1, :]], axis=0)
        for c in range(2):
            value = exact_dot(both, cols[c], LAST_DIMS)
            push[k, 0, c] = value[0:EXT]
            push[k, 1, c] = value[EXT : 2 * EXT]


def fine_kernel(at, own, rows_a, rows_b, cols_a, cols_b, push, own_push, fine, guess, sent, coarse_nu,
                one, two, coef, rough, rough_two, rough_coef):
    even_x = lax.rem(at[1], 2) == 0
    even_y = lax.rem(at[2], 2) == 0
    outside, side_mask = edges(at)
    fine_edge, rough_edge = ((15, 80), outside, side_mask), ((9, 26), outside, side_mask)
    after_all = jnp.where(even_y, cols_a[...], cols_b[...])
    before_all = jnp.where(even_y, cols_b[...], cols_a[...])
    lane = lanes((80, 128))
    for f in range(4):
        for c in range(5):
            if c < 4:
                cut = slice(128 * c, 128 * c + 128)
                a, b = rows_a[f, :, cut], rows_b[f, :, cut]
                pieces = [(8, 8, jnp.where(even_x, b, a)), (16, 64, own[f, :, cut]), (80, 8, jnp.where(even_x, a, b))]
            else:
                after, before = rolled(after_all, -8 * f), rolled(before_all, 120 - 8 * f)
                pieces = [(8, 80, jnp.where(lane < 8, after, jnp.where(lane >= 120, before, 0.0)))]
            for r, count, value in pieces:
                if f < 3:
                    one[f, c, r : r + count, :] = value * FINE_SCALE[f]
                else:
                    coefficients(coef, c, pl.ds(r, count), value, FINE[0])

    i, j = sublanes((COLS, 128)), lanes((COLS, 128))
    gather = jnp.where(i // 4 == j, 0.0625, 0.0)
    i, j = sublanes((128, 128)), lanes((128, 128))
    gather_side = jnp.where(((i < 8) & (i // 4 == j)) | ((i >= 120) & ((i - 120) // 4 == j - 126)), 0.0625, 0.0)

    def row_sum(ref, first, count):
        parts = [ref[pl.ds(first + k, count, stride=4), :] for k in range(4)]
        return (parts[0] + parts[1]) + (parts[2] + parts[3])

    def pick(f, c):
        return one.at[f, c] if f < 3 else coef.at[0, c]

    body = [jnp.concatenate([row_sum(pick(f, c), 0, 24) for c in range(4)], axis=1) for f in range(4)]
    side = [row_sum(pick(f, 4), 0, 24) for f in range(4)]
    body = exact_dot(jnp.concatenate(body, axis=0), gather)
    side = exact_dot(jnp.concatenate(side, axis=0), gather_side)
    rough[...] = jnp.zeros(rough.shape, F32)
    rough_two[...] = jnp.zeros(rough_two.shape, F32)
    rough_coef[...] = jnp.zeros(rough_coef.shape, F32)
    for c, value in enumerate((body, side)):
        for f in range(3):
            rough[f, c, 6:30, :] = value[24 * f : 24 * f + 24, :] * FINE_TO_COARSE[f]
        coefficients(rough_coef, c, pl.ds(6, 24), value[72:96, :] * 0.5, COARSE[0])
    coarse_nu[...] = rough_coef[0, 0, 10:26, :]

    def coarse_push(d, c, r):
        return own_push[d, c, r, :]

    for k in range(3):
        advance(rough, rough_two, rough_coef, coarse_push, 0, 9 + 8 * k, 8, 2, (0, 1), COARSE, rough_edge)
    for k in range(2):
        advance(rough_two, rough, rough_coef, coarse_push, 0, 10 + 8 * k, 8, 2, (0,), COARSE, rough_edge)
    for f in range(3):
        guess[16 * f : 16 * f + 16, :] = rough[f, 0, 10:26, :]

    def fine_push(d, c, r):
        return push[d, c, r, :]

    for src, dst, first, count, wanted in (
        (one, two, 12, 9, range(5)),
        (two, one, 12, 9, range(5)),
        (one, two, 12, 9, range(5)),
        (two, one, 16, 8, range(4)),
    ):
        for k in range(count):
            advance(src, dst, coef, fine_push, 0, first + 8 * k, 8, 5, wanted, FINE, fine_edge)
    for f in range(3):
        for c in range(4):
            fine[f, :, 128 * c : 128 * c + 128] = one[f, c, 16:80, :] * (1.0 / FINE_SCALE[f])
    ends = [jnp.concatenate([row_sum(one.at[f, c], 16, 16) for c in range(4)], axis=1) for f in range(3)]
    ends = exact_dot(jnp.concatenate(ends, axis=0), gather)
    first_slice = at[0] == 0
    for f in range(3):
        cut = slice(16 * f, 16 * f + 16)
        defect = ends[cut] * FINE_TO_COARSE[f] - jnp.where(first_slice, 0.0, guess[cut, :])
        for m in range(HALF):
            sent[m, cut, :] = defect


def plane_of(held, nu, q):
    return nu[...] if q == NU else held[q // 3, 16 * (q % 3) : 16 * (q % 3) + 16, :]


def cols_kernel(at, held, nu, send_a, send_b):
    even_y = lax.rem(at[2], 2) == 0
    lane = lanes((16, 128))
    for g, members in enumerate(GROUPS):
        left = jnp.zeros((16, 128), F32)
        right = jnp.zeros((16, 128), F32)
        for slot, q in enumerate(members):
            offset = slot * WIDTH
            value = plane_of(held, nu, q)
            mine = (lane >= offset) & (lane < offset + WIDTH)
            left = jnp.where(mine, rolled(value, offset), left)
            right = jnp.where(mine, rolled(value, offset + WIDTH), right)
        send_a[16 * g : 16 * g + 16, :] = jnp.where(even_y, right, left)
        send_b[16 * g : 16 * g + 16, :] = jnp.where(even_y, left, right)


def rows_kernel(at, held, nu, cols_a, cols_b, send_a, send_b):
    even = lax.rem(at[1], 2) == 0

    def put(place, rows, value):
        if rows == 16:
            send_a[place : place + 16, :] = value
            send_b[place : place + 16, :] = value
        else:
            send_a[place : place + 8, :] = jnp.where(even, value[8:16], value[0:8])
            send_b[place : place + 8, :] = jnp.where(even, value[0:8], value[8:16])

    for q, rows in PARTS:
        put(PART_AT[q][0], rows, plane_of(held, nu, q))
    for g, (place, rows) in STRIP_AT.items():
        put(place, rows, cols_a[16 * g : 16 * g + 16, :])
        put(place + rows, rows, cols_b[16 * g : 16 * g + 16, :])


def assemble(at, held, nu, cols_a, cols_b, rows_a, rows_b, put):
    even_x = lax.rem(at[1], 2) == 0
    even_y = lax.rem(at[2], 2) == 0

    def sides(place, rows):
        a, b = rows_a[place : place + rows, :], rows_b[place : place + rows, :]
        return jnp.where(even_x, b, a), jnp.where(even_x, a, b)

    for q in range(NU + 1):
        put(q, 0, 16, plane_of(held, nu, q))
        if q in PART_AT:
            place, rows = PART_AT[q]
            before, after = sides(place, rows)
            put(q, 0, 16 - rows, before)
            put(q, 0, 32, after)
    for g, members in enumerate(GROUPS):
        cut = slice(16 * g, 16 * g + 16)
        blocks = [(16, cols_a[cut, :], cols_b[cut, :])]
        if g in STRIP_AT:
            place, rows = STRIP_AT[g]
            before_a, after_a = sides(place, rows)
            before_b, after_b = sides(place + rows, rows)
            blocks += [(16 - rows, before_a, before_b), (32, after_a, after_b)]
        for first, a, b in blocks:
            lane = lanes(a.shape)
            after, before = jnp.where(even_y, a, b), jnp.where(even_y, b, a)
            for slot, q in enumerate(members):
                if first == 16 or q in PART_AT:
                    hi, lo = rolled(after, -slot * WIDTH), rolled(before, 128 - WIDTH - slot * WIDTH)
                    put(q, 1, first, jnp.where(lane < WIDTH, hi, jnp.where(lane >= 128 - WIDTH, lo, 0.0)))


def putter(extra, coef):
    def put(q, c, row, value):
        rows = pl.ds(row, value.shape[0])
        if q == NU:
            coefficients(coef, c, rows, value, COARSE[0])
        else:
            extra[q, c, rows, :] = value

    return put


def chain(first_k, one, two, coef, push, extra, kept, at):
    edge = ((8 + 15, 8 + 32),) + edges(at)

    for k in range(first_k, HALF):
        def pushed(d, c, r, k=k):
            return push[k, d, c, r, :]

        def keep_and_add(f, c, r, value, k=k):
            if c == 0:
                kept[k, f, r, :] = value
            return value + extra[3 * k + f, c, pl.ds(r.start - 8, r.size), :]

        for half in range(2):
            halo = 2 * (HALF - 1 - k) + 1 - half
            count = 2 + -(-halo // 4)
            first = min(8 + 16 - halo, 8 + EXT - 8 * count)
            src, dst = (one, two) if half == 0 else (two, one)
            post = keep_and_add if half else None
            for i in range(count):
                advance(src, dst, coef, pushed, 8, first + 8 * i, 8, 2, (0, 1), COARSE, edge, post=post)


def low_kernel(at, held, nu, cols_a, cols_b, rows_b, rows_a, push, state, moved, extra, coef, one, two, kept):
    @pl.when(at[0] < HALF)
    def _():
        assemble(at, held, nu, cols_a, cols_b, rows_a, rows_b, putter(extra, coef))
        for f in range(3):
            for c in range(2):
                one[f, c, 8:56, :] = extra[f, c]
        chain(1, one, two, coef, push, extra, kept, at)
        lane = lanes((CROWS, 128))
        sides = jnp.zeros((CROWS, 128), F32)
        for f in range(3):
            state[16 * f : 16 * f + 16, :] = one[f, 0, 24:40, :]
            sides = jnp.where(lane // 32 == f, rolled(one[f, 1, 24:40, :], 16 + 32 * f), sides)
        state[48:64, :] = sides
        for f in range(3):
            moved[16 * f : 16 * f + 16, :] = kept[jnp.maximum(at[0], 1), f, 24:40, :]


def planes_kernel(at, held, nu, cols_a, cols_b, rows_b, rows_a, extra, coef):
    @pl.when(at[0] >= HALF)
    def _():
        assemble(at, held, nu, cols_a, cols_b, rows_a, rows_b, putter(extra, coef))


def high_kernel(at, state, state_a, state_b, extra, coef, push, fine, guess, moved_low, out, one, two, kept, moved, spread, result, sems):
    even_x = lax.rem(at[1], 2) == 0

    @pl.when(at[0] < HALF)
    def _():
        moved[...] = moved_low[...]

    @pl.when(at[0] >= HALF)
    def _():
        lane = lanes((CROWS, 128))
        a, b = state_a[...], state_b[...]
        for row, block in ((8, jnp.where(even_x, b, a)), (24, state[...]), (40, jnp.where(even_x, a, b))):
            for f in range(3):
                one[f, 0, row : row + 16, :] = block[16 * f : 16 * f + 16]
                side = rolled(block[48:64], -(16 + 32 * f))
                one[f, 1, row : row + 16, :] = jnp.where((lane < 16) | (lane >= 112), side, 0.0)
        chain(0, one, two, coef, push, extra, kept, at)
        for f in range(3):
            moved[16 * f : 16 * f + 16, :] = kept[at[0] - HALF, f, 24:40, :]

    parts = []
    for f in range(3):
        cut = slice(16 * f, 16 * f + 16)
        parts.append(jnp.where(at[0] == 0, 0.0, (moved[cut, :] - guess[cut, :]) * (1.0 / COARSE_SCALE[f])))
    change = jnp.concatenate(parts, axis=0)
    i, j = sublanes((128, COLS)), lanes((128, COLS))
    change = exact_dot(change, jnp.where(i == j // 4, 1.0, 0.0))
    copies = []
    for f in range(3):
        for c in range(4):
            cut = slice(128 * c, 128 * c + 128)
            for k in range(4):
                spread[f, c, pl.ds(k, CROWS, stride=4), :] = change[16 * f : 16 * f + 16, cut]
            result[f, :, cut] = fine[f, :, cut] + spread[f, c]
        copies.append(pltpu.make_async_copy(result.at[f], out.at[f], sems.at[f]))
        copies[f].start()
    for copy in copies:
        copy.wait()


def place():
    return (*[lax.axis_index(a) for a in ("cuts", "sx", "sy")], lax.axis_size("sx"), lax.axis_size("sy"))


VMEM = pl.BlockSpec(memory_space=pltpu.VMEM)
HBM = pl.BlockSpec(memory_space=pltpu.HBM)


def call(kernel, args, outs, scratch=(), far=0, sems=0, away=False):
    shapes = [jax.ShapeDtypeStruct(s, F32) for s in outs]
    near = len(args) - far
    memory = [s if not isinstance(s, tuple) else pltpu.VMEM(s, F32) for s in scratch]
    if sems:
        memory.append(pltpu.SemaphoreType.DMA((sems,)))

    def placed(*refs):
        kernel(place(), *refs)

    return pl.pallas_call(
        placed,
        out_shape=shapes,
        in_specs=[VMEM] * near + [HBM] * far,
        out_specs=[HBM if away else VMEM] * len(shapes),
        scratch_shapes=memory,
        compiler_params=pltpu.CompilerParams(vmem_limit_bytes=48 * 1024 * 1024),
    )(*args)


def swap(x, axis, pairs):
    return lax.ppermute(x, axis, [(a, b) for a, b in pairs] + [(b, a) for a, b in pairs])


def swap_half(x, count, pairs, cuts):
    both = [(a, b) for a, b in pairs] + [(b, a) for a, b in pairs]
    return lax.ppermute(x, ("cuts", "sx"), [(n * count + a, n * count + b) for n in cuts for a, b in both])


def on_device(starts, viscosity, turbine_x, turbine_y, yaw_index):
    count_x, count_y = lax.axis_size("sx"), lax.axis_size("sy")
    at = place()
    start = starts[0]
    x_a = [(i, i + 1) for i in range(0, count_x - 1, 2)]
    x_b = [(i, i + 1) for i in range(1, count_x - 1, 2)]
    y_a = [(i, i + 1) for i in range(0, count_y - 1, 2)]
    y_b = [(i, i + 1) for i in range(1, count_y - 1, 2)]
    turbines = (turbine_x[None, :], turbine_y[None, :], yaw_index)
    turbine_scratch = [pltpu.VMEM((1, 64), jnp.int32), pltpu.VMEM((1, 64), jnp.int32), pltpu.VMEM((CUTS, 64), jnp.int32)]

    odd = at[1] % 2
    rows_b = swap(edge_rows(start, viscosity, 56 * odd), "sx", x_b)
    rows_a = swap(edge_rows(start, viscosity, 56 * (1 - odd)), "sx", x_a)
    own = jnp.concatenate([start, viscosity[None]])
    send_a, send_b = call(side_kernel, (own, rows_b, rows_a), [(80, 128)] * 2)
    cols_a = swap(send_a, "sy", y_a)
    cols_b = swap(send_b, "sy", y_b)
    push, own_push = call(
        push_kernel, turbines, [(2, 5, 96, 128), (2, 2, 40, 128)], turbine_scratch, far=3, sems=3)
    fine, guess, sent, coarse_nu = call(
        fine_kernel,
        (own, rows_a, rows_b, cols_a, cols_b, push, own_push),
        [(3, ROWS, COLS), (48, 128), (HALF, 48, 128), (CROWS, 128)],
        [(3, 5, 96, 128), (3, 5, 96, 128), (4, 5, 96, 128), (3, 2, 40, 128), (3, 2, 40, 128), (4, 2, 40, 128)],
    )
    halves = [list(range(HALF)), list(range(HALF, CUTS))]
    held = lax.all_to_all(sent, "cuts", 0, 0, axis_index_groups=halves)
    send_a, send_b = call(cols_kernel, (held, coarse_nu), [(STRIPS, 128)] * 2)
    cols_a = swap(send_a, "sy", y_a)
    cols_b = swap(send_b, "sy", y_b)
    (chain_push,) = call(
        chain_push_kernel, turbines, [(HALF, 2, 2, EXT, 128)], turbine_scratch, far=3, sems=3)
    send_a, send_b = call(rows_kernel, (held, coarse_nu, cols_a, cols_b), [(MESSAGE, 128)] * 2)
    low, high = range(HALF), range(HALF, CUTS)
    rows_a = swap(send_a, "sx", x_a)
    rows_b = swap(send_b, "sx", x_b)
    blocks = (held, coarse_nu, cols_a, cols_b, rows_b, rows_a)
    field, planes, terms = (3, 2, 64, 128), (3 * HALF, 2, EXT, 128), (4, 2, EXT, 128)
    state, moved = call(
        low_kernel, blocks + (chain_push,), [(64, 128), (48, 128)], [planes, terms, field, field, (HALF, 3, 64, 128)])
    goes = [(m, m + 4 if m >= 4 else m + 12) for m in low]
    state_b, state_a = [
        lax.ppermute(state, ("cuts", "sx"), [(m * count_x + i, n * count_x + (i ^ flip)) for m, n in goes for i in range(count_x)])
        for flip in (0, 1)
    ]
    extra, coef = call(planes_kernel, (held, coarse_nu, cols_a, cols_b, rows_b, rows_a), [planes, terms])
    state = state_b
    state_b = swap_half(state, count_x, x_b, high)
    (out,) = call(
        high_kernel,
        (state, state_a, state_b, extra, coef, chain_push, fine, guess, moved),
        [(3, ROWS, COLS)],
        [field, field, (HALF, 3, 64, 128), (48, 128), (3, 4, ROWS, 128), (3, ROWS, COLS)],
        sems=3, away=True,
    )
    return out[None]


def solution(mesh):
    in_specs = (P("cuts", None, "sx", "sy"), P("sx", "sy"), P(), P(), P())
    out_specs = P("cuts", None, "sx", "sy")
    return jax.shard_map(
        on_device, mesh=mesh, in_specs=in_specs, out_specs=out_specs, check_vma=False
    )
```

```python
import math

import jax
import jax.numpy as jnp
import numpy as np
from jax import lax
from jax.experimental import pallas as pl
from jax.experimental.pallas import tpu as pltpu
from jax.sharding import PartitionSpec as P

YAWS = 7
CUTS = 16
REACH = 3
F32 = jnp.float32
BF16 = jnp.bfloat16

FINE = (0.3, 0.25, 0.01)
FINE_THRUST = 0.5
FINE_SCALE = (0.25, 0.25, 0.025)
COARSE = (0.15, 0.125, 0.0025)
COARSE_THRUST = 1.0
COARSE_SCALE = (0.125, 0.125, 0.00625)
FINE_TO_COARSE = (0.5, 0.5, 0.25)

ROWS, COLS = 64, 512
CROWS, CCOLS = 16, 128
HALF = CUTS // 2
EXT = 48
NU = 24
ANGLES = [(k - 0.5 * (YAWS - 1)) * (math.pi / 18.0) for k in range(YAWS)]
WEIGHT_X = [float(np.float32(math.cos(t) ** 3)) for t in ANGLES]
WEIGHT_Y = [float(np.float32(math.cos(t) ** 2 * math.sin(t))) for t in ANGLES]

WIDTH = 32
_ORDER = list(range(9)) + [NU, 21, 22] + list(range(9, 21)) + [23]
GROUPS = [_ORDER[_i : _i + 4] for _i in range(0, len(_ORDER), 4)]
STRIPS = 16 * len(GROUPS)
PARTS = [(q, 16) for q in range(0, 9)] + [(q, 8) for q in range(9, 21)] + [(NU, 16)]
PART_AT = {}
_at = 0
for _q, _rows in PARTS:
    PART_AT[_q] = (_at, _rows)
    _at += _rows
STRIP_AT = {}
for _g, _rows in ((0, 16), (1, 16), (2, 16), (3, 8), (4, 8), (5, 8)):
    STRIP_AT[_g] = (_at, _rows)
    _at += 2 * _rows
MESSAGE = _at


def lanes(shape):
    return lax.broadcasted_iota(jnp.int32, shape, len(shape) - 1)


def sublanes(shape):
    return lax.broadcasted_iota(jnp.int32, shape, len(shape) - 2)


def rolled(x, by):
    return pltpu.roll(x, by % 128, 1) if by % 128 else x


def split3(x):
    high = x.astype(BF16)
    rest = x - high.astype(F32)
    middle = rest.astype(BF16)
    return high, middle, (rest - middle.astype(F32)).astype(BF16)


def exact_dot(x, y, dims=(((1,), (0,)), ((), ()))):
    count = x.shape[0]
    stacked = jnp.concatenate(split3(x), axis=0)
    out = lax.dot_general(stacked, y.astype(BF16), dims, preferred_element_type=F32)
    return out[0:count] + (out[count : 2 * count] + out[2 * count : 3 * count])


def advance(src, dst, coef, push, shift, row, count, tiles, wanted, terms, edge, post=None):
    (row_before, row_after), (factor_before, factor_after), side_mask = edge
    _, lift, gain = terms
    lane = lanes((count, 128))
    low, high = lane == 0, lane == 127
    here, east, west = pl.ds(row, count), pl.ds(row + 1, count), pl.ds(row - 1, count)
    there = pl.ds(row - shift, count)
    mid = [[src[f, c, here, :] for c in range(tiles)] for f in range(3)]
    up = [[pltpu.roll(mid[f][c], 127, 1) for c in range(tiles)] for f in range(3)]
    down = [[pltpu.roll(mid[f][c], 1, 1) for c in range(tiles)] for f in range(3)]
    for c in wanted:
        after, before = (c + 1) % tiles, (c - 1) % tiles
        u, v, p = mid[0][c], mid[1][c], mid[2][c]
        un, vn, pn = [jnp.where(high, up[f][after], up[f][c]) for f in range(3)]
        us, vs, ps = [jnp.where(low, down[f][before], down[f][c]) for f in range(3)]
        ue, ve, pe = [src[f, c, east, :] for f in range(3)]
        uw, vw, pw = [src[f, c, west, :] for f in range(3)]
        nu, nu_carry, keep, keep_p = [coef[k, c, there, :] for k in range(4)]
        to_east, to_west = nu - u, nu_carry + u
        lifted = u + lift
        size = jnp.abs(lifted)
        drag = lifted * size / (size + lift)
        new_u = ue * to_east + uw * to_west + nu * (un + us) + keep * u - (pe - pw) - push(0, c, there) * drag
        new_v = ve * to_east + vw * to_west + nu * (vn + vs) + keep * v - (pn - ps) - push(1, c, there) * drag
        new_p = nu * ((pe + pw) + (pn + ps)) + keep_p * p - gain * ((ue - uw) + (vn - vs))
        new = [new_u, new_v, new_p]
        if c == tiles - 1:
            new = [f * side_mask for f in new]
        line = sublanes((count, 128))
        if row <= row_before < row + count:
            inside = jnp.where(line == row_before - row, factor_before, 1.0)
            new = [f * inside for f in new]
        if row <= row_after < row + count:
            inside = jnp.where(line == row_after - row, factor_after, 1.0)
            new = [f * inside for f in new]
        for f in range(3):
            if post is not None:
                new[f] = post(f, c, here, new[f])
            dst[f, c, here, :] = new[f]


def edges(at):
    lane = lanes((8, 128))
    outside = [jnp.where(at[1] > 0, 1.0, 0.0), jnp.where(at[1] < at[3] - 1, 1.0, 0.0)]
    side = jnp.where(lane < 64, jnp.where(at[2] < at[4] - 1, 1.0, 0.0), jnp.where(at[2] > 0, 1.0, 0.0))
    return tuple(outside), side


def coefficients(coef, c, rows, nu, carry):
    coef[0, c, rows, :] = nu
    coef[1, c, rows, :] = nu + carry
    coef[2, c, rows, :] = (1.0 - carry) - 4.0 * nu
    coef[3, c, rows, :] = 1.0 - 4.0 * nu


def yaw_weights(yaw):
    wx = jnp.zeros(yaw.shape, F32)
    wy = jnp.zeros(yaw.shape, F32)
    for k in range(YAWS):
        hit = yaw == k
        wx = jnp.where(hit, WEIGHT_X[k], wx)
        wy = jnp.where(hit, WEIGHT_Y[k], wy)
    return wx, wy


def fetch(pairs, sems):
    copies = [pltpu.make_async_copy(a, b, sems.at[i]) for i, (a, b) in enumerate(pairs)]
    for copy in copies:
        copy.start()
    for copy in copies:
        copy.wait()


def edge_kernel(at, own, send_b, send_a):
    even = lax.rem(at[1], 2) == 0
    for f in range(4):
        first, last = own[f, 0:8, :], own[f, ROWS - 8 : ROWS, :]
        send_a[f] = jnp.where(even, last, first)
        send_b[f] = jnp.where(even, first, last)


def side_kernel(at, own, got_b, got_a, send_a, send_b):
    even_x = lax.rem(at[1], 2) == 0
    even_y = lax.rem(at[2], 2) == 0
    for r0, count in ((0, 8), (8, 64), (72, 8)):
        lane = lanes((count, 128))
        left = jnp.zeros((count, 128), F32)
        right = jnp.zeros((count, 128), F32)
        for f in range(4):
            if r0 == 8:
                a, b = own[f, :, 0:128], own[f, :, COLS - 128 : COLS]
            else:
                from_a = jnp.logical_xor(even_x, r0 == 0)
                a = jnp.where(from_a, got_a[f, :, 0:128], got_b[f, :, 0:128])
                b = jnp.where(from_a, got_a[f, :, COLS - 128 : COLS], got_b[f, :, COLS - 128 : COLS])
            mine = (lane >= 8 * f) & (lane < 8 * f + 8)
            left = jnp.where(mine, rolled(a, 8 * f), left)
            right = jnp.where(mine, rolled(b, 8 * f + 8), right)
        send_a[r0 : r0 + count, :] = jnp.where(even_y, right, left)
        send_b[r0 : r0 + count, :] = jnp.where(even_y, left, right)


def fine_cols(sy, c, shape):
    i = sublanes(shape)
    return sy * COLS + (128 * c + i if c < 4 else jnp.where(i < 64, COLS + i, i - 128))


def coarse_cols(sy, c, ty):
    i = sublanes((128, 64))
    col = sy * CCOLS + (i if c == 0 else jnp.where(i < 64, CCOLS + i, i - 128))
    hit = jnp.zeros((128, 64), F32)
    for offset in range(4):
        hit = hit + jnp.where(jnp.abs(4 * col + offset - ty) <= REACH, 0.25, 0.0)
    return hit


LAST_DIMS = (((1,), (1,)), ((), ()))


def push_kernel(at, tx_in, ty_in, yaw_in, fine_push, own_push, tx_ref, ty_ref, yaw_ref, sems):
    fetch([(tx_in, tx_ref), (ty_in, ty_ref), (yaw_in, yaw_ref)], sems)
    tx, ty = tx_ref[...], ty_ref[...]
    mine = sublanes((CUTS, 64)) == at[0]
    wx, wy = yaw_weights(jnp.sum(jnp.where(mine, yaw_ref[...], 0), axis=0, keepdims=True))
    row = at[1] * ROWS - 16 + sublanes((96, 64))
    hit = jnp.where(row == tx, FINE_THRUST, 0.0)
    both = jnp.concatenate([hit * wx, hit * wy], axis=0)
    for c in range(5):
        cols = jnp.where(jnp.abs(fine_cols(at[2], c, (128, 64)) - ty) <= REACH, 1.0, 0.0)
        push = exact_dot(both, cols, LAST_DIMS)
        fine_push[0, c] = push[0:96]
        fine_push[1, c] = push[96:192]
    row = at[1] * CROWS - 10 + sublanes((40, 64))
    hit = jnp.where(row == tx // 4, 0.25 * COARSE_THRUST, 0.0)
    both = jnp.concatenate([hit * wx, hit * wy], axis=0)
    for c in range(2):
        push = exact_dot(both, coarse_cols(at[2], c, ty), LAST_DIMS)
        own_push[0, c] = push[0:40]
        own_push[1, c] = push[40:80]


def chain_push_kernel(at, tx_in, ty_in, yaw_in, push, tx_ref, ty_ref, yaw_ref, sems):
    fetch([(tx_in, tx_ref), (ty_in, ty_ref), (yaw_in, yaw_ref)], sems)
    tx, ty = tx_ref[...], ty_ref[...]
    row = at[1] * CROWS - 16 + sublanes((EXT, 64))
    hit = jnp.where(row == tx // 4, 0.25 * COARSE_THRUST, 0.0)
    wx, wy = yaw_weights(yaw_ref[pl.ds(pl.multiple_of(at[0] // HALF * HALF, HALF), HALF), :])
    cols = [coarse_cols(at[2], c, ty) for c in range(2)]
    for k in range(HALF):
        both = jnp.concatenate([hit * wx[k : k + 1, :], hit * wy[k : k + 1, :]], axis=0)
        for c in range(2):
            value = exact_dot(both, cols[c], LAST_DIMS)
            push[k, 0, c] = value[0:EXT]
            push[k, 1, c] = value[EXT : 2 * EXT]


def fine_kernel(at, own, rows_b, rows_a, cols_a, cols_b, push, own_push, fine, guess, sent, coarse_nu,
                one, two, coef, rough, rough_two, rough_coef):
    even_x = lax.rem(at[1], 2) == 0
    even_y = lax.rem(at[2], 2) == 0
    outside, side_mask = edges(at)
    fine_edge, rough_edge = ((15, 80), outside, side_mask), ((9, 26), outside, side_mask)
    after_all = jnp.where(even_y, cols_a[...], cols_b[...])
    before_all = jnp.where(even_y, cols_b[...], cols_a[...])
    lane = lanes((80, 128))
    for f in range(4):
        for c in range(5):
            if c < 4:
                cut = slice(128 * c, 128 * c + 128)
                a, b = rows_a[f, :, cut], rows_b[f, :, cut]
                pieces = [(8, 8, jnp.where(even_x, b, a)), (16, 64, own[f, :, cut]), (80, 8, jnp.where(even_x, a, b))]
            else:
                after, before = rolled(after_all, -8 * f), rolled(before_all, 120 - 8 * f)
                pieces = [(8, 80, jnp.where(lane < 8, after, jnp.where(lane >= 120, before, 0.0)))]
            for r, count, value in pieces:
                if f < 3:
                    one[f, c, r : r + count, :] = value * FINE_SCALE[f]
                else:
                    coefficients(coef, c, pl.ds(r, count), value, FINE[0])

    i, j = sublanes((COLS, 128)), lanes((COLS, 128))
    gather = jnp.where(i // 4 == j, 0.0625, 0.0)
    i, j = sublanes((128, 128)), lanes((128, 128))
    gather_side = jnp.where(((i < 8) & (i // 4 == j)) | ((i >= 120) & ((i - 120) // 4 == j - 126)), 0.0625, 0.0)

    def row_sum(ref, first, count):
        parts = [ref[pl.ds(first + k, count, stride=4), :] for k in range(4)]
        return (parts[0] + parts[1]) + (parts[2] + parts[3])

    def pick(f, c):
        return one.at[f, c] if f < 3 else coef.at[0, c]

    body = [jnp.concatenate([row_sum(pick(f, c), 0, 24) for c in range(4)], axis=1) for f in range(4)]
    side = [row_sum(pick(f, 4), 0, 24) for f in range(4)]
    body = exact_dot(jnp.concatenate(body, axis=0), gather)
    side = exact_dot(jnp.concatenate(side, axis=0), gather_side)
    rough[...] = jnp.zeros(rough.shape, F32)
    rough_two[...] = jnp.zeros(rough_two.shape, F32)
    rough_coef[...] = jnp.zeros(rough_coef.shape, F32)
    for c, value in enumerate((body, side)):
        for f in range(3):
            rough[f, c, 6:30, :] = value[24 * f : 24 * f + 24, :] * FINE_TO_COARSE[f]
        coefficients(rough_coef, c, pl.ds(6, 24), value[72:96, :] * 0.5, COARSE[0])
    coarse_nu[...] = rough_coef[0, 0, 10:26, :]

    def coarse_push(d, c, r):
        return own_push[d, c, r, :]

    for k in range(3):
        advance(rough, rough_two, rough_coef, coarse_push, 0, 9 + 8 * k, 8, 2, (0, 1), COARSE, rough_edge)
    for k in range(2):
        advance(rough_two, rough, rough_coef, coarse_push, 0, 10 + 8 * k, 8, 2, (0,), COARSE, rough_edge)
    for f in range(3):
        guess[16 * f : 16 * f + 16, :] = rough[f, 0, 10:26, :]

    def fine_push(d, c, r):
        return push[d, c, r, :]

    for src, dst, first, count, wanted in (
        (one, two, 12, 9, range(5)),
        (two, one, 12, 9, range(5)),
        (one, two, 12, 9, range(5)),
        (two, one, 16, 8, range(4)),
    ):
        for k in range(count):
            advance(src, dst, coef, fine_push, 0, first + 8 * k, 8, 5, wanted, FINE, fine_edge)
    for f in range(3):
        for c in range(4):
            fine[f, :, 128 * c : 128 * c + 128] = one[f, c, 16:80, :] * (1.0 / FINE_SCALE[f])
    ends = [jnp.concatenate([row_sum(one.at[f, c], 16, 16) for c in range(4)], axis=1) for f in range(3)]
    ends = exact_dot(jnp.concatenate(ends, axis=0), gather)
    first_slice = at[0] == 0
    for f in range(3):
        cut = slice(16 * f, 16 * f + 16)
        defect = ends[cut] * FINE_TO_COARSE[f] - jnp.where(first_slice, 0.0, guess[cut, :])
        for m in range(HALF):
            sent[m, cut, :] = defect


def plane_of(held, nu, q):
    return nu[...] if q == NU else held[q // 3, 16 * (q % 3) : 16 * (q % 3) + 16, :]


def cols_kernel(at, held, nu, send_a, send_b):
    even_y = lax.rem(at[2], 2) == 0
    lane = lanes((16, 128))
    for g, members in enumerate(GROUPS):
        left = jnp.zeros((16, 128), F32)
        right = jnp.zeros((16, 128), F32)
        for slot, q in enumerate(members):
            offset = slot * WIDTH
            value = plane_of(held, nu, q)
            mine = (lane >= offset) & (lane < offset + WIDTH)
            left = jnp.where(mine, rolled(value, offset), left)
            right = jnp.where(mine, rolled(value, offset + WIDTH), right)
        send_a[16 * g : 16 * g + 16, :] = jnp.where(even_y, right, left)
        send_b[16 * g : 16 * g + 16, :] = jnp.where(even_y, left, right)


def rows_kernel(at, held, nu, cols_a, cols_b, send_a, send_b):
    even = lax.rem(at[1], 2) == 0

    def put(place, rows, value):
        if rows == 16:
            send_a[place : place + 16, :] = value
            send_b[place : place + 16, :] = value
        else:
            send_a[place : place + 8, :] = jnp.where(even, value[8:16], value[0:8])
            send_b[place : place + 8, :] = jnp.where(even, value[0:8], value[8:16])

    for q, rows in PARTS:
        put(PART_AT[q][0], rows, plane_of(held, nu, q))
    for g, (place, rows) in STRIP_AT.items():
        put(place, rows, cols_a[16 * g : 16 * g + 16, :])
        put(place + rows, rows, cols_b[16 * g : 16 * g + 16, :])


def assemble(at, held, nu, cols_a, cols_b, rows_a, rows_b, put):
    even_x = lax.rem(at[1], 2) == 0
    even_y = lax.rem(at[2], 2) == 0

    def sides(place, rows):
        a, b = rows_a[place : place + rows, :], rows_b[place : place + rows, :]
        return jnp.where(even_x, b, a), jnp.where(even_x, a, b)

    for q in range(NU + 1):
        put(q, 0, 16, plane_of(held, nu, q))
        if q in PART_AT:
            place, rows = PART_AT[q]
            before, after = sides(place, rows)
            put(q, 0, 16 - rows, before)
            put(q, 0, 32, after)
    for g, members in enumerate(GROUPS):
        cut = slice(16 * g, 16 * g + 16)
        blocks = [(16, cols_a[cut, :], cols_b[cut, :])]
        if g in STRIP_AT:
            place, rows = STRIP_AT[g]
            before_a, after_a = sides(place, rows)
            before_b, after_b = sides(place + rows, rows)
            blocks += [(16 - rows, before_a, before_b), (32, after_a, after_b)]
        for first, a, b in blocks:
            lane = lanes(a.shape)
            after, before = jnp.where(even_y, a, b), jnp.where(even_y, b, a)
            for slot, q in enumerate(members):
                if first == 16 or q in PART_AT:
                    hi, lo = rolled(after, -slot * WIDTH), rolled(before, 128 - WIDTH - slot * WIDTH)
                    put(q, 1, first, jnp.where(lane < WIDTH, hi, jnp.where(lane >= 128 - WIDTH, lo, 0.0)))


def putter(extra, coef):
    def put(q, c, row, value):
        rows = pl.ds(row, value.shape[0])
        if q == NU:
            coefficients(coef, c, rows, value, COARSE[0])
        else:
            extra[q, c, rows, :] = value

    return put


def chain(first_k, one, two, coef, push, extra, kept, at):
    edge = ((8 + 15, 8 + 32),) + edges(at)

    for k in range(first_k, HALF):
        def pushed(d, c, r, k=k):
            return push[k, d, c, r, :]

        def keep_and_add(f, c, r, value, k=k):
            if c == 0:
                kept[k, f, r, :] = value
            return value + extra[3 * k + f, c, pl.ds(r.start - 8, r.size), :]

        for half in range(2):
            halo = 2 * (HALF - 1 - k) + 1 - half
            count = 2 + -(-halo // 4)
            first = min(8 + 16 - halo, 8 + EXT - 8 * count)
            src, dst = (one, two) if half == 0 else (two, one)
            post = keep_and_add if half else None
            for i in range(count):
                advance(src, dst, coef, pushed, 8, first + 8 * i, 8, 2, (0, 1), COARSE, edge, post=post)


def low_kernel(at, held, nu, cols_a, cols_b, rows_b, rows_a, push, state, moved, extra, coef, one, two, kept):
    @pl.when(at[0] < HALF)
    def _():
        assemble(at, held, nu, cols_a, cols_b, rows_a, rows_b, putter(extra, coef))
        for f in range(3):
            for c in range(2):
                one[f, c, 8:56, :] = extra[f, c]
        chain(1, one, two, coef, push, extra, kept, at)
        lane = lanes((CROWS, 128))
        sides = jnp.zeros((CROWS, 128), F32)
        for f in range(3):
            state[16 * f : 16 * f + 16, :] = one[f, 0, 24:40, :]
            sides = jnp.where(lane // 32 == f, rolled(one[f, 1, 24:40, :], 16 + 32 * f), sides)
        state[48:64, :] = sides
        for f in range(3):
            moved[16 * f : 16 * f + 16, :] = kept[jnp.maximum(at[0], 1), f, 24:40, :]


def planes_kernel(at, held, nu, cols_a, cols_b, rows_b, rows_a, extra, coef):
    @pl.when(at[0] >= HALF)
    def _():
        assemble(at, held, nu, cols_a, cols_b, rows_a, rows_b, putter(extra, coef))


def high_kernel(at, state, state_a, state_b, extra, coef, push, fine, guess, moved_low, out, one, two, kept, moved, spread, result, sems):
    even_x = lax.rem(at[1], 2) == 0

    @pl.when(at[0] < HALF)
    def _():
        moved[...] = moved_low[...]

    @pl.when(at[0] >= HALF)
    def _():
        lane = lanes((CROWS, 128))
        a, b = state_a[...], state_b[...]
        for row, block in ((8, jnp.where(even_x, b, a)), (24, state[...]), (40, jnp.where(even_x, a, b))):
            for f in range(3):
                one[f, 0, row : row + 16, :] = block[16 * f : 16 * f + 16]
                side = rolled(block[48:64], -(16 + 32 * f))
                one[f, 1, row : row + 16, :] = jnp.where((lane < 16) | (lane >= 112), side, 0.0)
        chain(0, one, two, coef, push, extra, kept, at)
        for f in range(3):
            moved[16 * f : 16 * f + 16, :] = kept[at[0] - HALF, f, 24:40, :]

    parts = []
    for f in range(3):
        cut = slice(16 * f, 16 * f + 16)
        parts.append(jnp.where(at[0] == 0, 0.0, (moved[cut, :] - guess[cut, :]) * (1.0 / COARSE_SCALE[f])))
    change = jnp.concatenate(parts, axis=0)
    i, j = sublanes((128, COLS)), lanes((128, COLS))
    change = exact_dot(change, jnp.where(i == j // 4, 1.0, 0.0))
    copies = []
    for f in range(3):
        for c in range(4):
            cut = slice(128 * c, 128 * c + 128)
            for k in range(4):
                spread[f, c, pl.ds(k, CROWS, stride=4), :] = change[16 * f : 16 * f + 16, cut]
            result[f, :, cut] = fine[f, :, cut] + spread[f, c]
        copies.append(pltpu.make_async_copy(result.at[f], out.at[f], sems.at[f]))
        copies[f].start()
    for copy in copies:
        copy.wait()


def place():
    return (*[lax.axis_index(a) for a in ("cuts", "sx", "sy")], lax.axis_size("sx"), lax.axis_size("sy"))


VMEM = pl.BlockSpec(memory_space=pltpu.VMEM)
HBM = pl.BlockSpec(memory_space=pltpu.HBM)


def call(kernel, args, outs, scratch=(), far=0, sems=0, away=False):
    shapes = [jax.ShapeDtypeStruct(s, F32) for s in outs]
    near = len(args) - far
    memory = [s if not isinstance(s, tuple) else pltpu.VMEM(s, F32) for s in scratch]
    if sems:
        memory.append(pltpu.SemaphoreType.DMA((sems,)))

    def placed(*refs):
        kernel(place(), *refs)

    return pl.pallas_call(
        placed,
        out_shape=shapes,
        in_specs=[VMEM] * near + [HBM] * far,
        out_specs=[HBM if away else VMEM] * len(shapes),
        scratch_shapes=memory,
        compiler_params=pltpu.CompilerParams(vmem_limit_bytes=48 * 1024 * 1024),
    )(*args)


def swap(x, axis, pairs):
    return lax.ppermute(x, axis, [(a, b) for a, b in pairs] + [(b, a) for a, b in pairs])


def swap_half(x, count, pairs, cuts):
    both = [(a, b) for a, b in pairs] + [(b, a) for a, b in pairs]
    return lax.ppermute(x, ("cuts", "sx"), [(n * count + a, n * count + b) for n in cuts for a, b in both])


def on_device(starts, viscosity, turbine_x, turbine_y, yaw_index):
    count_x, count_y = lax.axis_size("sx"), lax.axis_size("sy")
    at = place()
    start = starts[0]
    x_a = [(i, i + 1) for i in range(0, count_x - 1, 2)]
    x_b = [(i, i + 1) for i in range(1, count_x - 1, 2)]
    y_a = [(i, i + 1) for i in range(0, count_y - 1, 2)]
    y_b = [(i, i + 1) for i in range(1, count_y - 1, 2)]
    turbines = (turbine_x[None, :], turbine_y[None, :], yaw_index)
    turbine_scratch = [pltpu.VMEM((1, 64), jnp.int32), pltpu.VMEM((1, 64), jnp.int32), pltpu.VMEM((CUTS, 64), jnp.int32)]

    own = jnp.concatenate([start, viscosity[None]])
    send_b, send_a = call(edge_kernel, (own,), [(4, 8, COLS)] * 2)
    rows_b = swap(send_b, "sx", x_b)
    rows_a = swap(send_a, "sx", x_a)
    send_a, send_b = call(side_kernel, (own, rows_b, rows_a), [(80, 128)] * 2)
    cols_a = swap(send_a, "sy", y_a)
    cols_b = swap(send_b, "sy", y_b)
    push, own_push = call(
        push_kernel, turbines, [(2, 5, 96, 128), (2, 2, 40, 128)], turbine_scratch, far=3, sems=3)
    fine, guess, sent, coarse_nu = call(
        fine_kernel,
        (own, rows_b, rows_a, cols_a, cols_b, push, own_push),
        [(3, ROWS, COLS), (48, 128), (HALF, 48, 128), (CROWS, 128)],
        [(3, 5, 96, 128), (3, 5, 96, 128), (4, 5, 96, 128), (3, 2, 40, 128), (3, 2, 40, 128), (4, 2, 40, 128)],
    )
    halves = [list(range(HALF)), list(range(HALF, CUTS))]
    held = lax.all_to_all(sent, "cuts", 0, 0, axis_index_groups=halves)
    send_a, send_b = call(cols_kernel, (held, coarse_nu), [(STRIPS, 128)] * 2)
    cols_a = swap(send_a, "sy", y_a)
    cols_b = swap(send_b, "sy", y_b)
    (chain_push,) = call(
        chain_push_kernel, turbines, [(HALF, 2, 2, EXT, 128)], turbine_scratch, far=3, sems=3)
    send_a, send_b = call(rows_kernel, (held, coarse_nu, cols_a, cols_b), [(MESSAGE, 128)] * 2)
    low, high = range(HALF), range(HALF, CUTS)
    rows_a = swap(send_a, "sx", x_a)
    rows_b = swap(send_b, "sx", x_b)
    blocks = (held, coarse_nu, cols_a, cols_b, rows_b, rows_a)
    field, planes, terms = (3, 2, 64, 128), (3 * HALF, 2, EXT, 128), (4, 2, EXT, 128)
    state, moved = call(
        low_kernel, blocks + (chain_push,), [(64, 128), (48, 128)], [planes, terms, field, field, (HALF, 3, 64, 128)])
    goes = [(m, m + 4 if m >= 4 else m + 12) for m in low]
    state_b, state_a = [
        lax.ppermute(state, ("cuts", "sx"), [(m * count_x + i, n * count_x + (i ^ flip)) for m, n in goes for i in range(count_x)])
        for flip in (0, 1)
    ]
    extra, coef = call(planes_kernel, (held, coarse_nu, cols_a, cols_b, rows_b, rows_a), [planes, terms])
    state = state_b
    state_b = swap_half(state, count_x, x_b, high)
    (out,) = call(
        high_kernel,
        (state, state_a, state_b, extra, coef, chain_push, fine, guess, moved),
        [(3, ROWS, COLS)],
        [field, field, (HALF, 3, 64, 128), (48, 128), (3, 4, ROWS, 128), (3, ROWS, COLS)],
        sems=3, away=True,
    )
    return out[None]


def solution(mesh):
    in_specs = (P("cuts", None, "sx", "sy"), P("sx", "sy"), P(), P(), P())
    out_specs = P("cuts", None, "sx", "sy")
    return jax.shard_map(
        on_device, mesh=mesh, in_specs=in_specs, out_specs=out_specs, check_vma=False
    )
```

```python
import math

import jax
import jax.numpy as jnp
import numpy as np
from jax import lax
from jax.experimental import pallas as pl
from jax.experimental.pallas import tpu as pltpu
from jax.sharding import PartitionSpec as P

YAWS = 7
CUTS = 16
REACH = 3
F32 = jnp.float32
BF16 = jnp.bfloat16

FINE = (0.3, 0.25, 0.01)
FINE_THRUST = 0.5
FINE_SCALE = (0.25, 0.25, 0.025)
COARSE = (0.15, 0.125, 0.0025)
COARSE_THRUST = 1.0
COARSE_SCALE = (0.125, 0.125, 0.00625)
FINE_TO_COARSE = (0.5, 0.5, 0.25)

ROWS, COLS = 64, 512
CROWS, CCOLS = 16, 128
HALF = CUTS // 2
EXT = 48
NU = 24
ANGLES = [(k - 0.5 * (YAWS - 1)) * (math.pi / 18.0) for k in range(YAWS)]
WEIGHT_X = [float(np.float32(math.cos(t) ** 3)) for t in ANGLES]
WEIGHT_Y = [float(np.float32(math.cos(t) ** 2 * math.sin(t))) for t in ANGLES]

WIDTH = 32
_ORDER = list(range(9)) + [NU, 21, 22] + list(range(9, 21)) + [23]
GROUPS = [_ORDER[_i : _i + 4] for _i in range(0, len(_ORDER), 4)]
STRIPS = 16 * len(GROUPS)
PARTS = [(q, 16) for q in range(0, 9)] + [(q, 8) for q in range(9, 21)] + [(NU, 16)]
PART_AT = {}
_at = 0
for _q, _rows in PARTS:
    PART_AT[_q] = (_at, _rows)
    _at += _rows
STRIP_AT = {}
for _g, _rows in ((0, 16), (1, 16), (2, 16), (3, 8), (4, 8), (5, 8)):
    STRIP_AT[_g] = (_at, _rows)
    _at += 2 * _rows
MESSAGE = _at


def lanes(shape):
    return lax.broadcasted_iota(jnp.int32, shape, len(shape) - 1)


def sublanes(shape):
    return lax.broadcasted_iota(jnp.int32, shape, len(shape) - 2)


def rolled(x, by):
    return pltpu.roll(x, by % 128, 1) if by % 128 else x


def split3(x):
    high = x.astype(BF16)
    rest = x - high.astype(F32)
    middle = rest.astype(BF16)
    return high, middle, (rest - middle.astype(F32)).astype(BF16)


def exact_dot(x, y, dims=(((1,), (0,)), ((), ()))):
    count = x.shape[0]
    stacked = jnp.concatenate(split3(x), axis=0)
    out = lax.dot_general(stacked, y.astype(BF16), dims, preferred_element_type=F32)
    return out[0:count] + (out[count : 2 * count] + out[2 * count : 3 * count])


def advance(src, dst, coef, push, shift, row, count, tiles, wanted, terms, edge, post=None):
    (row_before, row_after), (factor_before, factor_after), side_mask = edge
    _, lift, gain = terms
    lane = lanes((count, 128))
    low, high = lane == 0, lane == 127
    here, east, west = pl.ds(row, count), pl.ds(row + 1, count), pl.ds(row - 1, count)
    there = pl.ds(row - shift, count)
    mid = [[src[f, c, here, :] for c in range(tiles)] for f in range(3)]
    up = [[pltpu.roll(mid[f][c], 127, 1) for c in range(tiles)] for f in range(3)]
    down = [[pltpu.roll(mid[f][c], 1, 1) for c in range(tiles)] for f in range(3)]
    for c in wanted:
        after, before = (c + 1) % tiles, (c - 1) % tiles
        u, v, p = mid[0][c], mid[1][c], mid[2][c]
        un, vn, pn = [jnp.where(high, up[f][after], up[f][c]) for f in range(3)]
        us, vs, ps = [jnp.where(low, down[f][before], down[f][c]) for f in range(3)]
        ue, ve, pe = [src[f, c, east, :] for f in range(3)]
        uw, vw, pw = [src[f, c, west, :] for f in range(3)]
        nu, nu_carry, keep, keep_p = [coef[k, c, there, :] for k in range(4)]
        to_east, to_west = nu - u, nu_carry + u
        lifted = u + lift
        size = jnp.abs(lifted)
        drag = lifted * size / (size + lift)
        new_u = ue * to_east + uw * to_west + nu * (un + us) + keep * u - (pe - pw) - push(0, c, there) * drag
        new_v = ve * to_east + vw * to_west + nu * (vn + vs) + keep * v - (pn - ps) - push(1, c, there) * drag
        new_p = nu * ((pe + pw) + (pn + ps)) + keep_p * p - gain * ((ue - uw) + (vn - vs))
        new = [new_u, new_v, new_p]
        if c == tiles - 1:
            new = [f * side_mask for f in new]
        line = sublanes((count, 128))
        if row <= row_before < row + count:
            inside = jnp.where(line == row_before - row, factor_before, 1.0)
            new = [f * inside for f in new]
        if row <= row_after < row + count:
            inside = jnp.where(line == row_after - row, factor_after, 1.0)
            new = [f * inside for f in new]
        for f in range(3):
            if post is not None:
                new[f] = post(f, c, here, new[f])
            dst[f, c, here, :] = new[f]


def edges(at):
    lane = lanes((8, 128))
    outside = [jnp.where(at[1] > 0, 1.0, 0.0), jnp.where(at[1] < at[3] - 1, 1.0, 0.0)]
    side = jnp.where(lane < 64, jnp.where(at[2] < at[4] - 1, 1.0, 0.0), jnp.where(at[2] > 0, 1.0, 0.0))
    return tuple(outside), side


def coefficients(coef, c, rows, nu, carry):
    coef[0, c, rows, :] = nu
    coef[1, c, rows, :] = nu + carry
    coef[2, c, rows, :] = (1.0 - carry) - 4.0 * nu
    coef[3, c, rows, :] = 1.0 - 4.0 * nu


def yaw_weights(yaw):
    wx = jnp.zeros(yaw.shape, F32)
    wy = jnp.zeros(yaw.shape, F32)
    for k in range(YAWS):
        hit = yaw == k
        wx = jnp.where(hit, WEIGHT_X[k], wx)
        wy = jnp.where(hit, WEIGHT_Y[k], wy)
    return wx, wy


def fetch(pairs, sems):
    copies = [pltpu.make_async_copy(a, b, sems.at[i]) for i, (a, b) in enumerate(pairs)]
    for copy in copies:
        copy.start()
    for copy in copies:
        copy.wait()


def edge_kernel(at, own, send_b, send_a):
    even = lax.rem(at[1], 2) == 0
    for f in range(4):
        first, last = own[f, 0:8, :], own[f, ROWS - 8 : ROWS, :]
        send_a[f] = jnp.where(even, last, first)
        send_b[f] = jnp.where(even, first, last)


def side_kernel(at, own, got_b, got_a, send_a, send_b, left_all, right_all):
    even_x = lax.rem(at[1], 2) == 0
    even_y = lax.rem(at[2], 2) == 0
    for r0, count in ((0, 8), (8, 64), (72, 8)):
        lane = lanes((count, 128))
        left = jnp.zeros((count, 128), F32)
        right = jnp.zeros((count, 128), F32)
        for f in range(4):
            if r0 == 8:
                a, b = own[f, :, 0:128], own[f, :, COLS - 128 : COLS]
            else:
                from_a = jnp.logical_xor(even_x, r0 == 0)
                a = jnp.where(from_a, got_a[f, :, 0:128], got_b[f, :, 0:128])
                b = jnp.where(from_a, got_a[f, :, COLS - 128 : COLS], got_b[f, :, COLS - 128 : COLS])
            mine = (lane >= 8 * f) & (lane < 8 * f + 8)
            left = jnp.where(mine, rolled(a, 8 * f), left)
            right = jnp.where(mine, rolled(b, 8 * f + 8), right)
        left_all[r0 : r0 + count, :] = left
        right_all[r0 : r0 + count, :] = right
    left_all[80:96, :] = jnp.zeros((16, 128), F32)
    right_all[80:96, :] = jnp.zeros((16, 128), F32)
    lane = lanes((24, 128))
    left, right = left_all[0:24, :], right_all[0:24, :]
    for k in range(1, 4):
        left = jnp.where(lane // 32 == k, rolled(left_all[24 * k : 24 * k + 24, :], 32 * k), left)
        right = jnp.where(lane // 32 == k, rolled(right_all[24 * k : 24 * k + 24, :], 32 * k), right)
    send_a[...] = jnp.where(even_y, right, left)
    send_b[...] = jnp.where(even_y, left, right)


def fine_cols(sy, c, shape):
    i = sublanes(shape)
    return sy * COLS + (128 * c + i if c < 4 else jnp.where(i < 64, COLS + i, i - 128))


def coarse_cols(sy, c, ty):
    i = sublanes((128, 64))
    col = sy * CCOLS + (i if c == 0 else jnp.where(i < 64, CCOLS + i, i - 128))
    hit = jnp.zeros((128, 64), F32)
    for offset in range(4):
        hit = hit + jnp.where(jnp.abs(4 * col + offset - ty) <= REACH, 0.25, 0.0)
    return hit


LAST_DIMS = (((1,), (1,)), ((), ()))


def push_kernel(at, tx_in, ty_in, yaw_in, fine_push, own_push, tx_ref, ty_ref, yaw_ref, sems):
    fetch([(tx_in, tx_ref), (ty_in, ty_ref), (yaw_in, yaw_ref)], sems)
    tx, ty = tx_ref[...], ty_ref[...]
    mine = sublanes((CUTS, 64)) == at[0]
    wx, wy = yaw_weights(jnp.sum(jnp.where(mine, yaw_ref[...], 0), axis=0, keepdims=True))
    row = at[1] * ROWS - 16 + sublanes((96, 64))
    hit = jnp.where(row == tx, FINE_THRUST, 0.0)
    both = jnp.concatenate([hit * wx, hit * wy], axis=0)
    for c in range(5):
        cols = jnp.where(jnp.abs(fine_cols(at[2], c, (128, 64)) - ty) <= REACH, 1.0, 0.0)
        push = exact_dot(both, cols, LAST_DIMS)
        fine_push[0, c] = push[0:96]
        fine_push[1, c] = push[96:192]
    row = at[1] * CROWS - 10 + sublanes((40, 64))
    hit = jnp.where(row == tx // 4, 0.25 * COARSE_THRUST, 0.0)
    both = jnp.concatenate([hit * wx, hit * wy], axis=0)
    for c in range(2):
        push = exact_dot(both, coarse_cols(at[2], c, ty), LAST_DIMS)
        own_push[0, c] = push[0:40]
        own_push[1, c] = push[40:80]


def chain_push_kernel(at, tx_in, ty_in, yaw_in, push, tx_ref, ty_ref, yaw_ref, sems):
    fetch([(tx_in, tx_ref), (ty_in, ty_ref), (yaw_in, yaw_ref)], sems)
    tx, ty = tx_ref[...], ty_ref[...]
    row = at[1] * CROWS - 16 + sublanes((EXT, 64))
    hit = jnp.where(row == tx // 4, 0.25 * COARSE_THRUST, 0.0)
    wx, wy = yaw_weights(yaw_ref[pl.ds(pl.multiple_of(at[0] // HALF * HALF, HALF), HALF), :])
    cols = [coarse_cols(at[2], c, ty) for c in range(2)]
    for k in range(HALF):
        both = jnp.concatenate([hit * wx[k : k + 1, :], hit * wy[k : k + 1, :]], axis=0)
        for c in range(2):
            value = exact_dot(both, cols[c], LAST_DIMS)
            push[k, 0, c] = value[0:EXT]
            push[k, 1, c] = value[EXT : 2 * EXT]


def fine_kernel(at, own, rows_b, rows_a, cols_a, cols_b, push, own_push, fine, guess, sent, coarse_nu,
                one, two, coef, rough, rough_two, rough_coef):
    even_x = lax.rem(at[1], 2) == 0
    even_y = lax.rem(at[2], 2) == 0
    outside, side_mask = edges(at)
    fine_edge, rough_edge = ((15, 80), outside, side_mask), ((9, 26), outside, side_mask)
    after_all = jnp.where(even_y, cols_a[...], cols_b[...])
    before_all = jnp.where(even_y, cols_b[...], cols_a[...])
    for f in range(4):
        for c in range(5):
            if c < 4:
                cut = slice(128 * c, 128 * c + 128)
                a, b = rows_a[f, :, cut], rows_b[f, :, cut]
                pieces = [(8, 8, jnp.where(even_x, b, a)), (16, 64, own[f, :, cut]), (80, 8, jnp.where(even_x, a, b))]
            else:
                pieces = []
                for k in range(4):
                    count = 24 if k < 3 else 8
                    after = rolled(after_all[0:count], -32 * k - 8 * f)
                    before = rolled(before_all[0:count], 120 - 32 * k - 8 * f)
                    lane = lanes((count, 128))
                    value = jnp.where(lane < 8, after, jnp.where(lane >= 120, before, 0.0))
                    pieces.append((8 + 24 * k, count, value))
            for r, count, value in pieces:
                if f < 3:
                    one[f, c, r : r + count, :] = value * FINE_SCALE[f]
                else:
                    coefficients(coef, c, pl.ds(r, count), value, FINE[0])

    i, j = sublanes((COLS, 128)), lanes((COLS, 128))
    gather = jnp.where(i // 4 == j, 0.0625, 0.0)
    i, j = sublanes((128, 128)), lanes((128, 128))
    gather_side = jnp.where(((i < 8) & (i // 4 == j)) | ((i >= 120) & ((i - 120) // 4 == j - 126)), 0.0625, 0.0)

    def row_sum(ref, first, count):
        parts = [ref[pl.ds(first + k, count, stride=4), :] for k in range(4)]
        return (parts[0] + parts[1]) + (parts[2] + parts[3])

    def pick(f, c):
        return one.at[f, c] if f < 3 else coef.at[0, c]

    body = [jnp.concatenate([row_sum(pick(f, c), 0, 24) for c in range(4)], axis=1) for f in range(4)]
    side = [row_sum(pick(f, 4), 0, 24) for f in range(4)]
    body = exact_dot(jnp.concatenate(body, axis=0), gather)
    side = exact_dot(jnp.concatenate(side, axis=0), gather_side)
    rough[...] = jnp.zeros(rough.shape, F32)
    rough_two[...] = jnp.zeros(rough_two.shape, F32)
    rough_coef[...] = jnp.zeros(rough_coef.shape, F32)
    for c, value in enumerate((body, side)):
        for f in range(3):
            rough[f, c, 6:30, :] = value[24 * f : 24 * f + 24, :] * FINE_TO_COARSE[f]
        coefficients(rough_coef, c, pl.ds(6, 24), value[72:96, :] * 0.5, COARSE[0])
    coarse_nu[...] = rough_coef[0, 0, 10:26, :]

    def coarse_push(d, c, r):
        return own_push[d, c, r, :]

    for k in range(3):
        advance(rough, rough_two, rough_coef, coarse_push, 0, 9 + 8 * k, 8, 2, (0, 1), COARSE, rough_edge)
    for k in range(2):
        advance(rough_two, rough, rough_coef, coarse_push, 0, 10 + 8 * k, 8, 2, (0,), COARSE, rough_edge)
    for f in range(3):
        guess[16 * f : 16 * f + 16, :] = rough[f, 0, 10:26, :]

    def fine_push(d, c, r):
        return push[d, c, r, :]

    for src, dst, first, count, wanted in (
        (one, two, 12, 9, range(5)),
        (two, one, 12, 9, range(5)),
        (one, two, 12, 9, range(5)),
        (two, one, 16, 8, range(4)),
    ):
        for k in range(count):
            advance(src, dst, coef, fine_push, 0, first + 8 * k, 8, 5, wanted, FINE, fine_edge)
    for f in range(3):
        for c in range(4):
            fine[f, :, 128 * c : 128 * c + 128] = one[f, c, 16:80, :] * (1.0 / FINE_SCALE[f])
    ends = [jnp.concatenate([row_sum(one.at[f, c], 16, 16) for c in range(4)], axis=1) for f in range(3)]
    ends = exact_dot(jnp.concatenate(ends, axis=0), gather)
    first_slice = at[0] == 0
    for f in range(3):
        cut = slice(16 * f, 16 * f + 16)
        defect = ends[cut] * FINE_TO_COARSE[f] - jnp.where(first_slice, 0.0, guess[cut, :])
        for m in range(HALF):
            sent[m, cut, :] = defect


def plane_of(held, nu, q):
    return nu[...] if q == NU else held[q // 3, 16 * (q % 3) : 16 * (q % 3) + 16, :]


def cols_kernel(at, held, nu, send_a, send_b):
    even_y = lax.rem(at[2], 2) == 0
    lane = lanes((16, 128))
    for g, members in enumerate(GROUPS):
        left = jnp.zeros((16, 128), F32)
        right = jnp.zeros((16, 128), F32)
        for slot, q in enumerate(members):
            offset = slot * WIDTH
            value = plane_of(held, nu, q)
            mine = (lane >= offset) & (lane < offset + WIDTH)
            left = jnp.where(mine, rolled(value, offset), left)
            right = jnp.where(mine, rolled(value, offset + WIDTH), right)
        send_a[16 * g : 16 * g + 16, :] = jnp.where(even_y, right, left)
        send_b[16 * g : 16 * g + 16, :] = jnp.where(even_y, left, right)


def rows_kernel(at, held, nu, cols_a, cols_b, send_a, send_b):
    even = lax.rem(at[1], 2) == 0

    def put(place, rows, value):
        if rows == 16:
            send_a[place : place + 16, :] = value
            send_b[place : place + 16, :] = value
        else:
            send_a[place : place + 8, :] = jnp.where(even, value[8:16], value[0:8])
            send_b[place : place + 8, :] = jnp.where(even, value[0:8], value[8:16])

    for q, rows in PARTS:
        put(PART_AT[q][0], rows, plane_of(held, nu, q))
    for g, (place, rows) in STRIP_AT.items():
        put(place, rows, cols_a[16 * g : 16 * g + 16, :])
        put(place + rows, rows, cols_b[16 * g : 16 * g + 16, :])


def assemble(at, held, nu, cols_a, cols_b, rows_a, rows_b, put):
    even_x = lax.rem(at[1], 2) == 0
    even_y = lax.rem(at[2], 2) == 0

    def sides(place, rows):
        a, b = rows_a[place : place + rows, :], rows_b[place : place + rows, :]
        return jnp.where(even_x, b, a), jnp.where(even_x, a, b)

    for q in range(NU + 1):
        put(q, 0, 16, plane_of(held, nu, q))
        if q in PART_AT:
            place, rows = PART_AT[q]
            before, after = sides(place, rows)
            put(q, 0, 16 - rows, before)
            put(q, 0, 32, after)
    for g, members in enumerate(GROUPS):
        cut = slice(16 * g, 16 * g + 16)
        blocks = [(16, cols_a[cut, :], cols_b[cut, :])]
        if g in STRIP_AT:
            place, rows = STRIP_AT[g]
            before_a, after_a = sides(place, rows)
            before_b, after_b = sides(place + rows, rows)
            blocks += [(16 - rows, before_a, before_b), (32, after_a, after_b)]
        for first, a, b in blocks:
            lane = lanes(a.shape)
            after, before = jnp.where(even_y, a, b), jnp.where(even_y, b, a)
            for slot, q in enumerate(members):
                if first == 16 or q in PART_AT:
                    hi, lo = rolled(after, -slot * WIDTH), rolled(before, 128 - WIDTH - slot * WIDTH)
                    put(q, 1, first, jnp.where(lane < WIDTH, hi, jnp.where(lane >= 128 - WIDTH, lo, 0.0)))


def putter(extra, coef):
    def put(q, c, row, value):
        rows = pl.ds(row, value.shape[0])
        if q == NU:
            coefficients(coef, c, rows, value, COARSE[0])
        else:
            extra[q, c, rows, :] = value

    return put


def chain(first_k, one, two, coef, push, extra, kept, at):
    edge = ((8 + 15, 8 + 32),) + edges(at)

    for k in range(first_k, HALF):
        def pushed(d, c, r, k=k):
            return push[k, d, c, r, :]

        def keep_and_add(f, c, r, value, k=k):
            if c == 0:
                kept[k, f, r, :] = value
            return value + extra[3 * k + f, c, pl.ds(r.start - 8, r.size), :]

        for half in range(2):
            halo = 2 * (HALF - 1 - k) + 1 - half
            count = 2 + -(-halo // 4)
            first = min(8 + 16 - halo, 8 + EXT - 8 * count)
            src, dst = (one, two) if half == 0 else (two, one)
            post = keep_and_add if half else None
            for i in range(count):
                advance(src, dst, coef, pushed, 8, first + 8 * i, 8, 2, (0, 1), COARSE, edge, post=post)


def low_kernel(at, held, nu, cols_a, cols_b, rows_b, rows_a, push, state, moved, extra, coef, one, two, kept):
    @pl.when(at[0] < HALF)
    def _():
        assemble(at, held, nu, cols_a, cols_b, rows_a, rows_b, putter(extra, coef))
        for f in range(3):
            for c in range(2):
                one[f, c, 8:56, :] = extra[f, c]
        chain(1, one, two, coef, push, extra, kept, at)
        lane = lanes((CROWS, 128))
        sides = jnp.zeros((CROWS, 128), F32)
        for f in range(3):
            state[16 * f : 16 * f + 16, :] = one[f, 0, 24:40, :]
            sides = jnp.where(lane // 32 == f, rolled(one[f, 1, 24:40, :], 16 + 32 * f), sides)
        state[48:64, :] = sides
        for f in range(3):
            moved[16 * f : 16 * f + 16, :] = kept[jnp.maximum(at[0], 1), f, 24:40, :]


def planes_kernel(at, held, nu, cols_a, cols_b, rows_b, rows_a, extra, coef):
    @pl.when(at[0] >= HALF)
    def _():
        assemble(at, held, nu, cols_a, cols_b, rows_a, rows_b, putter(extra, coef))


def high_kernel(at, state, state_a, state_b, extra, coef, push, fine, guess, moved_low, out, one, two, kept, moved, spread, result, sems):
    even_x = lax.rem(at[1], 2) == 0

    @pl.when(at[0] < HALF)
    def _():
        moved[...] = moved_low[...]

    @pl.when(at[0] >= HALF)
    def _():
        lane = lanes((CROWS, 128))
        a, b = state_a[...], state_b[...]
        for row, block in ((8, jnp.where(even_x, b, a)), (24, state[...]), (40, jnp.where(even_x, a, b))):
            for f in range(3):
                one[f, 0, row : row + 16, :] = block[16 * f : 16 * f + 16]
                side = rolled(block[48:64], -(16 + 32 * f))
                one[f, 1, row : row + 16, :] = jnp.where((lane < 16) | (lane >= 112), side, 0.0)
        chain(0, one, two, coef, push, extra, kept, at)
        for f in range(3):
            moved[16 * f : 16 * f + 16, :] = kept[at[0] - HALF, f, 24:40, :]

    parts = []
    for f in range(3):
        cut = slice(16 * f, 16 * f + 16)
        parts.append(jnp.where(at[0] == 0, 0.0, (moved[cut, :] - guess[cut, :]) * (1.0 / COARSE_SCALE[f])))
    change = jnp.concatenate(parts, axis=0)
    i, j = sublanes((128, COLS)), lanes((128, COLS))
    change = exact_dot(change, jnp.where(i == j // 4, 1.0, 0.0))
    copies = []
    for f in range(3):
        for c in range(4):
            cut = slice(128 * c, 128 * c + 128)
            for k in range(4):
                spread[f, c, pl.ds(k, CROWS, stride=4), :] = change[16 * f : 16 * f + 16, cut]
            result[f, :, cut] = fine[f, :, cut] + spread[f, c]
        copies.append(pltpu.make_async_copy(result.at[f], out.at[f], sems.at[f]))
        copies[f].start()
    for copy in copies:
        copy.wait()


def place():
    return (*[lax.axis_index(a) for a in ("cuts", "sx", "sy")], lax.axis_size("sx"), lax.axis_size("sy"))


VMEM = pl.BlockSpec(memory_space=pltpu.VMEM)
HBM = pl.BlockSpec(memory_space=pltpu.HBM)


def call(kernel, args, outs, scratch=(), far=0, sems=0, away=False):
    shapes = [jax.ShapeDtypeStruct(s, F32) for s in outs]
    near = len(args) - far
    memory = [s if not isinstance(s, tuple) else pltpu.VMEM(s, F32) for s in scratch]
    if sems:
        memory.append(pltpu.SemaphoreType.DMA((sems,)))

    def placed(*refs):
        kernel(place(), *refs)

    return pl.pallas_call(
        placed,
        out_shape=shapes,
        in_specs=[VMEM] * near + [HBM] * far,
        out_specs=[HBM if away else VMEM] * len(shapes),
        scratch_shapes=memory,
        compiler_params=pltpu.CompilerParams(vmem_limit_bytes=48 * 1024 * 1024),
    )(*args)


def swap(x, axis, pairs):
    return lax.ppermute(x, axis, [(a, b) for a, b in pairs] + [(b, a) for a, b in pairs])


def swap_half(x, count, pairs, cuts):
    both = [(a, b) for a, b in pairs] + [(b, a) for a, b in pairs]
    return lax.ppermute(x, ("cuts", "sx"), [(n * count + a, n * count + b) for n in cuts for a, b in both])


def on_device(starts, viscosity, turbine_x, turbine_y, yaw_index):
    count_x, count_y = lax.axis_size("sx"), lax.axis_size("sy")
    at = place()
    start = starts[0]
    x_a = [(i, i + 1) for i in range(0, count_x - 1, 2)]
    x_b = [(i, i + 1) for i in range(1, count_x - 1, 2)]
    y_a = [(i, i + 1) for i in range(0, count_y - 1, 2)]
    y_b = [(i, i + 1) for i in range(1, count_y - 1, 2)]
    turbines = (turbine_x[None, :], turbine_y[None, :], yaw_index)
    turbine_scratch = [pltpu.VMEM((1, 64), jnp.int32), pltpu.VMEM((1, 64), jnp.int32), pltpu.VMEM((CUTS, 64), jnp.int32)]

    own = jnp.concatenate([start, viscosity[None]])
    send_b, send_a = call(edge_kernel, (own,), [(4, 8, COLS)] * 2)
    rows_b = swap(send_b, "sx", x_b)
    rows_a = swap(send_a, "sx", x_a)
    send_a, send_b = call(side_kernel, (own, rows_b, rows_a), [(24, 128)] * 2, [(96, 128)] * 2)
    cols_a = swap(send_a, "sy", y_a)
    cols_b = swap(send_b, "sy", y_b)
    push, own_push = call(
        push_kernel, turbines, [(2, 5, 96, 128), (2, 2, 40, 128)], turbine_scratch, far=3, sems=3)
    fine, guess, sent, coarse_nu = call(
        fine_kernel,
        (own, rows_b, rows_a, cols_a, cols_b, push, own_push),
        [(3, ROWS, COLS), (48, 128), (HALF, 48, 128), (CROWS, 128)],
        [(3, 5, 96, 128), (3, 5, 96, 128), (4, 5, 96, 128), (3, 2, 40, 128), (3, 2, 40, 128), (4, 2, 40, 128)],
    )
    halves = [list(range(HALF)), list(range(HALF, CUTS))]
    held = lax.all_to_all(sent, "cuts", 0, 0, axis_index_groups=halves)
    send_a, send_b = call(cols_kernel, (held, coarse_nu), [(STRIPS, 128)] * 2)
    cols_a = swap(send_a, "sy", y_a)
    cols_b = swap(send_b, "sy", y_b)
    (chain_push,) = call(
        chain_push_kernel, turbines, [(HALF, 2, 2, EXT, 128)], turbine_scratch, far=3, sems=3)
    send_a, send_b = call(rows_kernel, (held, coarse_nu, cols_a, cols_b), [(MESSAGE, 128)] * 2)
    low, high = range(HALF), range(HALF, CUTS)
    rows_a = swap(send_a, "sx", x_a)
    rows_b = swap(send_b, "sx", x_b)
    blocks = (held, coarse_nu, cols_a, cols_b, rows_b, rows_a)
    field, planes, terms = (3, 2, 64, 128), (3 * HALF, 2, EXT, 128), (4, 2, EXT, 128)
    state, moved = call(
        low_kernel, blocks + (chain_push,), [(64, 128), (48, 128)], [planes, terms, field, field, (HALF, 3, 64, 128)])
    goes = [(m, m + 4 if m >= 4 else m + 12) for m in low]
    state_b, state_a = [
        lax.ppermute(state, ("cuts", "sx"), [(m * count_x + i, n * count_x + (i ^ flip)) for m, n in goes for i in range(count_x)])
        for flip in (0, 1)
    ]
    extra, coef = call(planes_kernel, (held, coarse_nu, cols_a, cols_b, rows_b, rows_a), [planes, terms])
    state = state_b
    state_b = swap_half(state, count_x, x_b, high)
    (out,) = call(
        high_kernel,
        (state, state_a, state_b, extra, coef, chain_push, fine, guess, moved),
        [(3, ROWS, COLS)],
        [field, field, (HALF, 3, 64, 128), (48, 128), (3, 4, ROWS, 128), (3, ROWS, COLS)],
        sems=3, away=True,
    )
    return out[None]


def solution(mesh):
    in_specs = (P("cuts", None, "sx", "sy"), P("sx", "sy"), P(), P(), P())
    out_specs = P("cuts", None, "sx", "sy")
    return jax.shard_map(
        on_device, mesh=mesh, in_specs=in_specs, out_specs=out_specs, check_vma=False
    )
```
